128 devices in a mesh: dp: 64 (over x_lo, z, y, core), tensor: 2 (over x_hi).
Axes of the slice: x: 4 (x_hi: 2, x_lo: 2; x = x_hi * 2 + x_lo), y: 4, z: 4, core: 2. Of those that a mesh axis runs over, the one named last changes fastest.
Arguments:
- tokens: bfloat16 [14336, 2048], P(('dp', 'tensor')), may hold values from -24 to 24
- segment_ids: int32 [14336], P('dp'), may hold values from 0 to 3, as said below
- attn_gain: bfloat16 [2048], P('dp'), may hold values from 0.099609375 to 1.8984375
- w_query: bfloat16 [2048, 2048], P('dp', 'tensor'), may hold values from -0.125 to 0.125
- w_key: bfloat16 [2048, 512], P('dp', 'tensor'), may hold values from -0.125 to 0.125
- w_value: bfloat16 [2048, 512], P('dp', 'tensor'), may hold values from -0.125 to 0.125
- w_out: bfloat16 [2048, 2048], P('tensor', 'dp'), may hold values from -0.75 to 0.75
- mlp_gain: bfloat16 [2048], P('dp'), may hold values from 0.099609375 to 1.8984375
- w_gate: bfloat16 [2048, 8192], P('dp', 'tensor'), may hold values from -0.125 to 0.125
- w_up: bfloat16 [2048, 8192], P('dp', 'tensor'), may hold values from -0.125 to 0.125
- w_down: bfloat16 [8192, 2048], P('tensor', 'dp'), may hold values from -0.125 to 0.125
- cotangent: bfloat16 [14336, 2048], P(('dp', 'tensor')), may hold values from -24 to 24
Outputs:
- layer_output: bfloat16 [14336, 2048], P(('dp', 'tensor'))
- input_grad: float32 [14336, 2048], P(('dp', 'tensor'))
- attn_gain_grad: float32 [2048], P('dp')
- query_grad: float32 [2048, 2048], P('dp', 'tensor')
- key_grad: float32 [2048, 512], P('dp', 'tensor')
- value_grad: float32 [2048, 512], P('dp', 'tensor')
- out_grad: float32 [2048, 2048], P('tensor', 'dp')
- mlp_gain_grad: float32 [2048], P('dp')
- gate_grad: float32 [2048, 8192], P('dp', 'tensor')
- up_grad: float32 [2048, 8192], P('dp', 'tensor')
- down_grad: float32 [8192, 2048], P('tensor', 'dp')
The draws below stay inside these ranges and needn't reach their ends.
Inputs may be any that keep to these rules, and one draw needn't show every extreme that they name: `segment_ids`: within each aligned block of 224 tokens (the tokens of one index of dp) the ids start at 0, never fall and rise by one at each new sequence; a block holds 1 to 4 sequences and some block holds 4; sequences never cross a block's end, and equal ids in different blocks are different sequences.
All inputs are finite; a program needn't handle non-finite values.
Results may differ from the reference program's by a relative error of at most 0.015.
Values may be sent and summed in bfloat16 or wider, within the bound.
No kernel may reach another device: no remote copies, remote signals or barrier semaphores. Data moves between devices by JAX's collectives and lax.ppermute only.
A program may use at most 320 MiB of HBM per device.

```python
import math
import jax
import jax.numpy as jnp
from jax import lax

D = 2048
HEADS = 32
KV_HEADS = 8
HEAD = 64
FF = 8192
TOK_DEV = 224
SEQS = 4
TOKENS = 14336
N_DP = 64


def draw_segment_ids(key, part):
    key = jax.random.fold_in(key, 11)
    count_key, place_key, full_key = jax.random.split(key, 3)
    seq_counts = jax.random.randint(count_key, (N_DP,), 1, SEQS + 1)
    busiest = jax.random.randint(full_key, (), 0, N_DP)
    seq_counts = jnp.where(jnp.arange(N_DP) == busiest, SEQS, seq_counts)
    middle = TOK_DEV // 2
    cut_spots = jnp.arange(1, TOK_DEV - 1)
    cut_spots = cut_spots + (cut_spots >= middle).astype(jnp.int32)
    ranking = jax.vmap(lambda block_key: jax.random.permutation(block_key, TOK_DEV - 2))(jax.random.split(place_key, N_DP))
    chosen = jnp.where(ranking < (seq_counts - 1)[:, None], 1, 0).astype(jnp.int32)
    cut_flags = jnp.zeros((N_DP, TOK_DEV), jnp.int32).at[:, cut_spots].set(chosen)
    return jnp.cumsum(cut_flags, axis=1).reshape(-1).astype(jnp.int32)


def spiked(values, rng, source, target, parts, factor):
    owner, partner = [(jnp.arange(values.shape[axis_at]) // (values.shape[axis_at] // parts)).reshape([-1 if axis == axis_at else 1 for axis in range(values.ndim)]) for axis_at in (source, target)]
    chosen = jax.random.permutation(rng, parts)[partner]
    strong = (owner == chosen) | (owner == (partner + parts // 2) % parts)
    return jnp.where(strong, factor * values, values)


def block_levels(rng, dims, cuts, least, high):
    factor_of = 1.0
    for position, shards_of in cuts:
        draws = jax.random.uniform(jax.random.fold_in(jax.random.fold_in(rng, 6), position), (shards_of,), jnp.float32, least / len(cuts), high / len(cuts))
        factor_of = factor_of * jnp.repeat(jnp.exp(draws), dims[position] // shards_of).reshape((-1,) + (1,) * (len(dims) - 1 - position))
    return factor_of


def scatter_about(own_key, extent, deviation, bound, cuts=(), held_as=jnp.bfloat16):
    values = deviation * jax.random.normal(own_key, extent, jnp.float32)
    if cuts:
        values = values * block_levels(own_key, extent, cuts, -0.22, 0.18)
    return jnp.clip(values, -bound, bound).astype(held_as)


def gaussian_with(own_key, shape, deviation, limit, cuts, heavy, held_as=jnp.bfloat16):
    values = deviation * jax.random.normal(own_key, shape, jnp.float32)
    if cuts:
        values = values * block_levels(own_key, shape, cuts, -0.22, 0.18)
    return jnp.clip(spiked(values, jax.random.fold_in(own_key, 3), *heavy), -limit, limit).astype(held_as)


def setup_inputs(seed: int = 0) -> dict:
    key_list = jax.random.split(jax.random.key(seed), 13)
    return {
        "tokens": gaussian_with(key_list[0], (TOKENS, D), 1.0, 24.0, ((0, 128),), (0, 1, 128, 5.5)),
        "segment_ids": draw_segment_ids(jax.random.fold_in(key_list[12], 71), 0),
        "attn_gain": jnp.clip(1.0 + 0.18 * jax.random.normal(key_list[2], (D,), jnp.float32), 0.099609375, 1.8984375).astype(jnp.bfloat16),
        "w_query": scatter_about(key_list[3], (D, HEADS * HEAD), D ** -0.5, 0.125, ((0, 64), (1, 2))),
        "w_key": scatter_about(key_list[4], (D, KV_HEADS * HEAD), D ** -0.5, 0.125, ((0, 64), (1, 2))),
        "w_value": scatter_about(key_list[5], (D, KV_HEADS * HEAD), D ** -0.5, 0.125, ((0, 64), (1, 2))),
        "w_out": scatter_about(key_list[6], (HEADS * HEAD, D), (D // 32) ** -0.5, 0.75, ((0, 2), (1, 64))),
        "mlp_gain": jnp.clip(1.0 + 0.18 * jax.random.normal(key_list[7], (D,), jnp.float32), 0.099609375, 1.8984375).astype(jnp.bfloat16),
        "w_gate": scatter_about(key_list[8], (D, FF), D ** -0.5, 0.125, ((0, 64), (1, 2))),
        "w_up": scatter_about(key_list[9], (D, FF), D ** -0.5, 0.125, ((0, 64), (1, 2))),
        "w_down": scatter_about(key_list[10], (FF, D), (FF // 4) ** -0.5, 0.125, ((0, 2), (1, 64))),
        "cotangent": gaussian_with(key_list[11], (TOKENS, D), 1.0, 24.0, ((0, 128),), (0, 1, 128, 5.5)),
    }


EPSILON = 1e-05
ROPE_BASE = 500000.0
MASKED = -1e+30
PRECISE = lax.Precision.HIGHEST

@jax.custom_vjp
def low(v):
    return lax.optimization_barrier(v.astype(jnp.bfloat16)).astype(jnp.float32)

@jax.custom_vjp
def low_back(v):
    return v

def low_keep(v):
    return (low(v), None)

def low_pass(kept, grad):
    return (grad,)

def back_keep(v):
    return (v, None)

def back_low(kept, grad):
    return (low(grad),)
low.defvjp(low_keep, low_pass)
low_back.defvjp(back_keep, back_low)

def rms_norm(values, gain_row):
    return values * lax.rsqrt(lax.optimization_barrier(jnp.mean(values * values, axis=-1, keepdims=True)) + EPSILON) * gain_row

def positions_of(segment):
    earlier = lax.optimization_barrier(jnp.sum((segment[None, :] < segment[:, None]).astype(jnp.int32), axis=1))
    return jnp.arange(segment.shape[0], dtype=jnp.int32) - earlier

def rotary_tables(positions, half_width):
    exponent = jnp.arange(half_width).astype(jnp.float32) / half_width
    frequency = jnp.exp(-math.log(ROPE_BASE) * exponent)
    angles = positions.astype(jnp.float32)[..., None] * frequency
    return (jnp.cos(angles)[..., None, :], jnp.sin(angles)[..., None, :])

def rotate(values, cosines, sines):
    half_width = values.shape[-1] // 2
    first_half = values[..., :half_width]
    second_half = values[..., half_width:]
    return jnp.concatenate([first_half * cosines - second_half * sines, second_half * cosines + first_half * sines], axis=-1)

def attend_block(pieces):
    query_rot, key_rot, value_rows, allowed = pieces
    scores = low_back(jnp.einsum('ahgd,bhd->hgab', query_rot, key_rot, precision=PRECISE) * (1.0 / math.sqrt(HEAD)))
    scores = jnp.where(allowed, scores, MASKED)
    row_max = lax.optimization_barrier(jnp.max(scores, axis=-1, keepdims=True))
    weights = jnp.exp(scores - row_max)
    attention = low(weights / lax.optimization_barrier(jnp.sum(weights, axis=-1, keepdims=True)))
    return jnp.einsum('hgab,bhd->ahgd', attention, value_rows, precision=PRECISE)

def reference(tokens, segment_ids, attn_gain, w_query, w_key, w_value, w_out, mlp_gain, w_gate, w_up, w_down, cotangent):
    group_size = HEADS // KV_HEADS
    segments = segment_ids.reshape(N_DP, TOK_DEV)
    positions = jax.vmap(positions_of)(segments)
    cosines, sines = rotary_tables(positions, HEAD // 2)
    token_order = jnp.arange(TOK_DEV)
    allowed = (segments[:, :, None] == segments[:, None, :]) & (token_order[None, None, :] <= token_order[None, :, None])
    attend_saved = jax.checkpoint(attend_block)

    def forward(resid_in, gain_attn, query_map, key_map, value_map, out_map, gain_mlp, gate_map, up_map, down_map):
        normed = low(rms_norm(resid_in, gain_attn))
        query = low_back(jnp.dot(normed, query_map, precision=PRECISE)).reshape(N_DP, TOK_DEV, HEADS, HEAD)
        key_rows = low_back(jnp.dot(normed, key_map, precision=PRECISE)).reshape(N_DP, TOK_DEV, KV_HEADS, HEAD)
        value_rows = low(low_back(jnp.dot(normed, value_map, precision=PRECISE))).reshape(N_DP, TOK_DEV, KV_HEADS, HEAD)
        query_rot = low(rotate(query, cosines, sines)).reshape(N_DP, TOK_DEV, KV_HEADS, group_size, HEAD)
        key_rot = low(rotate(key_rows, cosines, sines))
        mixed = lax.map(attend_saved, (query_rot, key_rot, value_rows, allowed))
        mixed = low(low_back(mixed.reshape(TOKENS, HEADS * HEAD)))
        resid = resid_in + low_back(jnp.dot(mixed, out_map, precision=PRECISE))
        normed2 = low(rms_norm(resid, gain_mlp))
        gate = low_back(jnp.dot(normed2, gate_map, precision=PRECISE))
        up_rows = low_back(jnp.dot(normed2, up_map, precision=PRECISE))
        hidden = low(jax.nn.silu(gate) * up_rows)
        return resid + low_back(jnp.dot(hidden, down_map, precision=PRECISE))
    result, pullback = jax.vjp(forward, tokens.astype(jnp.float32), attn_gain.astype(jnp.float32), w_query.astype(jnp.float32), w_key.astype(jnp.float32), w_value.astype(jnp.float32), w_out.astype(jnp.float32), mlp_gain.astype(jnp.float32), w_gate.astype(jnp.float32), w_up.astype(jnp.float32), w_down.astype(jnp.float32))
    grads = pullback(cotangent.astype(jnp.float32))
    return (result.astype(jnp.bfloat16), grads[0], grads[1], grads[2], grads[3], grads[4], grads[5], grads[6], grads[7], grads[8], grads[9])
```

```python
import math

import jax
import jax.numpy as jnp
from jax import lax
from jax.sharding import Mesh
from jax.sharding import PartitionSpec as P

HEADS = 32
KV_HEADS = 8
GROUP = HEADS // KV_HEADS
EPSILON = 1e-05
ROPE_BASE = 500000.0
MASKED = -1e30
GAIN_COLS = 128
BF = jnp.bfloat16
F32 = jnp.float32

SWAP = [(0, 1), (1, 0)]


def mm(left, right):
    return jnp.dot(left, right, preferred_element_type=F32)


def mm_nt(left, right):
    return lax.dot_general(left, right, (((1,), (1,)), ((), ())), preferred_element_type=F32)


def mm_tn(left, right):
    return lax.dot_general(left, right, (((0,), (0,)), ((), ())), preferred_element_type=F32)


AT = (0, 2, 1, 3)


def from_chip(value, k):
    return lax.ppermute(value, ("a", "t"), [(AT[(i + k) % 4], AT[i]) for i in range(4)])


def to_chip(value, k):
    return lax.ppermute(value, ("a", "t"), [(AT[i], AT[(i + k) % 4]) for i in range(4)])


def gather_rows(rows):
    mine = jnp.concatenate(
        [rows, from_chip(rows, 2), from_chip(rows, 1), from_chip(rows, 3)], axis=0
    )
    return jnp.concatenate([mine, lax.ppermute(mine, "c", SWAP)], axis=0)


def scatter_rows(partial):
    half = partial.shape[0] // 2
    other = lax.ppermute(partial[half:].astype(BF), "c", SWAP)
    chip = partial[:half] + other.astype(F32)
    part = half // 4
    own, p2, p1, p3 = (chip[i * part : (i + 1) * part] for i in range(4))
    total = own
    for piece, k in ((p2, 2), (p1, 1), (p3, 3)):
        total = total + to_chip(piece.astype(BF), k).astype(F32)
    return total


def spread(pack, a, c):
    _, r, n = pack.shape
    by_core = pack.reshape(2, 2, r, n)
    keep = lax.dynamic_index_in_dim(by_core, c, 1, keepdims=False)
    give = lax.dynamic_index_in_dim(by_core, 1 - c, 1, keepdims=False)
    got = lax.ppermute(give, "c", SWAP)
    first = c == 0
    both = jnp.concatenate([jnp.where(first, keep, got), jnp.where(first, got, keep)], axis=1)
    keep_a = lax.dynamic_index_in_dim(both, a, 0, keepdims=False)
    give_a = lax.dynamic_index_in_dim(both, 1 - a, 0, keepdims=False)
    got_a = lax.ppermute(give_a, "a", SWAP)
    first_a = a == 0
    return jnp.where(first_a, keep_a, got_a), jnp.where(first_a, got_a, keep_a)


def unspread(low, high, a, c):
    rows, n = low.shape
    r = rows // 2
    first_a = a == 0
    keep_a = jnp.where(first_a, low, high)
    give_a = jnp.where(first_a, high, low)
    got_a = lax.ppermute(give_a, "a", SWAP)
    quarters = jnp.stack([jnp.where(first_a, keep_a, got_a), jnp.where(first_a, got_a, keep_a)])
    quarters = quarters.reshape(2, 2, r, n)
    keep = lax.dynamic_index_in_dim(quarters, c, 1, keepdims=False)
    give = lax.dynamic_index_in_dim(quarters, 1 - c, 1, keepdims=False)
    got = lax.ppermute(give, "c", SWAP)
    first = c == 0
    return jnp.stack([jnp.where(first, keep, got), jnp.where(first, got, keep)], axis=1).reshape(
        4, r, n
    )


def quarters_of(weight):
    rows, columns = weight.shape
    return weight.reshape(rows, 4, columns // 4).transpose(1, 0, 2)


def whole_columns(quarters):
    _, rows, columns = quarters.shape
    return quarters.transpose(1, 0, 2).reshape(rows, 4 * columns)


def rotate(values, cosines, sines):
    half = values.shape[-1] // 2
    first, second = values[..., :half], values[..., half:]
    return jnp.concatenate([first * cosines - second * sines, second * cosines + first * sines], -1)


def norm_back(rescaled, factor, gain, upstream):
    inner = upstream * gain
    return factor * (inner - rescaled * jnp.mean(inner * rescaled, axis=-1, keepdims=True))


def local(
    tokens, segment_ids, attn_gain, w_query, w_key, w_value, w_out,
    mlp_gain, w_gate, w_up, w_down, cotangent,
):
    a, c, t = lax.axis_index("a"), lax.axis_index("c"), lax.axis_index("t")
    own, d_model = tokens.shape
    block = segment_ids.shape[0]
    r = w_query.shape[0]
    nq = w_query.shape[1] // 4
    nk = w_key.shape[1] // 4
    ff = w_gate.shape[1] // 4
    head = nk
    scale = 1.0 / math.sqrt(head)

    gains = jnp.stack([attn_gain, mlp_gain], axis=1)
    gains = jnp.pad(gains, ((0, 0), (0, GAIN_COLS - 2)))
    attn_pack = jnp.concatenate(
        [
            quarters_of(w_query),
            quarters_of(w_key),
            quarters_of(w_value),
            quarters_of(w_out.T),
            jnp.broadcast_to(gains, (4, r, GAIN_COLS)),
        ],
        axis=2,
    )
    attn_low, attn_high = spread(attn_pack, a, c)
    x_rows = gather_rows(tokens)
    attn_low = lax.all_gather(attn_low, ("z", "y"), axis=0, tiled=True)
    attn_high = lax.all_gather(attn_high, ("z", "y"), axis=0, tiled=True)
    attn_w = jnp.concatenate([attn_low, attn_high], axis=0)
    mlp_pack = jnp.concatenate(
        [quarters_of(w_gate), quarters_of(w_up), quarters_of(w_down.T)], axis=2
    )
    mlp_low, mlp_high = spread(mlp_pack, a, c)
    mlp_low = lax.all_gather(mlp_low, ("z", "y"), axis=0, tiled=True)
    mlp_high = lax.all_gather(mlp_high, ("z", "y"), axis=0, tiled=True)
    half_d = d_model // 2

    cut = nq + 2 * nk
    w_qkv, w_out_t = attn_w[:, :cut], attn_w[:, cut : cut + nq]
    gain_a = attn_w[:, cut + nq].astype(F32)
    gain_m = attn_w[:, cut + nq + 1].astype(F32)

    seg_pair = jnp.stack([segment_ids, lax.ppermute(segment_ids, "a", SWAP)])
    seg = jnp.concatenate([seg_pair, lax.ppermute(seg_pair, "c", SWAP)], axis=0)
    turn = jnp.stack([t, t ^ a, t, t ^ a])[:, None]
    seg = jnp.where(turn == 0, seg, jnp.roll(seg, own, axis=1))
    order = (jnp.arange(block, dtype=jnp.int32)[None, :] + turn * own) % block
    earlier = jnp.sum((seg[:, None, :] < seg[:, :, None]).astype(jnp.int32), axis=2)
    positions = order - earlier
    allowed = (seg[:, :, None] == seg[:, None, :]) & (order[:, None, :] <= order[:, :, None])
    frequency = jnp.exp(
        -math.log(ROPE_BASE) * (jnp.arange(head // 2).astype(F32) / (head // 2))
    )
    angles = positions.astype(F32)[:, :, None, None] * frequency
    cosines, sines = jnp.cos(angles), jnp.sin(angles)

    xf = x_rows.astype(F32)
    factor1 = lax.rsqrt(jnp.mean(xf * xf, axis=-1, keepdims=True) + EPSILON)
    u1 = xf * factor1
    normed = (u1 * gain_a).astype(BF)
    qkv = mm(normed, w_qkv)
    query = rotate(qkv[:, :nq].reshape(4, block, GROUP, head), cosines, sines).astype(BF)
    key = rotate(qkv[:, nq : nq + nk].reshape(4, block, 1, head), cosines, sines)
    key = key.astype(BF).reshape(4, block, head)
    value = qkv[:, nq + nk :].astype(BF).reshape(4, block, head)
    scores = jnp.einsum("nahd,nbd->nhab", query, key, preferred_element_type=F32) * scale
    scores = jnp.where(allowed[:, None], scores, MASKED)
    row_max = jnp.max(scores, axis=-1, keepdims=True)
    weights = jnp.exp(scores - row_max)
    probs = weights / jnp.sum(weights, axis=-1, keepdims=True)
    probs_b = probs.astype(BF)
    mixed = jnp.einsum("nhab,nbd->nahd", probs_b, value, preferred_element_type=F32)
    mixed = mixed.astype(BF).reshape(4 * block, nq)
    resid = tokens.astype(F32) + scatter_rows(mm_nt(mixed, w_out_t))

    factor2 = lax.rsqrt(jnp.mean(resid * resid, axis=-1, keepdims=True) + EPSILON)
    u2 = resid * factor2
    n2 = gather_rows((u2 * gain_m).astype(BF))
    c_rows = gather_rows(cotangent)
    gate_up = mm(n2[:, :half_d], mlp_low[:, : 2 * ff]) + mm(n2[:, half_d:], mlp_high[:, : 2 * ff])
    gate, up = gate_up[:, :ff], gate_up[:, ff:]
    sig = jax.nn.sigmoid(gate)
    silu = gate * sig
    hidden = (silu * up).astype(BF)
    d_hidden = mm(c_rows[:, :half_d], mlp_low[:, 2 * ff :]) + mm(
        c_rows[:, half_d:], mlp_high[:, 2 * ff :]
    )
    d_gate = (d_hidden * up * sig * (1.0 + gate * (1.0 - sig))).astype(BF)
    d_up = (d_hidden * silu).astype(BF)
    d_gu = jnp.concatenate([d_gate, d_up], axis=1)
    d_n2 = scatter_rows(
        jnp.concatenate(
            [mm_nt(d_gu, mlp_low[:, : 2 * ff]), mm_nt(d_gu, mlp_high[:, : 2 * ff])], axis=1
        )
    )

    def mlp_grads(part):
        grads = jnp.concatenate(
            [mm_tn(n2[:, part], d_gu).astype(BF), mm_tn(c_rows[:, part], hidden).astype(BF)], axis=1
        )
        return lax.psum_scatter(grads, ("z", "y"), scatter_dimension=0, tiled=True)

    g_low = mlp_grads(slice(0, half_d))
    g_high = mlp_grads(slice(half_d, d_model))
    out_part = jnp.concatenate(
        [mm_nt(hidden, mlp_low[:, 2 * ff :]), mm_nt(hidden, mlp_high[:, 2 * ff :])], axis=1
    )
    layer_output = (resid + scatter_rows(out_part)).astype(BF)

    upstream = cotangent.astype(F32)
    mlp_gain_part = jnp.sum(d_n2 * u2, axis=0)
    d_resid = upstream + norm_back(u2, factor2, gain_m, d_n2)
    d_branch = gather_rows(d_resid.astype(BF))

    out_grad = mm_tn(d_branch, mixed)
    d_mixed = mm(d_branch, w_out_t).astype(BF).reshape(4, block, GROUP, head)
    d_value = jnp.einsum("nhab,nahd->nbd", probs_b, d_mixed, preferred_element_type=F32)
    d_probs = jnp.einsum("nahd,nbd->nhab", d_mixed, value, preferred_element_type=F32)
    d_scores = (probs * (d_probs - jnp.sum(d_probs * probs, axis=-1, keepdims=True))).astype(BF)
    d_query = jnp.einsum("nhab,nbd->nahd", d_scores, key, preferred_element_type=F32) * scale
    d_key = jnp.einsum("nhab,nahd->nbd", d_scores, query, preferred_element_type=F32) * scale
    d_query = rotate(d_query, cosines, -sines).astype(BF).reshape(4 * block, nq)
    d_key = rotate(d_key[:, :, None, :], cosines, -sines).astype(BF).reshape(4 * block, nk)
    d_value = d_value.astype(BF).reshape(4 * block, nk)
    d_qkv = jnp.concatenate([d_query, d_key, d_value], axis=1)
    qkv_grad = mm_tn(normed, d_qkv)
    d_n1_part = mm_nt(d_qkv, w_qkv)
    attn_gain_part = jnp.sum(d_n1_part * u1, axis=0)
    d_n1 = scatter_rows(d_n1_part)
    input_grad = d_resid + norm_back(u1[:own], factor1[:own], gain_a, d_n1)

    gain_parts = jnp.stack([attn_gain_part, mlp_gain_part], axis=1).astype(BF)
    gain_parts = jnp.pad(gain_parts, ((0, 0), (0, GAIN_COLS - 2)))
    attn_grads = jnp.concatenate([qkv_grad.astype(BF), out_grad.astype(BF), gain_parts], axis=1)
    h_low = lax.psum_scatter(attn_grads[:half_d], ("z", "y"), scatter_dimension=0, tiled=True)
    h_high = lax.psum_scatter(attn_grads[half_d:], ("z", "y"), scatter_dimension=0, tiled=True)

    g = unspread(g_low, g_high, a, c).astype(F32)
    gate_grad = whole_columns(g[:, :, :ff])
    up_grad = whole_columns(g[:, :, ff : 2 * ff])
    down_grad = whole_columns(g[:, :, 2 * ff :]).T
    h = unspread(h_low, h_high, a, c).astype(F32)
    query_grad = whole_columns(h[:, :, :nq])
    key_grad = whole_columns(h[:, :, nq : nq + nk])
    value_grad = whole_columns(h[:, :, nq + nk : cut])
    out_grad = whole_columns(h[:, :, cut : cut + nq]).T
    gain_grads = jnp.sum(h[:, :, cut + nq : cut + nq + 2], axis=0).T
    gain_grads = gain_grads + lax.ppermute(gain_grads, "t", SWAP)
    return (
        layer_output, input_grad, gain_grads[0], query_grad, key_grad, value_grad, out_grad,
        gain_grads[1], gate_grad, up_grad, down_grad,
    )


def solution(mesh):
    fine = Mesh(mesh.devices.reshape(2, 4, 4, 2, 2), ("a", "z", "y", "c", "t"))
    dp = ("a", "z", "y", "c")
    rows = P(dp + ("t",), None)
    return jax.shard_map(
        local,
        mesh=fine,
        in_specs=(
            rows, P(dp), P(dp), P(dp, "t"), P(dp, "t"), P(dp, "t"), P("t", dp),
            P(dp), P(dp, "t"), P(dp, "t"), P("t", dp), rows,
        ),
        out_specs=(
            rows, rows, P(dp), P(dp, "t"), P(dp, "t"), P(dp, "t"), P("t", dp),
            P(dp), P(dp, "t"), P(dp, "t"), P("t", dp),
        ),
        check_vma=False,
    )
```

```python
import math

import jax
import jax.numpy as jnp
from jax import lax
from jax.experimental import pallas as pl
from jax.experimental.pallas import tpu as pltpu
from jax.sharding import Mesh
from jax.sharding import PartitionSpec as P

HEADS = 32
KV_HEADS = 8
GROUP = HEADS // KV_HEADS
EPSILON = 1e-05
ROPE_BASE = 500000.0
MASKED = -1e30
GAIN_COLS = 128
VMEM_LIMIT = 56 * 2**20
BF = jnp.bfloat16
F32 = jnp.float32

SWAP = [(0, 1), (1, 0)]


def mm(left, right):
    return jnp.dot(left, right, preferred_element_type=F32)


def mm_nt(left, right):
    return lax.dot_general(left, right, (((1,), (1,)), ((), ())), preferred_element_type=F32)


def mm_tn(left, right):
    return lax.dot_general(left, right, (((0,), (0,)), ((), ())), preferred_element_type=F32)


AT = (0, 2, 1, 3)


def from_chip(value, k):
    return lax.ppermute(value, ("a", "t"), [(AT[(i + k) % 4], AT[i]) for i in range(4)])


def to_chip(value, k):
    return lax.ppermute(value, ("a", "t"), [(AT[i], AT[(i + k) % 4]) for i in range(4)])


def gather_rows(rows):
    mine = [rows, from_chip(rows, 2), from_chip(rows, 1), from_chip(rows, 3)]
    return mine + [lax.ppermute(piece, "c", SWAP) for piece in mine]


def scatter_rows(mine, other):
    got = lax.ppermute(other, "c", SWAP)
    rows = mine.shape[0] // 4
    chip = [
        mine[i * rows : (i + 1) * rows].astype(F32) + got[i * rows : (i + 1) * rows].astype(F32)
        for i in range(4)
    ]
    total = chip[0]
    for i, k in ((1, 2), (2, 1), (3, 3)):
        total = total + to_chip(chip[i].astype(BF), k).astype(F32)
    return total


def spread(pack, a, c):
    _, r, n = pack.shape
    by_core = pack.reshape(2, 2, r, n)
    keep = lax.dynamic_index_in_dim(by_core, c, 1, keepdims=False)
    give = lax.dynamic_index_in_dim(by_core, 1 - c, 1, keepdims=False)
    got = lax.ppermute(give, "c", SWAP)
    first = c == 0
    both = jnp.concatenate([jnp.where(first, keep, got), jnp.where(first, got, keep)], axis=1)
    keep_a = lax.dynamic_index_in_dim(both, a, 0, keepdims=False)
    give_a = lax.dynamic_index_in_dim(both, 1 - a, 0, keepdims=False)
    got_a = lax.ppermute(give_a, "a", SWAP)
    first_a = a == 0
    return jnp.concatenate(
        [jnp.where(first_a, keep_a, got_a), jnp.where(first_a, got_a, keep_a)], axis=0
    )


def unspread(rows, a, c):
    r, n = rows.shape[0] // 4, rows.shape[1]
    low, high = rows[: 2 * r], rows[2 * r :]
    first_a = a == 0
    keep_a = jnp.where(first_a, low, high)
    give_a = jnp.where(first_a, high, low)
    got_a = lax.ppermute(give_a, "a", SWAP)
    quarters = jnp.stack([jnp.where(first_a, keep_a, got_a), jnp.where(first_a, got_a, keep_a)])
    quarters = quarters.reshape(2, 2, r, n)
    keep = lax.dynamic_index_in_dim(quarters, c, 1, keepdims=False)
    give = lax.dynamic_index_in_dim(quarters, 1 - c, 1, keepdims=False)
    got = lax.ppermute(give, "c", SWAP)
    first = c == 0
    return jnp.stack([jnp.where(first, keep, got), jnp.where(first, got, keep)], axis=1).reshape(
        4, r, n
    )


def scatter_along(grads, axis, place):
    total = lax.dynamic_index_in_dim(grads, place, 1, keepdims=False).astype(F32)
    for k in (2, 1, 3):
        piece = lax.dynamic_index_in_dim(grads, (place + k) % 4, 1, keepdims=False)
        got = lax.ppermute(piece, axis, [(i, (i + k) % 4) for i in range(4)])
        total = total + got.astype(F32)
    return total


def scatter_zy(grads, first):
    rows, n = grads.shape
    i = rows // 16
    z, y = lax.axis_index("z"), lax.axis_index("y")
    if first == "z":
        part = scatter_along(grads.reshape(1, 4, 4 * i, n), "z", z).astype(BF)
        part = scatter_along(part.reshape(1, 4, i, n), "y", y)
    else:
        part = scatter_along(grads.reshape(4, 4, i, n), "y", y).astype(BF)
        part = scatter_along(part.reshape(1, 4, i, n), "z", z)
    return part.reshape(i, n).astype(BF)


def quarters_of(weight):
    rows, columns = weight.shape
    return weight.reshape(rows, 4, columns // 4).transpose(1, 0, 2)


def whole_columns(quarters):
    _, rows, columns = quarters.shape
    return quarters.transpose(1, 0, 2).reshape(rows, 4 * columns)


def to_place(rows):
    n, d = rows.shape
    return rows.reshape(n, 2, 16, d // 32).transpose(0, 2, 1, 3).reshape(n, d)


def from_place(rows):
    n, d = rows.shape
    return rows.reshape(n, 16, 2, d // 32).transpose(0, 2, 1, 3).reshape(n, d)


def norm_back(rescaled, factor, gain, upstream):
    inner = upstream * gain
    return factor * (inner - rescaled * jnp.mean(inner * rescaled, axis=-1, keepdims=True))


def step_block(s):
    return (s + 2) % 4


def row_block(width):
    return lambda rows: pl.BlockSpec((rows, width), lambda s: (step_block(s), 0))


def fixed(shape):
    return pl.BlockSpec(shape, lambda *_: (0,) * len(shape))


def halves(rows, width):
    return [
        pl.BlockSpec((rows, width), lambda s: (jnp.maximum(s - 2, 0), 0)),
        pl.BlockSpec((rows, width), lambda s: (jnp.minimum(s, 1), 0)),
    ]


def load_block(s, pieces, scratch):
    part = pieces[0].shape[0]
    for b in range(4):

        @pl.when(step_block(s) == b)
        def _():
            scratch[:part] = pieces[2 * b][...]
            scratch[part:] = pieces[2 * b + 1][...]


def store_half(s, mine_ref, other_ref, value):
    @pl.when(s < 2)
    def _():
        other_ref[...] = value

    @pl.when(s >= 2)
    def _():
        mine_ref[...] = value


def pick_rows(columns):
    one = (
        lax.broadcasted_iota(jnp.int32, (8, columns.shape[1]), 0)
        == lax.broadcasted_iota(jnp.int32, (8, columns.shape[1]), 1)
    ).astype(BF)
    return mm_nt(one, columns)


def turn(values, cosines, sines, head):
    width = values.shape[1]
    lane = lax.broadcasted_iota(jnp.int32, values.shape, 1)
    low = lane % head < head // 2
    partner = jnp.where(
        low, pltpu.roll(values, width - head // 2, 1), pltpu.roll(values, head // 2, 1)
    )
    return values * cosines + partner * sines


def double(values, times):
    return jnp.concatenate([values] * times, axis=1)


def by_head(values, head):
    lane = lax.broadcasted_iota(jnp.int32, values.shape, 1) // head
    zero = jnp.zeros_like(values)
    return jnp.concatenate([jnp.where(lane == h, values, zero) for h in range(GROUP)], axis=0)


def take_heads(values, rows, head):
    lane = lax.broadcasted_iota(jnp.int32, (rows, values.shape[1]), 1) // head
    out = values[:rows]
    for h in range(1, GROUP):
        out = jnp.where(lane == h, values[h * rows : (h + 1) * rows], out)
    return out


def fold_heads(values, head):
    pair = values[:, : 2 * head] + values[:, 2 * head :]
    return pair + pltpu.roll(pair, head, 1)


def attn_forward_kernel(head, *refs):
    pieces = refs[:8]
    (w_ref, cos_ref, sin_ref, mask_ref,
     mine_ref, other_ref, normed_ref, factor_ref, q_ref, k_ref, v_ref, probs_ref, mixed_ref,
     gains_ref, x_ref, gain_scr) = refs[8:]
    s = pl.program_id(0)
    nq, cut = GROUP * head, (GROUP + 2) * head
    rows = x_ref.shape[0]

    @pl.when(s == 0)
    def _():
        gain_scr[...] = pick_rows(w_ref[:, cut + nq :])
        gains_ref[...] = gain_scr[...]

    load_block(s, pieces, x_ref)
    x = x_ref[...].astype(F32)
    factor = lax.rsqrt(jnp.mean(x * x, axis=-1, keepdims=True) + EPSILON)
    factor_ref[...] = jnp.broadcast_to(factor, factor_ref.shape)
    normed = (x * factor * gain_scr[0:1, :]).astype(BF)
    normed_ref[...] = normed
    qkv = mm(normed, w_ref[:, :cut])
    cosines, sines = cos_ref[...], sin_ref[...]
    query = turn(qkv[:, :nq], double(cosines, 2), double(sines, 2), head).astype(BF)
    kv = qkv[:, nq:]
    turned = turn(kv, cosines, sines, head)
    low = lax.broadcasted_iota(jnp.int32, kv.shape, 1) < head
    key = double(jnp.where(low, turned, pltpu.roll(turned, head, 1)), 2).astype(BF)
    value = double(jnp.where(low, pltpu.roll(kv, head, 1), kv), 2).astype(BF)
    q_ref[...] = query
    k_ref[...] = key
    v_ref[...] = value
    scores = mm_nt(by_head(query, head), key) * (1.0 / math.sqrt(head))
    allowed = mask_ref[...] == 0
    scores = jnp.where(jnp.concatenate([allowed] * GROUP, axis=0), scores, MASKED)
    weights = jnp.exp(scores - jnp.max(scores, axis=-1, keepdims=True))
    probs = weights / jnp.sum(weights, axis=-1, keepdims=True)
    probs_ref[...] = probs
    mixed = take_heads(mm(probs.astype(BF), value), rows, head).astype(BF)
    mixed_ref[...] = mixed
    store_half(s, mine_ref, other_ref, mm_nt(mixed, w_ref[:, cut : cut + nq]).astype(BF))


def attn_forward(pieces, w, cosines, sines, mask, head):
    part, d = pieces[0].shape
    rows = 2 * part
    nq = GROUP * head
    spec = lambda width: row_block(width)(rows)
    return pl.pallas_call(
        lambda *refs: attn_forward_kernel(head, *refs),
        grid=(4,),
        in_specs=[fixed(p.shape) for p in pieces]
        + [fixed(w.shape), spec(2 * head), spec(2 * head), spec(rows)],
        out_specs=halves(rows, d)
        + [spec(d), spec(128), spec(nq), spec(nq), spec(nq)]
        + [pl.BlockSpec((GROUP * rows, rows), lambda s: (step_block(s), 0)), spec(nq), fixed((8, d))],
        out_shape=[jax.ShapeDtypeStruct((2 * rows, d), BF)] * 2
        + [jax.ShapeDtypeStruct((4 * rows, d), BF), jax.ShapeDtypeStruct((4 * rows, 128), F32)]
        + [jax.ShapeDtypeStruct((4 * rows, nq), BF)] * 3
        + [
            jax.ShapeDtypeStruct((4 * GROUP * rows, rows), F32),
            jax.ShapeDtypeStruct((4 * rows, nq), BF),
            jax.ShapeDtypeStruct((8, d), F32),
        ],
        scratch_shapes=[pltpu.VMEM((rows, d), BF), pltpu.VMEM((8, d), F32)],
        compiler_params=pltpu.CompilerParams(vmem_limit_bytes=VMEM_LIMIT),
        cost_estimate=pl.CostEstimate(
            flops=8 * rows * d * (GROUP * 2 + 2) * head + 16 * rows * rows * nq * 2,
            bytes_accessed=20 * 2**20,
            transcendentals=16 * rows * rows,
        ),
    )(*pieces, w, cosines, sines, mask)


def attn_backward_kernel(head, *refs):
    d_pieces, x_pieces = refs[:8], refs[8:16]
    (w_ref, cos_ref, sin_ref, factor_ref, normed_ref, q_ref, k_ref, v_ref, probs_ref, mixed_ref,
     extra_ref,
     mine_ref, other_ref, gq_ref, gkv_ref, go_ref,
     db_ref, x_ref, acc_q, acc_kv, acc_o, gain_acc) = refs[16:]
    s = pl.program_id(0)
    nq, cut = GROUP * head, (GROUP + 2) * head
    rows = x_ref.shape[0]
    scale = 1.0 / math.sqrt(head)

    @pl.when(s == 0)
    def _():
        acc_q[...] = jnp.zeros_like(acc_q)
        acc_kv[...] = jnp.zeros_like(acc_kv)
        acc_o[...] = jnp.zeros_like(acc_o)
        gain_acc[...] = jnp.zeros_like(gain_acc)

    load_block(s, d_pieces, db_ref)
    load_block(s, x_pieces, x_ref)
    d_branch = db_ref[...]
    acc_o[...] += mm_tn(d_branch, mixed_ref[...])
    d_mixed = by_head(mm(d_branch, w_ref[:, cut : cut + nq]).astype(BF), head)
    d_probs = mm_nt(d_mixed, v_ref[...])
    probs = probs_ref[...]
    d_value = fold_heads(mm_tn(probs.astype(BF), d_mixed), head)
    d_scores = probs * (d_probs - jnp.sum(d_probs * probs, axis=-1, keepdims=True))
    d_scores = d_scores.astype(BF)
    d_query = take_heads(mm(d_scores, k_ref[...]), rows, head) * scale
    d_key = fold_heads(mm_tn(d_scores, by_head(q_ref[...], head)), head) * scale
    cosines, sines = cos_ref[...], -sin_ref[...]
    d_query = turn(d_query, double(cosines, 2), double(sines, 2), head).astype(BF)
    d_key = turn(d_key, cosines, sines, head)
    low = lax.broadcasted_iota(jnp.int32, d_key.shape, 1) < head
    d_kv = jnp.where(low, d_key, d_value).astype(BF)
    normed = normed_ref[...]
    acc_q[...] += mm_tn(normed, d_query)
    acc_kv[...] += mm_tn(normed, d_kv)
    d_normed = mm_nt(d_query, w_ref[:, :nq]) + mm_nt(d_kv, w_ref[:, nq:cut])
    store_half(s, mine_ref, other_ref, d_normed.astype(BF))
    u1 = x_ref[...].astype(F32) * factor_ref[:, :1]
    gain_acc[0:1, :] += jnp.sum(d_normed * u1, axis=0, keepdims=True)

    @pl.when(s == 3)
    def _():
        gq_ref[...] = acc_q[...].astype(BF)
        go_ref[...] = acc_o[...].astype(BF)
        gkv_ref[:, : 2 * head] = acc_kv[...].astype(BF)
        gains = gain_acc[...] + extra_ref[...]
        one = (
            lax.broadcasted_iota(jnp.int32, (8, 128), 0)
            == lax.broadcasted_iota(jnp.int32, (8, 128), 1)
        ).astype(BF)
        gkv_ref[:, 2 * head :] = mm_tn(gains.astype(BF), one).astype(BF)


def attn_backward(d_pieces, x_pieces, w, cosines, sines, saved, extra, head):
    factor, normed, query, key, value, probs, mixed = saved
    part, d = d_pieces[0].shape
    rows = 2 * part
    nq = GROUP * head
    spec = lambda width: row_block(width)(rows)
    return pl.pallas_call(
        lambda *refs: attn_backward_kernel(head, *refs),
        grid=(4,),
        in_specs=[fixed(p.shape) for p in (*d_pieces, *x_pieces)]
        + [fixed(w.shape), spec(2 * head), spec(2 * head), spec(128), spec(d)]
        + [spec(nq), spec(nq), spec(nq)]
        + [pl.BlockSpec((GROUP * rows, rows), lambda s: (step_block(s), 0)), spec(nq), fixed((8, d))],
        out_specs=halves(rows, d) + [fixed((d, nq)), fixed((d, 2 * head + 128)), fixed((d, nq))],
        out_shape=[jax.ShapeDtypeStruct((2 * rows, d), BF)] * 2
        + [
            jax.ShapeDtypeStruct((d, nq), BF),
            jax.ShapeDtypeStruct((d, 2 * head + 128), BF),
            jax.ShapeDtypeStruct((d, nq), BF),
        ],
        scratch_shapes=[
            pltpu.VMEM((rows, d), BF),
            pltpu.VMEM((rows, d), BF),
            pltpu.VMEM((d, nq), F32),
            pltpu.VMEM((d, 2 * head), F32),
            pltpu.VMEM((d, nq), F32),
            pltpu.VMEM((8, d), F32),
        ],
        compiler_params=pltpu.CompilerParams(vmem_limit_bytes=VMEM_LIMIT),
        cost_estimate=pl.CostEstimate(
            flops=16 * rows * d * (GROUP * 2 + 2) * head + 16 * rows * rows * nq * 6,
            bytes_accessed=30 * 2**20,
            transcendentals=0,
        ),
    )(*d_pieces, *x_pieces, w, cosines, sines, factor, normed, query, key, value, probs, mixed, extra)


def mlp_kernel(tile, *refs):
    n_pieces, c_pieces = refs[:8], refs[8:16]
    w_ref, h_ref, mine_ref, other_ref, n_ref, c_ref, acc = refs[16:]
    j = pl.program_id(0)
    part = n_pieces[0].shape[0]

    @pl.when(j == 0)
    def _():
        for i in range(8):
            n_ref[i * part : (i + 1) * part] = n_pieces[i][...]
            c_ref[i * part : (i + 1) * part] = c_pieces[i][...]

    chunk = 4 * part
    for m in range(2):
        rows = slice(m * chunk, (m + 1) * chunk)
        gate_up = mm(n_ref[rows], w_ref[:, : 2 * tile])
        d_hidden = mm(c_ref[rows], w_ref[:, 2 * tile :])
        gate, up = gate_up[:, :tile], gate_up[:, tile:]
        sig = jax.nn.sigmoid(gate)
        silu = gate * sig
        h_ref[rows, 2 * tile :] = (silu * up).astype(BF)
        h_ref[rows, :tile] = (d_hidden * up * sig * (1.0 + gate * (1.0 - sig))).astype(BF)
        h_ref[rows, tile : 2 * tile] = (d_hidden * silu).astype(BF)
        update = mm_nt(h_ref[rows, : 2 * tile], w_ref[:, : 2 * tile])

        @pl.when(j == 0)
        def _():
            acc[rows] = update

        @pl.when((j > 0) & (j < 3))
        def _():
            acc[rows] += update

        @pl.when(j == 3)
        def _():
            (mine_ref, other_ref)[m][...] = (acc[rows] + update).astype(BF)


def mlp(n_pieces, c_pieces, w):
    part, d = n_pieces[0].shape
    rows, columns = 8 * part, w.shape[1]
    tile = columns // 12
    once = lambda shape: pl.BlockSpec(shape, lambda j: (0, 0))
    return pl.pallas_call(
        lambda *refs: mlp_kernel(tile, *refs),
        grid=(4,),
        in_specs=[once((part, d))] * 16 + [pl.BlockSpec((d, 3 * tile), lambda j: (0, j))],
        out_specs=[pl.BlockSpec((rows, 3 * tile), lambda j: (0, j))]
        + [once((rows // 2, d))] * 2
        + [once((rows, d))] * 2,
        out_shape=[jax.ShapeDtypeStruct((rows, columns), BF)]
        + [jax.ShapeDtypeStruct((rows // 2, d), BF)] * 2
        + [jax.ShapeDtypeStruct((rows, d), BF)] * 2,
        scratch_shapes=[pltpu.VMEM((rows, d), F32)],
        compiler_params=pltpu.CompilerParams(vmem_limit_bytes=VMEM_LIMIT),
        cost_estimate=pl.CostEstimate(
            flops=2 * rows * d * columns * 5 // 3, bytes_accessed=40 * 2**20, transcendentals=0
        ),
    )(*n_pieces, *c_pieces, w)


def mlp_grads_kernel(tile, n_ref, c_ref, h_ref, w_ref, g_ref, mine_ref, other_ref, nt, ct, acc):
    j = pl.program_id(0)

    @pl.when(j == 0)
    def _():
        nt[...] = n_ref[...].T
        ct[...] = c_ref[...].T

    g_ref[:, : 2 * tile] = mm(nt[...], h_ref[:, : 2 * tile]).astype(BF)
    g_ref[:, 2 * tile :] = mm(ct[...], h_ref[:, 2 * tile :]).astype(BF)
    half = acc.shape[0] // 2
    for m in range(2):
        rows = slice(m * half, (m + 1) * half)
        update = mm_nt(h_ref[rows, 2 * tile :], w_ref[...])

        @pl.when(j == 0)
        def _():
            acc[rows] = update

        @pl.when((j > 0) & (j < 3))
        def _():
            acc[rows] += update

        @pl.when(j == 3)
        def _():
            (mine_ref, other_ref)[m][...] = (acc[rows] + update).astype(BF)


def mlp_grads(n_all, c_all, h_all, w):
    rows, d = n_all.shape
    columns = h_all.shape[1]
    tile = columns // 12
    once = lambda shape: pl.BlockSpec(shape, lambda j: (0, 0))
    return pl.pallas_call(
        lambda *refs: mlp_grads_kernel(tile, *refs),
        grid=(4,),
        in_specs=[once((rows, d))] * 2
        + [
            pl.BlockSpec((rows, 3 * tile), lambda j: (0, j)),
            pl.BlockSpec((d, tile), lambda j: (0, 3 * j + 2)),
        ],
        out_specs=[pl.BlockSpec((d, 3 * tile), lambda j: (0, j))] + [once((rows // 2, d))] * 2,
        out_shape=[jax.ShapeDtypeStruct((d, columns), BF)]
        + [jax.ShapeDtypeStruct((rows // 2, d), BF)] * 2,
        scratch_shapes=[
            pltpu.VMEM((d, rows), BF),
            pltpu.VMEM((d, rows), BF),
            pltpu.VMEM((rows, d), F32),
        ],
        compiler_params=pltpu.CompilerParams(vmem_limit_bytes=VMEM_LIMIT),
        cost_estimate=pl.CostEstimate(
            flops=2 * rows * d * columns * 4 // 3, bytes_accessed=40 * 2**20, transcendentals=0
        ),
    )(n_all, c_all, h_all, w)


def local(
    tokens, segment_ids, attn_gain, w_query, w_key, w_value, w_out,
    mlp_gain, w_gate, w_up, w_down, cotangent,
):
    a, c, t = lax.axis_index("a"), lax.axis_index("c"), lax.axis_index("t")
    own, d_model = tokens.shape
    block = segment_ids.shape[0]
    r = w_query.shape[0]
    nq = w_query.shape[1] // 4
    nk = w_key.shape[1] // 4
    ff = w_gate.shape[1] // 4
    head = nk
    tile = ff // 4
    cut = nq + 2 * nk

    gains = jnp.stack([attn_gain, mlp_gain], axis=1)
    gains = jnp.pad(gains, ((0, 0), (0, GAIN_COLS - 2)))
    attn_pack = jnp.concatenate(
        [
            quarters_of(w_query),
            quarters_of(w_key),
            quarters_of(w_value),
            quarters_of(w_out.T),
            jnp.broadcast_to(gains, (4, r, GAIN_COLS)),
        ],
        axis=2,
    )
    attn_w = lax.all_gather(spread(attn_pack, a, c), ("z", "y"), axis=0, tiled=True)
    mlp_pack = jnp.stack(
        [w.reshape(r, 4, 4, tile).transpose(1, 0, 2, 3) for w in (w_gate, w_up, w_down.T)], axis=3
    ).reshape(4, r, 3 * ff)
    mlp_w = lax.all_gather(spread(mlp_pack, a, c), ("z", "y"), axis=0, tiled=True)

    x_own = to_place(tokens)
    x_pieces = gather_rows(x_own)

    seg_pair = jnp.stack([segment_ids, lax.ppermute(segment_ids, "a", SWAP)])
    seg = jnp.concatenate([seg_pair, lax.ppermute(seg_pair, "c", SWAP)], axis=0)
    shift = jnp.stack([t, t ^ a, t, t ^ a])[:, None]
    seg = jnp.where(shift == 0, seg, jnp.roll(seg, own, axis=1))
    order = (jnp.arange(block, dtype=jnp.int32)[None, :] + shift * own) % block
    earlier = jnp.sum((seg[:, None, :] < seg[:, :, None]).astype(jnp.int32), axis=2)
    positions = (order - earlier).reshape(4 * block, 1)
    allowed = (seg[:, :, None] == seg[:, None, :]) & (order[:, None, :] <= order[:, :, None])
    mask = jnp.where(allowed, 0.0, MASKED).astype(F32).reshape(4 * block, block)
    lane = jnp.arange(2 * head)
    frequency = jnp.exp(
        -math.log(ROPE_BASE) * ((lane % (head // 2)).astype(F32) / (head // 2))
    )
    angles = positions.astype(F32) * frequency
    cosines = jnp.cos(angles)
    sines = jnp.where(lane % head < head // 2, -1.0, 1.0) * jnp.sin(angles)

    forward = attn_forward(x_pieces, attn_w, cosines, sines, mask, head)
    mine, other, normed, factor1, query, key, value, probs, mixed, gain_rows = forward
    gain_a, gain_m = gain_rows[0], gain_rows[1]
    resid = x_own.astype(F32) + scatter_rows(mine, other)

    factor2 = lax.rsqrt(jnp.mean(resid * resid, axis=-1, keepdims=True) + EPSILON)
    u2 = resid * factor2
    n_pieces = gather_rows((u2 * gain_m).astype(BF))
    c_own = to_place(cotangent)
    c_pieces = gather_rows(c_own)
    h_all, mine, other, n_all, c_all = mlp(n_pieces, c_pieces, mlp_w)
    d_n2 = scatter_rows(mine, other)
    mlp_grad, mine, other = mlp_grads(n_all, c_all, h_all, mlp_w)
    mlp_grad = lax.psum_scatter(mlp_grad, ("z", "y"), scatter_dimension=0, tiled=True)
    layer_output = from_place((resid + scatter_rows(mine, other)).astype(BF))

    mlp_gain_part = jnp.sum(d_n2 * u2, axis=0)
    d_resid = c_own.astype(F32) + norm_back(u2, factor2, gain_m, d_n2)
    d_pieces = gather_rows(d_resid.astype(BF))
    extra = jnp.pad(mlp_gain_part[None], ((1, 6), (0, 0)))
    saved = (factor1, normed, query, key, value, probs, mixed)
    mine, other, grad_q, grad_kv, grad_o = attn_backward(
        d_pieces, x_pieces, attn_w, cosines, sines, saved, extra, head
    )
    h = jnp.concatenate(
        [scatter_zy(grad_q, "z"), scatter_zy(grad_kv, "y"), scatter_zy(grad_o, "z")], axis=1
    )
    d_n1 = scatter_rows(mine, other)
    u1 = x_own.astype(F32) * factor1[:own, :1]
    input_grad = from_place(d_resid + norm_back(u1, factor1[:own, :1], gain_a, d_n1))

    g = unspread(mlp_grad, a, c).astype(F32).reshape(4, r, 4, 3, tile)
    gate_grad, up_grad, down_grad = (
        whole_columns(g[:, :, :, i].reshape(4, r, ff)) for i in range(3)
    )
    h = unspread(h, a, c).astype(F32)
    query_grad = whole_columns(h[:, :, :nq])
    key_grad = whole_columns(h[:, :, nq : nq + nk])
    value_grad = whole_columns(h[:, :, nq + nk : cut])
    out_grad = whole_columns(h[:, :, cut + GAIN_COLS :]).T
    gain_grads = jnp.sum(h[:, :, cut : cut + 2], axis=0).T
    gain_grads = gain_grads + lax.ppermute(gain_grads, "t", SWAP)
    return (
        layer_output, input_grad, gain_grads[0], query_grad, key_grad, value_grad, out_grad,
        gain_grads[1], gate_grad, up_grad, down_grad.T,
    )


def solution(mesh):
    fine = Mesh(mesh.devices.reshape(2, 4, 4, 2, 2), ("a", "z", "y", "c", "t"))
    dp = ("a", "z", "y", "c")
    rows = P(dp + ("t",), None)
    return jax.shard_map(
        local,
        mesh=fine,
        in_specs=(
            rows, P(dp), P(dp), P(dp, "t"), P(dp, "t"), P(dp, "t"), P("t", dp),
            P(dp), P(dp, "t"), P(dp, "t"), P("t", dp), rows,
        ),
        out_specs=(
            rows, rows, P(dp), P(dp, "t"), P(dp, "t"), P(dp, "t"), P("t", dp),
            P(dp), P(dp, "t"), P(dp, "t"), P("t", dp),
        ),
        check_vma=False,
    )
```

```python
import math

import jax
import jax.numpy as jnp
from jax import lax
from jax.experimental import pallas as pl
from jax.experimental.pallas import tpu as pltpu
from jax.sharding import Mesh
from jax.sharding import PartitionSpec as P

HEADS = 32
KV_HEADS = 8
GROUP = HEADS // KV_HEADS
EPSILON = 1e-05
ROPE_BASE = 500000.0
MASKED = -1e30
GAIN_COLS = 128
VMEM_LIMIT = 56 * 2**20
BF = jnp.bfloat16
F32 = jnp.float32


def cost(micros):
    return pl.CostEstimate(flops=micros * 10**9, bytes_accessed=2**20, transcendentals=0)


SWAP = [(0, 1), (1, 0)]


def mm(left, right):
    return jnp.dot(left, right, preferred_element_type=F32)


def mm_nt(left, right):
    return lax.dot_general(left, right, (((1,), (1,)), ((), ())), preferred_element_type=F32)


def mm_tn(left, right):
    return lax.dot_general(left, right, (((0,), (0,)), ((), ())), preferred_element_type=F32)


AT = (0, 2, 1, 3)


def from_chip(value, k):
    return lax.ppermute(value, ("a", "t"), [(AT[(i + k) % 4], AT[i]) for i in range(4)])


def to_chip(value, k):
    return lax.ppermute(value, ("a", "t"), [(AT[i], AT[(i + k) % 4]) for i in range(4)])


def after(value, *others):
    return lax.optimization_barrier((value, *others))[0]


def swap_core(value):
    return lax.ppermute(value, "c", SWAP)


def gather_rows(rows):
    mine = [rows, from_chip(rows, 2), from_chip(rows, 1), from_chip(rows, 3)]
    return mine + [swap_core(piece) for piece in mine]


def chip_parts(mine, got):
    rows = mine.shape[0] // 4
    parts = [
        mine[i * rows : (i + 1) * rows].astype(F32) + got[i * rows : (i + 1) * rows].astype(F32)
        for i in range(4)
    ]
    return [parts[0]] + [part.astype(BF) for part in parts[1:]]


def send_parts(parts):
    return [to_chip(part, k) for part, k in zip(parts[1:], (2, 1, 3))]


def total_of(parts, got):
    total = parts[0]
    for part in got:
        total = total + part.astype(F32)
    return total


def spread(quarters, a, c, wait=()):
    first = c == 0
    r = quarters[0].shape[0]
    keep = [jnp.where(first, quarters[2 * i], quarters[2 * i + 1]) for i in range(2)]
    give = [jnp.where(first, quarters[2 * i + 1], quarters[2 * i]) for i in range(2)]
    got = swap_core(jnp.concatenate(give, axis=0))
    both = [
        jnp.concatenate([jnp.where(first, k, g), jnp.where(first, g, k)], axis=0)
        for k, g in zip(keep, (got[:r], got[r:]))
    ]
    first_a = a == 0
    keep_a = jnp.where(first_a, both[0], both[1])
    give_a = jnp.where(first_a, both[1], both[0])
    got_a = lax.ppermute(after(give_a, *wait), "a", SWAP)
    rows = [jnp.where(first_a, keep_a, got_a), jnp.where(first_a, got_a, keep_a)]
    return jnp.concatenate(rows, axis=0), got_a


def unspread(rows, a, c, wait=()):
    half = rows.shape[0] // 2
    r = half // 2
    low, high = rows[:half], rows[half:]
    first_a, first = a == 0, c == 0
    keep_a = jnp.where(first_a, low, high)
    give_a = jnp.where(first_a, high, low)
    got_a = lax.ppermute(after(give_a, *wait), "a", SWAP)
    by_a = [jnp.where(first_a, keep_a, got_a), jnp.where(first_a, got_a, keep_a)]
    keep = [jnp.where(first, v[:r], v[r:]) for v in by_a]
    give = [jnp.where(first, v[r:], v[:r]) for v in by_a]
    got = swap_core(jnp.concatenate(give, axis=0))
    quarters = []
    for k, g in zip(keep, (got[:r], got[r:])):
        quarters += [jnp.where(first, k, g), jnp.where(first, g, k)]
    return quarters, got_a


def columns_of(quarters, start, width):
    return jnp.concatenate([q[:, start : start + width] for q in quarters], axis=1).astype(F32)


def sum_along(pieces, axis):
    total = pieces[0].astype(F32)
    for k in (2, 1, 3):
        got = lax.ppermute(pieces[k], axis, [(i, (i + k) % 4) for i in range(4)])
        total = total + got.astype(F32)
    return total.astype(BF)


def sum_zy(by_z, by_y, *others):
    z, y = lax.axis_index("z"), lax.axis_index("y")
    first = after((sum_along(by_z, "z"), sum_along(by_y, "y")), *others)
    both = []
    for part, axis, place in zip(first, ("y", "z"), (y, z)):
        rows = part.shape[0] // 4
        pieces = [
            lax.dynamic_slice_in_dim(part, (place + k) % 4 * rows, rows, axis=0) for k in range(4)
        ]
        both.append(sum_along(pieces, axis))
    return jnp.concatenate(both, axis=1)


def to_place(rows):
    n, d = rows.shape
    return rows.reshape(n, 2, 16, d // 32).transpose(0, 2, 1, 3).reshape(n, d)


def from_place(rows):
    n, d = rows.shape
    return rows.reshape(n, 16, 2, d // 32).transpose(0, 2, 1, 3).reshape(n, d)


def norm_back(rescaled, factor, gain, upstream):
    inner = upstream * gain
    return factor * (inner - rescaled * jnp.mean(inner * rescaled, axis=-1, keepdims=True))


def step_block(s):
    return (s + 2) % 4


def row_block(width):
    return lambda rows: pl.BlockSpec((rows, width), lambda s: (step_block(s), 0))


def fixed(shape):
    return pl.BlockSpec(shape, lambda *_: (0,) * len(shape))


def halves(rows, width):
    return [
        pl.BlockSpec((rows, width), lambda s: (jnp.maximum(s - 2, 0), 0)),
        pl.BlockSpec((rows, width), lambda s: (jnp.minimum(s, 1), 0)),
    ]


def load_block(s, pieces, scratch):
    part = pieces[0].shape[0]
    for b in range(4):

        @pl.when(step_block(s) == b)
        def _():
            scratch[:part] = pieces[2 * b][...]
            scratch[part:] = pieces[2 * b + 1][...]


def store_half(s, mine_ref, other_ref, value):
    @pl.when(s < 2)
    def _():
        other_ref[...] = value

    @pl.when(s >= 2)
    def _():
        mine_ref[...] = value


def pick_rows(columns):
    one = (
        lax.broadcasted_iota(jnp.int32, (8, columns.shape[1]), 0)
        == lax.broadcasted_iota(jnp.int32, (8, columns.shape[1]), 1)
    ).astype(BF)
    return mm_nt(one, columns)


def turn(values, cosines, sines, head):
    width = values.shape[1]
    lane = lax.broadcasted_iota(jnp.int32, values.shape, 1)
    low = lane % head < head // 2
    partner = jnp.where(
        low, pltpu.roll(values, width - head // 2, 1), pltpu.roll(values, head // 2, 1)
    )
    return values * cosines + partner * sines


def double(values, times):
    return jnp.concatenate([values] * times, axis=1)


def by_head(values, head):
    lane = lax.broadcasted_iota(jnp.int32, values.shape, 1) // head
    zero = jnp.zeros_like(values)
    return jnp.concatenate([jnp.where(lane == h, values, zero) for h in range(GROUP)], axis=0)


def take_heads(values, rows, head):
    lane = lax.broadcasted_iota(jnp.int32, (rows, values.shape[1]), 1) // head
    out = values[:rows]
    for h in range(1, GROUP):
        out = jnp.where(lane == h, values[h * rows : (h + 1) * rows], out)
    return out


def fold_heads(values, head):
    pair = values[:, : 2 * head] + values[:, 2 * head :]
    return pair + pltpu.roll(pair, head, 1)


def attn_forward_kernel(head, *refs):
    pieces = refs[:8]
    (w_ref, cos_ref, sin_ref, mask_ref,
     mine_ref, other_ref, normed_ref, factor_ref, q_ref, k_ref, v_ref, probs_ref, mixed_ref,
     gains_ref, x_ref, gain_scr) = refs[8:]
    s = pl.program_id(0)
    nq, cut = GROUP * head, (GROUP + 2) * head
    rows = x_ref.shape[0]

    @pl.when(s == 0)
    def _():
        gain_scr[...] = pick_rows(w_ref[:, cut + nq :])
        gains_ref[...] = gain_scr[...]

    load_block(s, pieces, x_ref)
    x = x_ref[...].astype(F32)
    factor = lax.rsqrt(jnp.mean(x * x, axis=-1, keepdims=True) + EPSILON)
    factor_ref[...] = jnp.broadcast_to(factor, factor_ref.shape)
    normed = (x * factor * gain_scr[0:1, :]).astype(BF)
    normed_ref[...] = normed
    qkv = mm(normed, w_ref[:, :cut])
    cosines, sines = cos_ref[...], sin_ref[...]
    query = turn(qkv[:, :nq], double(cosines, 2), double(sines, 2), head).astype(BF)
    kv = qkv[:, nq:]
    turned = turn(kv, cosines, sines, head)
    low = lax.broadcasted_iota(jnp.int32, kv.shape, 1) < head
    key = double(jnp.where(low, turned, pltpu.roll(turned, head, 1)), 2).astype(BF)
    value = double(jnp.where(low, pltpu.roll(kv, head, 1), kv), 2).astype(BF)
    q_ref[...] = query
    k_ref[...] = key
    v_ref[...] = value
    scores = mm_nt(by_head(query, head), key) * (1.0 / math.sqrt(head))
    allowed = mask_ref[...] == 0
    scores = jnp.where(jnp.concatenate([allowed] * GROUP, axis=0), scores, MASKED)
    weights = jnp.exp(scores - jnp.max(scores, axis=-1, keepdims=True))
    probs = weights / jnp.sum(weights, axis=-1, keepdims=True)
    probs_ref[...] = probs
    mixed = take_heads(mm(probs.astype(BF), value), rows, head).astype(BF)
    mixed_ref[...] = mixed
    store_half(s, mine_ref, other_ref, mm_nt(mixed, w_ref[:, cut : cut + nq]).astype(BF))


def attn_forward(pieces, w, cosines, sines, mask, head):
    part, d = pieces[0].shape
    rows = 2 * part
    nq = GROUP * head
    spec = lambda width: row_block(width)(rows)
    return pl.pallas_call(
        lambda *refs: attn_forward_kernel(head, *refs),
        grid=(4,),
        in_specs=[fixed(p.shape) for p in pieces]
        + [fixed(w.shape), spec(2 * head), spec(2 * head), spec(rows)],
        out_specs=halves(rows, d)
        + [spec(d), spec(128), spec(nq), spec(nq), spec(nq)]
        + [pl.BlockSpec((GROUP * rows, rows), lambda s: (step_block(s), 0)), spec(nq), fixed((8, d))],
        out_shape=[jax.ShapeDtypeStruct((2 * rows, d), BF)] * 2
        + [jax.ShapeDtypeStruct((4 * rows, d), BF), jax.ShapeDtypeStruct((4 * rows, 128), F32)]
        + [jax.ShapeDtypeStruct((4 * rows, nq), BF)] * 3
        + [
            jax.ShapeDtypeStruct((4 * GROUP * rows, rows), F32),
            jax.ShapeDtypeStruct((4 * rows, nq), BF),
            jax.ShapeDtypeStruct((8, d), F32),
        ],
        scratch_shapes=[pltpu.VMEM((rows, d), BF), pltpu.VMEM((8, d), F32)],
        compiler_params=pltpu.CompilerParams(vmem_limit_bytes=VMEM_LIMIT),
        cost_estimate=cost(30),
    )(*pieces, w, cosines, sines, mask)


def attn_backward_kernel(head, *refs):
    d_pieces, x_pieces = refs[:8], refs[8:16]
    (w_ref, cos_ref, sin_ref, factor_ref, normed_ref, q_ref, k_ref, v_ref, probs_ref, mixed_ref,
     extra_ref, place_ref, mine_ref, other_ref) = refs[16:30]
    ga_refs, gb_refs = refs[30:34], refs[34:38]
    db_ref, x_ref, acc_a, acc_o, gain_acc = refs[38:]
    s = pl.program_id(0)
    nq, cut = GROUP * head, (GROUP + 2) * head
    rows = x_ref.shape[0]
    scale = 1.0 / math.sqrt(head)

    @pl.when(s == 0)
    def _():
        acc_a[...] = jnp.zeros_like(acc_a)
        acc_o[...] = jnp.zeros_like(acc_o)
        gain_acc[...] = jnp.zeros_like(gain_acc)

    load_block(s, d_pieces, db_ref)
    load_block(s, x_pieces, x_ref)
    d_branch = db_ref[...]
    acc_o[:, :nq] += mm_tn(d_branch, mixed_ref[...])
    d_mixed = by_head(mm(d_branch, w_ref[:, cut : cut + nq]).astype(BF), head)
    d_probs = mm_nt(d_mixed, v_ref[...])
    probs = probs_ref[...]
    d_value = fold_heads(mm_tn(probs.astype(BF), d_mixed), head)
    d_scores = probs * (d_probs - jnp.sum(d_probs * probs, axis=-1, keepdims=True))
    d_scores = d_scores.astype(BF)
    d_query = take_heads(mm(d_scores, k_ref[...]), rows, head) * scale
    d_key = fold_heads(mm_tn(d_scores, by_head(q_ref[...], head)), head) * scale
    cosines, sines = cos_ref[...], -sin_ref[...]
    d_query = turn(d_query, double(cosines, 2), double(sines, 2), head).astype(BF)
    d_key = turn(d_key, cosines, sines, head)
    low = lax.broadcasted_iota(jnp.int32, d_key.shape, 1) < head
    d_kv = jnp.where(low, d_key, d_value).astype(BF)
    d_qkv = jnp.concatenate([d_query, d_kv], axis=1)
    acc_a[...] += mm_tn(normed_ref[...], d_qkv)
    d_normed = mm_nt(d_qkv, w_ref[:, :cut])
    store_half(s, mine_ref, other_ref, d_normed.astype(BF))
    u1 = x_ref[...].astype(F32) * factor_ref[:, :1]
    gain_acc[0:1, :] += jnp.sum(d_normed * u1, axis=0, keepdims=True)

    @pl.when(s == 3)
    def _():
        gains = gain_acc[...] + extra_ref[...]
        one = (
            lax.broadcasted_iota(jnp.int32, (8, GAIN_COLS), 0)
            == lax.broadcasted_iota(jnp.int32, (8, GAIN_COLS), 1)
        ).astype(BF)
        acc_o[:, nq:] = mm_tn(gains.astype(BF), one)
        part = ga_refs[0].shape[0]
        small = part // 4
        for k in range(4):
            z = lax.rem(place_ref[0] + k, 4)
            y = lax.rem(place_ref[1] + k, 4)
            ga_refs[k][...] = acc_a[pl.ds(pl.multiple_of(z * part, part), part)].astype(BF)
            for i in range(4):
                at = pl.ds(pl.multiple_of(i * part + y * small, small), small)
                gb_refs[k][i * small : (i + 1) * small] = acc_o[at].astype(BF)


def attn_backward(d_pieces, x_pieces, w, cosines, sines, saved, extra, place, head):
    factor, normed, query, key, value, probs, mixed = saved
    part, d = d_pieces[0].shape
    rows = 2 * part
    nq, cut = GROUP * head, (GROUP + 2) * head
    spec = lambda width: row_block(width)(rows)
    grads = [(d // 4, cut)] * 4 + [(d // 4, nq + GAIN_COLS)] * 4
    return pl.pallas_call(
        lambda *refs: attn_backward_kernel(head, *refs),
        grid=(4,),
        in_specs=[fixed(p.shape) for p in (*d_pieces, *x_pieces)]
        + [fixed(w.shape), spec(2 * head), spec(2 * head), spec(128), spec(d)]
        + [spec(nq), spec(nq), spec(nq)]
        + [pl.BlockSpec((GROUP * rows, rows), lambda s: (step_block(s), 0)), spec(nq)]
        + [fixed((8, d)), pl.BlockSpec(memory_space=pltpu.SMEM)],
        out_specs=halves(rows, d) + [fixed(shape) for shape in grads],
        out_shape=[jax.ShapeDtypeStruct((2 * rows, d), BF)] * 2
        + [jax.ShapeDtypeStruct(shape, BF) for shape in grads],
        scratch_shapes=[
            pltpu.VMEM((rows, d), BF),
            pltpu.VMEM((rows, d), BF),
            pltpu.VMEM((d, cut), F32),
            pltpu.VMEM((d, nq + GAIN_COLS), F32),
            pltpu.VMEM((8, d), F32),
        ],
        compiler_params=pltpu.CompilerParams(vmem_limit_bytes=VMEM_LIMIT),
        cost_estimate=cost(10),
    )(*d_pieces, *x_pieces, w, cosines, sines, factor, normed, query, key, value, probs, mixed,
      extra, place)


def mlp_kernel(*refs):
    n_pieces, c_pieces = refs[:8], refs[8:16]
    (wg_ref, wu_ref, wd_ref, dg_ref, du_ref, hid_ref, mine_ref, other_ref,
     n_scr, c_scr, w_scr, d_scr) = refs[16:]
    j = pl.program_id(0)
    part = n_pieces[0].shape[0]
    tile = wg_ref.shape[1]
    ff = 4 * tile

    @pl.when(j == 0)
    def _():
        for i in range(8):
            n_scr[i * part : (i + 1) * part] = n_pieces[i][...]
            c_scr[i * part : (i + 1) * part] = c_pieces[i][...]

    for step in range(4):

        @pl.when(j == step)
        def _():
            w_scr[:, step * tile : (step + 1) * tile] = wg_ref[...]
            w_scr[:, ff + step * tile : ff + (step + 1) * tile] = wu_ref[...]
            gate = mm(n_scr[...], wg_ref[...])
            up = mm(n_scr[...], wu_ref[...])
            d_hidden = mm(c_scr[...], wd_ref[...])
            sig = jax.nn.sigmoid(gate)
            silu = gate * sig
            hid_ref[...] = (silu * up).astype(BF)
            d_gate = (d_hidden * up * sig * (1.0 + gate * (1.0 - sig))).astype(BF)
            d_up = (d_hidden * silu).astype(BF)
            dg_ref[...] = d_gate
            du_ref[...] = d_up
            d_scr[:, step * tile : (step + 1) * tile] = d_gate
            d_scr[:, ff + step * tile : ff + (step + 1) * tile] = d_up

    @pl.when(j >= 4)
    def _():
        wide = mine_ref.shape[1]
        rows = pl.ds(pl.multiple_of((j - 4) * wide, wide), wide)
        d_n2 = mm_nt(d_scr[...], w_scr[rows, :]).astype(BF)
        mine_ref[...] = d_n2[: 4 * part]
        other_ref[...] = d_n2[4 * part :]


def mlp(n_pieces, c_pieces, w):
    part, d = n_pieces[0].shape
    rows, ff = 8 * part, w.shape[1] // 3
    tile, wide = ff // 4, d // 4
    at = lambda k: pl.BlockSpec((d, tile), lambda j: (0, 4 * k + jnp.minimum(j, 3)))
    return pl.pallas_call(
        mlp_kernel,
        grid=(8,),
        in_specs=[fixed((part, d))] * 16 + [at(0), at(1), at(2)],
        out_specs=[pl.BlockSpec((rows, tile), lambda j: (0, jnp.minimum(j, 3)))] * 3
        + [pl.BlockSpec((rows // 2, wide), lambda j: (0, jnp.maximum(j - 4, 0)))] * 2,
        out_shape=[jax.ShapeDtypeStruct((rows, ff), BF)] * 3
        + [jax.ShapeDtypeStruct((rows // 2, d), BF)] * 2,
        scratch_shapes=[
            pltpu.VMEM((rows, d), BF),
            pltpu.VMEM((rows, d), BF),
            pltpu.VMEM((d, 2 * ff), BF),
            pltpu.VMEM((rows, 2 * ff), BF),
        ],
        compiler_params=pltpu.CompilerParams(vmem_limit_bytes=VMEM_LIMIT),
        cost_estimate=cost(40),
    )(*n_pieces, *c_pieces, w, w, w)


def mlp_grads_kernel(sides, *refs):
    pieces, rights = refs[:8], refs[8 : 8 + sides]
    g_ref, all_ref, turned_ref = refs[-3:]
    part = pieces[0].shape[0]
    j = pl.program_id(0)

    @pl.when(j == 0)
    def _():
        for i in range(8):
            all_ref[i * part : (i + 1) * part] = pieces[i][...]
        turned_ref[...] = all_ref[...].T

    for k in range(sides):

        @pl.when((j >= 4 * k) & (j < 4 * k + 4))
        def _():
            g_ref[...] = mm(turned_ref[...], rights[k][...]).astype(BF)


def mlp_grads(pieces, rights, into=None):
    part, d = pieces[0].shape
    rows, ff = rights[0].shape
    tile = ff // 4
    sides = len(rights)
    start = 0 if into is None else 12 - 4 * sides
    at = lambda k: pl.BlockSpec((rows, tile), lambda j: (0, jnp.clip(j - 4 * k, 0, 3)))
    extra = [] if into is None else [into]
    return pl.pallas_call(
        lambda *refs: mlp_grads_kernel(sides, *refs),
        grid=(4 * sides,),
        in_specs=[fixed((part, d))] * 8
        + [at(k) for k in range(sides)]
        + [pl.BlockSpec(memory_space=pl.ANY)] * len(extra),
        out_specs=pl.BlockSpec((d, tile), lambda j: (0, start + j)),
        out_shape=jax.ShapeDtypeStruct((d, 3 * ff), BF),
        input_output_aliases={8 + sides: 0} if extra else {},
        scratch_shapes=[pltpu.VMEM((rows, d), BF), pltpu.VMEM((d, rows), BF)],
        compiler_params=pltpu.CompilerParams(vmem_limit_bytes=VMEM_LIMIT),
        cost_estimate=cost(20 * sides),
    )(*pieces, *rights, *extra)


def mlp_out_kernel(x_ref, w_ref, mine_ref, other_ref):
    half = x_ref.shape[0] // 2
    out = mm_nt(x_ref[...], w_ref[...]).astype(BF)
    mine_ref[...] = out[:half]
    other_ref[...] = out[half:]


def mlp_out(hid, w):
    rows, ff = hid.shape
    d = w.shape[0]
    wide = d // 4
    return pl.pallas_call(
        mlp_out_kernel,
        grid=(4,),
        in_specs=[fixed((rows, ff)), pl.BlockSpec((wide, ff), lambda j: (j, 2))],
        out_specs=[pl.BlockSpec((rows // 2, wide), lambda j: (0, j))] * 2,
        out_shape=[jax.ShapeDtypeStruct((rows // 2, d), BF)] * 2,
        compiler_params=pltpu.CompilerParams(vmem_limit_bytes=VMEM_LIMIT),
        cost_estimate=cost(5),
    )(hid, w)


def token_tables(seg, shift, own, head):
    count, block = seg.shape
    seg = jnp.where(shift == 0, seg, jnp.roll(seg, own, axis=1))
    order = (jnp.arange(block, dtype=jnp.int32)[None, :] + shift * own) % block
    earlier = jnp.sum((seg[:, None, :] < seg[:, :, None]).astype(jnp.int32), axis=2)
    positions = (order - earlier).reshape(count * block, 1)
    allowed = (seg[:, :, None] == seg[:, None, :]) & (order[:, None, :] <= order[:, :, None])
    mask = jnp.where(allowed, 0.0, MASKED).astype(F32).reshape(count * block, block)
    lane = jnp.arange(2 * head)
    frequency = jnp.exp(-math.log(ROPE_BASE) * ((lane % (head // 2)).astype(F32) / (head // 2)))
    angles = positions.astype(F32) * frequency
    sines = jnp.where(lane % head < head // 2, -1.0, 1.0) * jnp.sin(angles)
    return jnp.cos(angles), sines, mask


def local(
    tokens, segment_ids, attn_gain, w_query, w_key, w_value, w_out,
    mlp_gain, w_gate, w_up, w_down, cotangent,
):
    a, c, t = lax.axis_index("a"), lax.axis_index("c"), lax.axis_index("t")
    own = tokens.shape[0]
    nq = w_query.shape[1] // 4
    nk = w_key.shape[1] // 4
    ff = w_gate.shape[1] // 4
    head = nk
    cut = nq + 2 * nk

    gains = jnp.stack([attn_gain, mlp_gain], axis=1)
    gains = jnp.pad(gains, ((0, 0), (0, GAIN_COLS - 2)))
    quarter = lambda w, i: w[:, i * w.shape[1] // 4 : (i + 1) * w.shape[1] // 4]
    attn_pack = [
        jnp.concatenate(
            [quarter(w, i) for w in (w_query, w_key, w_value, w_out.T)] + [gains], axis=1
        )
        for i in range(4)
    ]
    attn_rows, attn_got = spread(attn_pack, a, c)
    attn_w = lax.all_gather(attn_rows, ("z", "y"), axis=0, tiled=True)
    x_own, c_own = to_place(tokens), to_place(cotangent)
    x_pieces = gather_rows(after(x_own, attn_got))
    mlp_pack = [
        jnp.concatenate([quarter(w, i) for w in (w_gate, w_up, w_down.T)], axis=1) for i in range(4)
    ]
    mlp_rows, mlp_got = spread(mlp_pack, a, c, x_pieces[1:4])
    mlp_w = lax.all_gather(mlp_rows, ("z", "y"), axis=0, tiled=True)
    c_pieces = gather_rows(after(c_own, *x_pieces[1:4]))

    seg = jnp.stack([segment_ids, lax.ppermute(segment_ids, "a", SWAP)])
    seg = jnp.concatenate([seg, swap_core(seg)], axis=0)
    shift = jnp.stack([t, t ^ a, t, t ^ a])[:, None]
    cosines, sines, mask = token_tables(seg, shift, own, head)

    forward = attn_forward(
        after(x_pieces, *c_pieces[1:4]), attn_w, cosines, sines, mask, head
    )
    mine, other, normed, factor1, query, key, value, probs, mixed, gain_rows = forward
    gain_a, gain_m = gain_rows[0], gain_rows[1]
    parts = chip_parts(mine, swap_core(other))
    resid = x_own.astype(F32) + total_of(parts, send_parts(parts))

    factor2 = lax.rsqrt(jnp.mean(resid * resid, axis=-1, keepdims=True) + EPSILON)
    u2 = resid * factor2
    n_pieces = gather_rows((u2 * gain_m).astype(BF))
    d_gate, d_up, hidden, mine, other = mlp(n_pieces, c_pieces, mlp_w)
    parts = chip_parts(mine, swap_core(other))
    got = send_parts(parts)
    grads = mlp_grads(after(n_pieces, parts[1]), (d_gate, d_up))
    grads = mlp_grads(c_pieces, (hidden,), grads)
    *got, grads = after((*got, grads))
    d_n2 = total_of(parts, got)
    mlp_grad = lax.psum_scatter(grads, ("z", "y"), scatter_dimension=0, tiled=True)

    d_resid = c_own.astype(F32) + norm_back(u2, factor2, gain_m, d_n2)
    d_branch = d_resid.astype(BF)
    mlp_gain_part = jnp.sum(d_n2 * u2, axis=0)
    d_pieces = gather_rows(d_branch)
    out_mine, out_other = mlp_out(after(hidden, d_branch), mlp_w)
    out_parts = chip_parts(out_mine, swap_core(after(out_other, *d_pieces[1:4])))
    out_got = send_parts(out_parts)
    extra = jnp.pad(mlp_gain_part[None], ((1, 6), (0, 0)))
    place = jnp.stack([lax.axis_index("z"), lax.axis_index("y")]).astype(jnp.int32)
    saved = (factor1, normed, query, key, value, probs, mixed)
    mine, other, *sums = attn_backward(
        after(d_pieces, out_parts[1]), x_pieces, attn_w, cosines, sines, saved, extra, place, head
    )
    sums, other = after((sums, other), *out_got)
    parts = chip_parts(mine, swap_core(other))
    got = send_parts(parts)
    d_n1 = total_of(parts, got)
    layer_output = from_place((resid + total_of(out_parts, out_got)).astype(BF))
    h = sum_zy(sums[:4], sums[4:], layer_output, *got)

    factor1 = factor1[:own, :1]
    u1 = x_own.astype(F32) * factor1
    input_grad = from_place(d_resid + norm_back(u1, factor1, gain_a, d_n1))

    g, g_got = unspread(mlp_grad, a, c)
    gate_grad, up_grad, down_grad = (columns_of(g, i * ff, ff) for i in range(3))
    h, _ = unspread(h, a, c, (g_got,))
    query_grad = columns_of(h, 0, nq)
    key_grad = columns_of(h, nq, nk)
    value_grad = columns_of(h, nq + nk, nk)
    out_grad = columns_of(h, cut, nq).T
    gain_grads = sum(q[:, cut + nq : cut + nq + 2].astype(F32) for q in h).T
    gain_grads = gain_grads + lax.ppermute(gain_grads, "t", SWAP)
    return (
        layer_output, input_grad, gain_grads[0], query_grad, key_grad, value_grad, out_grad,
        gain_grads[1], gate_grad, up_grad, down_grad.T,
    )


def solution(mesh):
    fine = Mesh(mesh.devices.reshape(2, 4, 4, 2, 2), ("a", "z", "y", "c", "t"))
    dp = ("a", "z", "y", "c")
    rows = P(dp + ("t",), None)
    return jax.shard_map(
        local,
        mesh=fine,
        in_specs=(
            rows, P(dp), P(dp), P(dp, "t"), P(dp, "t"), P(dp, "t"), P("t", dp),
            P(dp), P(dp, "t"), P(dp, "t"), P("t", dp), rows,
        ),
        out_specs=(
            rows, rows, P(dp), P(dp, "t"), P(dp, "t"), P(dp, "t"), P("t", dp),
            P(dp), P(dp, "t"), P(dp, "t"), P("t", dp),
        ),
        check_vma=False,
    )
```

```python
import math

import jax
import jax.numpy as jnp
from jax import lax
from jax.experimental import pallas as pl
from jax.experimental.pallas import tpu as pltpu
from jax.sharding import Mesh
from jax.sharding import PartitionSpec as P

HEADS = 32
KV_HEADS = 8
GROUP = HEADS // KV_HEADS
EPSILON = 1e-05
ROPE_BASE = 500000.0
MASKED = -1e30
GAIN_COLS = 128
VMEM_LIMIT = 56 * 2**20
BF = jnp.bfloat16
F32 = jnp.float32


def cost(micros):
    return pl.CostEstimate(flops=micros * 10**9, bytes_accessed=2**20, transcendentals=0)


SWAP = [(0, 1), (1, 0)]


def mm(left, right):
    return jnp.dot(left, right, preferred_element_type=F32)


def mm_nt(left, right):
    return lax.dot_general(left, right, (((1,), (1,)), ((), ())), preferred_element_type=F32)


def mm_tn(left, right):
    return lax.dot_general(left, right, (((0,), (0,)), ((), ())), preferred_element_type=F32)


AT = (0, 2, 1, 3)


def from_chip(value, k):
    return lax.ppermute(value, ("a", "t"), [(AT[(i + k) % 4], AT[i]) for i in range(4)])


def to_chip(value, k):
    return lax.ppermute(value, ("a", "t"), [(AT[i], AT[(i + k) % 4]) for i in range(4)])


def after(value, *others):
    return lax.optimization_barrier((value, *others))[0]


def swap_core(value):
    return lax.ppermute(value, "c", SWAP)


def gather_rows(rows):
    mine = [rows, from_chip(rows, 2), from_chip(rows, 1), from_chip(rows, 3)]
    return mine + [swap_core(piece) for piece in mine]


def chip_parts(mine, got):
    rows = mine.shape[0] // 4
    parts = [
        mine[i * rows : (i + 1) * rows].astype(F32) + got[i * rows : (i + 1) * rows].astype(F32)
        for i in range(4)
    ]
    return [parts[0]] + [part.astype(BF) for part in parts[1:]]


def send_parts(parts):
    return [to_chip(part, k) for part, k in zip(parts[1:], (2, 1, 3))]


def total_of(parts, got):
    total = parts[0]
    for part in got:
        total = total + part.astype(F32)
    return total


def spread(quarters, a, c, wait=()):
    first = c == 0
    r = quarters[0].shape[0]
    keep = [jnp.where(first, quarters[2 * i], quarters[2 * i + 1]) for i in range(2)]
    give = [jnp.where(first, quarters[2 * i + 1], quarters[2 * i]) for i in range(2)]
    got = swap_core(jnp.concatenate(give, axis=0))
    both = [
        jnp.concatenate([jnp.where(first, k, g), jnp.where(first, g, k)], axis=0)
        for k, g in zip(keep, (got[:r], got[r:]))
    ]
    first_a = a == 0
    keep_a = jnp.where(first_a, both[0], both[1])
    give_a = jnp.where(first_a, both[1], both[0])
    got_a = lax.ppermute(after(give_a, *wait), "a", SWAP)
    rows = [jnp.where(first_a, keep_a, got_a), jnp.where(first_a, got_a, keep_a)]
    return jnp.concatenate(rows, axis=0), got_a


def unspread_x(rows, a):
    half = rows.shape[0] // 2
    first = a == 0
    give = jnp.where(first, rows[half:], rows[:half])
    return jnp.where(first, rows[:half], rows[half:]), lax.ppermute(give, "a", SWAP)


def unspread_core(mine, came, a, c):
    r = mine.shape[0] // 2
    first_a, first = a == 0, c == 0
    by_a = [jnp.where(first_a, mine, came), jnp.where(first_a, came, mine)]
    keep = [jnp.where(first, v[:r], v[r:]) for v in by_a]
    give = [jnp.where(first, v[r:], v[:r]) for v in by_a]
    got = swap_core(jnp.concatenate(give, axis=0))
    quarters = []
    for k, g in zip(keep, (got[:r], got[r:])):
        quarters += [jnp.where(first, k, g), jnp.where(first, g, k)]
    return quarters, got


def columns_of(quarters, start, width):
    return jnp.concatenate([q[:, start : start + width] for q in quarters], axis=1).astype(F32)


def to_place(rows):
    n, d = rows.shape
    return rows.reshape(n, 2, 16, d // 32).transpose(0, 2, 1, 3).reshape(n, d)


def norm_back(rescaled, factor, gain, upstream):
    inner = upstream * gain
    return factor * (inner - rescaled * jnp.mean(inner * rescaled, axis=-1, keepdims=True))


def step_block(s):
    return (s + 2) % 4


def row_block(width):
    return lambda rows: pl.BlockSpec((rows, width), lambda s: (step_block(s), 0))


def fixed(shape):
    return pl.BlockSpec(shape, lambda *_: (0,) * len(shape))


def halves(rows, width):
    return [
        pl.BlockSpec((rows, width), lambda s: (jnp.maximum(s - 2, 0), 0)),
        pl.BlockSpec((rows, width), lambda s: (jnp.minimum(s, 1), 0)),
    ]


def load_block(s, pieces, scratch):
    part = pieces[0].shape[0]
    for b in range(4):

        @pl.when(step_block(s) == b)
        def _():
            scratch[:part] = pieces[2 * b][...]
            scratch[part:] = pieces[2 * b + 1][...]


def store_half(s, mine_ref, other_ref, value):
    @pl.when(s < 2)
    def _():
        other_ref[...] = value

    @pl.when(s >= 2)
    def _():
        mine_ref[...] = value


def pick_rows(columns):
    one = (
        lax.broadcasted_iota(jnp.int32, (8, columns.shape[1]), 0)
        == lax.broadcasted_iota(jnp.int32, (8, columns.shape[1]), 1)
    ).astype(BF)
    return mm_nt(one, columns)


def turn(values, cosines, sines, head):
    width = values.shape[1]
    lane = lax.broadcasted_iota(jnp.int32, values.shape, 1)
    low = lane % head < head // 2
    partner = jnp.where(
        low, pltpu.roll(values, width - head // 2, 1), pltpu.roll(values, head // 2, 1)
    )
    return values * cosines + partner * sines


def double(values, times):
    return jnp.concatenate([values] * times, axis=1)


def by_head(values, head):
    lane = lax.broadcasted_iota(jnp.int32, values.shape, 1) // head
    zero = jnp.zeros_like(values)
    return jnp.concatenate([jnp.where(lane == h, values, zero) for h in range(GROUP)], axis=0)


def take_heads(values, rows, head):
    lane = lax.broadcasted_iota(jnp.int32, (rows, values.shape[1]), 1) // head
    out = values[:rows]
    for h in range(1, GROUP):
        out = jnp.where(lane == h, values[h * rows : (h + 1) * rows], out)
    return out


def fold_heads(values, head):
    pair = values[:, : 2 * head] + values[:, 2 * head :]
    return pair + pltpu.roll(pair, head, 1)


def attn_forward_kernel(head, *refs):
    pieces = refs[:8]
    (w_ref, cos_ref, sin_ref, mask_ref,
     mine_ref, other_ref, normed_ref, factor_ref, q_ref, k_ref, v_ref, probs_ref, mixed_ref,
     gains_ref, x_ref, gain_scr) = refs[8:]
    s = pl.program_id(0)
    nq, cut = GROUP * head, (GROUP + 2) * head
    rows = x_ref.shape[0]

    @pl.when(s == 0)
    def _():
        gain_scr[...] = pick_rows(w_ref[:, cut + nq :])
        gains_ref[...] = gain_scr[...]

    load_block(s, pieces, x_ref)
    x = x_ref[...].astype(F32)
    factor = lax.rsqrt(jnp.mean(x * x, axis=-1, keepdims=True) + EPSILON)
    factor_ref[...] = jnp.broadcast_to(factor, factor_ref.shape)
    normed = (x * factor * gain_scr[0:1, :]).astype(BF)
    normed_ref[...] = normed
    qkv = mm(normed, w_ref[:, :cut])
    cosines, sines = cos_ref[...], sin_ref[...]
    query = turn(qkv[:, :nq], double(cosines, 2), double(sines, 2), head).astype(BF)
    kv = qkv[:, nq:]
    turned = turn(kv, cosines, sines, head)
    low = lax.broadcasted_iota(jnp.int32, kv.shape, 1) < head
    key = double(jnp.where(low, turned, pltpu.roll(turned, head, 1)), 2).astype(BF)
    value = double(jnp.where(low, pltpu.roll(kv, head, 1), kv), 2).astype(BF)
    q_ref[...] = query
    k_ref[...] = key
    v_ref[...] = value
    scores = mm_nt(by_head(query, head), key) * (1.0 / math.sqrt(head))
    allowed = mask_ref[...] == 0
    scores = jnp.where(jnp.concatenate([allowed] * GROUP, axis=0), scores, MASKED)
    weights = jnp.exp(scores - jnp.max(scores, axis=-1, keepdims=True))
    probs = weights / jnp.sum(weights, axis=-1, keepdims=True)
    probs_ref[...] = probs
    mixed = take_heads(mm(probs.astype(BF), value), rows, head).astype(BF)
    mixed_ref[...] = mixed
    store_half(s, mine_ref, other_ref, mm_nt(mixed, w_ref[:, cut : cut + nq]).astype(BF))


def attn_forward(pieces, w, cosines, sines, mask, head):
    part, d = pieces[0].shape
    rows = 2 * part
    nq = GROUP * head
    spec = lambda width: row_block(width)(rows)
    return pl.pallas_call(
        lambda *refs: attn_forward_kernel(head, *refs),
        grid=(4,),
        in_specs=[fixed(p.shape) for p in pieces]
        + [fixed(w.shape), spec(2 * head), spec(2 * head), spec(rows)],
        out_specs=halves(rows, d)
        + [spec(d), spec(128), spec(nq), spec(nq), spec(nq)]
        + [pl.BlockSpec((GROUP * rows, rows), lambda s: (step_block(s), 0)), spec(nq), fixed((8, d))],
        out_shape=[jax.ShapeDtypeStruct((2 * rows, d), BF)] * 2
        + [jax.ShapeDtypeStruct((4 * rows, d), BF), jax.ShapeDtypeStruct((4 * rows, 128), F32)]
        + [jax.ShapeDtypeStruct((4 * rows, nq), BF)] * 3
        + [
            jax.ShapeDtypeStruct((4 * GROUP * rows, rows), F32),
            jax.ShapeDtypeStruct((4 * rows, nq), BF),
            jax.ShapeDtypeStruct((8, d), F32),
        ],
        scratch_shapes=[pltpu.VMEM((rows, d), BF), pltpu.VMEM((8, d), F32)],
        compiler_params=pltpu.CompilerParams(vmem_limit_bytes=VMEM_LIMIT),
        cost_estimate=cost(30),
    )(*pieces, w, cosines, sines, mask)


def attn_backward_kernel(head, *refs):
    d_pieces = refs[:8]
    (w_ref, cos_ref, sin_ref, normed_ref, q_ref, k_ref, v_ref, probs_ref, mixed_ref,
     mine_ref, other_ref, grad_ref, d_scr, qkv_scr) = refs[8:]
    s = pl.program_id(0)
    nq, cut = GROUP * head, (GROUP + 2) * head
    part = d_pieces[0].shape[0]
    rows = 2 * part
    scale = 1.0 / math.sqrt(head)

    @pl.when(s == 0)
    def _():
        for i in range(8):
            d_scr[i * part : (i + 1) * part] = d_pieces[i][...]

    here = pl.ds(pl.multiple_of(step_block(s) * rows, rows), rows)
    d_branch = d_scr[here]
    d_mixed = by_head(mm(d_branch, w_ref[:, cut : cut + nq]).astype(BF), head)
    d_probs = mm_nt(d_mixed, v_ref[...])
    probs = probs_ref[...]
    d_value = fold_heads(mm_tn(probs.astype(BF), d_mixed), head)
    d_scores = probs * (d_probs - jnp.sum(d_probs * probs, axis=-1, keepdims=True))
    d_scores = d_scores.astype(BF)
    d_query = take_heads(mm(d_scores, k_ref[...]), rows, head) * scale
    d_key = fold_heads(mm_tn(d_scores, by_head(q_ref[...], head)), head) * scale
    cosines, sines = cos_ref[...], -sin_ref[...]
    d_query = turn(d_query, double(cosines, 2), double(sines, 2), head).astype(BF)
    d_key = turn(d_key, cosines, sines, head)
    low = lax.broadcasted_iota(jnp.int32, d_key.shape, 1) < head
    d_kv = jnp.where(low, d_key, d_value).astype(BF)
    d_qkv = jnp.concatenate([d_query, d_kv], axis=1)
    qkv_scr[here] = d_qkv
    d_normed = mm_nt(d_qkv, w_ref[:, :cut])
    store_half(s, mine_ref, other_ref, d_normed.astype(BF))

    @pl.when(s == 3)
    def _():
        def put(value, start):
            size = value.shape[0] // 64
            for zy in range(16):
                for k, old in enumerate((0, 2, 1, 3)):
                    to, at = (zy * 4 + k) * size, (zy * 4 + old) * size
                    grad_ref[to : to + size, start : start + value.shape[1]] = value[at : at + size]

        put(mm_tn(normed_ref[...], qkv_scr[...]).astype(BF), 0)
        put(mm_tn(d_scr[...], mixed_ref[...]).astype(BF), cut)


def attn_backward(d_pieces, w, cosines, sines, saved, head):
    normed, query, key, value, probs, mixed = saved
    part, d = d_pieces[0].shape
    rows = 2 * part
    nq, cut = GROUP * head, (GROUP + 2) * head
    wide = cut + nq
    spec = lambda width: row_block(width)(rows)
    return pl.pallas_call(
        lambda *refs: attn_backward_kernel(head, *refs),
        grid=(4,),
        in_specs=[fixed(p.shape) for p in d_pieces]
        + [fixed(w.shape), spec(2 * head), spec(2 * head), fixed(normed.shape)]
        + [spec(nq), spec(nq), spec(nq)]
        + [pl.BlockSpec((GROUP * rows, rows), lambda s: (step_block(s), 0)), fixed(mixed.shape)],
        out_specs=halves(rows, d) + [fixed((d, wide))],
        out_shape=[jax.ShapeDtypeStruct((2 * rows, d), BF)] * 2
        + [jax.ShapeDtypeStruct((d, wide), BF)],
        scratch_shapes=[
            pltpu.VMEM((4 * rows, d), BF),
            pltpu.VMEM((4 * rows, cut), BF),
        ],
        compiler_params=pltpu.CompilerParams(vmem_limit_bytes=VMEM_LIMIT),
        cost_estimate=cost(10),
    )(*d_pieces, w, cosines, sines, normed, query, key, value, probs, mixed)


def mlp_kernel(*refs):
    n_pieces, c_pieces = refs[:8], refs[8:16]
    (wg_ref, wu_ref, wd_ref, dg_ref, du_ref, hid_ref, mine_ref, other_ref,
     n_scr, c_scr, w_scr, d_scr) = refs[16:]
    j = pl.program_id(0)
    part = n_pieces[0].shape[0]
    tile = wg_ref.shape[1]
    ff = 4 * tile

    @pl.when(j == 0)
    def _():
        for i in range(8):
            n_scr[i * part : (i + 1) * part] = n_pieces[i][...]
            c_scr[i * part : (i + 1) * part] = c_pieces[i][...]

    for step in range(4):

        @pl.when(j == step)
        def _():
            w_scr[:, step * tile : (step + 1) * tile] = wg_ref[...]
            w_scr[:, ff + step * tile : ff + (step + 1) * tile] = wu_ref[...]
            gate = mm(n_scr[...], wg_ref[...])
            up = mm(n_scr[...], wu_ref[...])
            d_hidden = mm(c_scr[...], wd_ref[...])
            sig = jax.nn.sigmoid(gate)
            silu = gate * sig
            hid_ref[...] = (silu * up).astype(BF)
            d_gate = (d_hidden * up * sig * (1.0 + gate * (1.0 - sig))).astype(BF)
            d_up = (d_hidden * silu).astype(BF)
            dg_ref[...] = d_gate
            du_ref[...] = d_up
            d_scr[:, step * tile : (step + 1) * tile] = d_gate
            d_scr[:, ff + step * tile : ff + (step + 1) * tile] = d_up

    @pl.when(j >= 4)
    def _():
        wide = mine_ref.shape[1]
        rows = pl.ds(pl.multiple_of((j - 4) * wide, wide), wide)
        d_n2 = mm_nt(d_scr[...], w_scr[rows, :]).astype(BF)
        mine_ref[...] = d_n2[: 4 * part]
        other_ref[...] = d_n2[4 * part :]


def mlp(n_pieces, c_pieces, w):
    part, d = n_pieces[0].shape
    rows, ff = 8 * part, w.shape[1] // 3
    tile, wide = ff // 4, d // 4
    at = lambda k: pl.BlockSpec((d, tile), lambda j: (0, 4 * k + jnp.minimum(j, 3)))
    return pl.pallas_call(
        mlp_kernel,
        grid=(8,),
        in_specs=[fixed((part, d))] * 16 + [at(0), at(1), at(2)],
        out_specs=[pl.BlockSpec((rows, tile), lambda j: (0, jnp.minimum(j, 3)))] * 3
        + [pl.BlockSpec((rows // 2, wide), lambda j: (0, jnp.maximum(j - 4, 0)))] * 2,
        out_shape=[jax.ShapeDtypeStruct((rows, ff), BF)] * 3
        + [jax.ShapeDtypeStruct((rows // 2, d), BF)] * 2,
        scratch_shapes=[
            pltpu.VMEM((rows, d), BF),
            pltpu.VMEM((rows, d), BF),
            pltpu.VMEM((d, 2 * ff), BF),
            pltpu.VMEM((rows, 2 * ff), BF),
        ],
        compiler_params=pltpu.CompilerParams(vmem_limit_bytes=VMEM_LIMIT),
        cost_estimate=cost(40),
    )(*n_pieces, *c_pieces, w, w, w)


def mlp_grads_kernel(*refs):
    n_pieces, c_pieces = refs[:8], refs[8:16]
    dg_ref, du_ref, hid_ref, g_ref = refs[16:]
    ff = dg_ref.shape[1]
    n_part = jnp.concatenate([piece[...] for piece in n_pieces], axis=0).T
    c_part = jnp.concatenate([piece[...] for piece in c_pieces], axis=0).T
    g_ref[:, :ff] = mm(n_part, dg_ref[...]).astype(BF)
    g_ref[:, ff : 2 * ff] = mm(n_part, du_ref[...]).astype(BF)
    g_ref[:, 2 * ff :] = mm(c_part, hid_ref[...]).astype(BF)


def mlp_grads(n_pieces, c_pieces, d_gate, d_up, hidden):
    part, d = n_pieces[0].shape
    rows, ff = hidden.shape
    wide = d // 8
    return pl.pallas_call(
        mlp_grads_kernel,
        grid=(8,),
        in_specs=[pl.BlockSpec((part, wide), lambda j: (0, j))] * 16 + [fixed((rows, ff))] * 3,
        out_specs=pl.BlockSpec((wide, 3 * ff), lambda j: (j, 0)),
        out_shape=jax.ShapeDtypeStruct((d, 3 * ff), BF),
        compiler_params=pltpu.CompilerParams(vmem_limit_bytes=VMEM_LIMIT),
        cost_estimate=cost(40),
    )(*n_pieces, *c_pieces, d_gate, d_up, hidden)


def mlp_out_kernel(x_ref, w_ref, mine_ref, other_ref):
    half = x_ref.shape[0] // 2
    out = mm_nt(x_ref[...], w_ref[...]).astype(BF)
    mine_ref[...] = out[:half]
    other_ref[...] = out[half:]


def mlp_out(hid, w):
    rows, ff = hid.shape
    d = w.shape[0]
    wide = d // 4
    return pl.pallas_call(
        mlp_out_kernel,
        grid=(4,),
        in_specs=[fixed((rows, ff)), pl.BlockSpec((wide, ff), lambda j: (j, 2))],
        out_specs=[pl.BlockSpec((rows // 2, wide), lambda j: (0, j))] * 2,
        out_shape=[jax.ShapeDtypeStruct((rows // 2, d), BF)] * 2,
        compiler_params=pltpu.CompilerParams(vmem_limit_bytes=VMEM_LIMIT),
        cost_estimate=cost(5),
    )(hid, w)


def store_placed(ref, value):
    tile = value.shape[1] // 16
    half = tile // 2
    low = lax.broadcasted_iota(jnp.int32, (value.shape[0], tile), 1) < half
    for i in range(8):
        even = value[:, 2 * i * tile : (2 * i + 1) * tile]
        odd = value[:, (2 * i + 1) * tile : (2 * i + 2) * tile]
        first = jnp.where(low, even, pltpu.roll(odd, half, 1))
        second = jnp.where(low, pltpu.roll(even, half, 1), odd)
        ref[:, i * tile : (i + 1) * tile] = first.astype(ref.dtype)
        ref[:, (8 + i) * tile : (9 + i) * tile] = second.astype(ref.dtype)


def layer_output_kernel(resid_ref, own_ref, g2_ref, g1_ref, g3_ref, out_ref):
    total = total_of([own_ref[...]], [g2_ref[...], g1_ref[...], g3_ref[...]])
    store_placed(out_ref, resid_ref[...] + total)


def input_grad_kernel(
    d_resid_ref, x_ref, factor_ref, gain_ref, own_ref, g2_ref, g1_ref, g3_ref, out_ref
):
    d_normed = total_of([own_ref[...]], [g2_ref[...], g1_ref[...], g3_ref[...]])
    factor = factor_ref[:, :1]
    u1 = x_ref[...].astype(F32) * factor
    back = norm_back(u1, factor, gain_ref[0:1, :], d_normed)
    store_placed(out_ref, d_resid_ref[...] + back)


def finish(kernel, arrays, specs, dtype):
    shape = arrays[0].shape
    return pl.pallas_call(
        kernel,
        grid=(1,),
        in_specs=specs,
        out_specs=fixed(shape),
        out_shape=jax.ShapeDtypeStruct(shape, dtype),
        compiler_params=pltpu.CompilerParams(vmem_limit_bytes=VMEM_LIMIT),
        cost_estimate=cost(2),
    )(*arrays)


def token_tables(seg, shift, own, head):
    count, block = seg.shape
    seg = jnp.where(shift == 0, seg, jnp.roll(seg, own, axis=1))
    order = (jnp.arange(block, dtype=jnp.int32)[None, :] + shift * own) % block
    earlier = jnp.sum((seg[:, None, :] < seg[:, :, None]).astype(jnp.int32), axis=2)
    positions = (order - earlier).reshape(count * block, 1)
    allowed = (seg[:, :, None] == seg[:, None, :]) & (order[:, None, :] <= order[:, :, None])
    mask = jnp.where(allowed, 0.0, MASKED).astype(F32).reshape(count * block, block)
    lane = jnp.arange(2 * head)
    frequency = jnp.exp(-math.log(ROPE_BASE) * ((lane % (head // 2)).astype(F32) / (head // 2)))
    angles = positions.astype(F32) * frequency
    sines = jnp.where(lane % head < head // 2, -1.0, 1.0) * jnp.sin(angles)
    return jnp.cos(angles), sines, mask


def local(
    tokens, segment_ids, attn_gain, w_query, w_key, w_value, w_out,
    mlp_gain, w_gate, w_up, w_down, cotangent,
):
    a, c, t = lax.axis_index("a"), lax.axis_index("c"), lax.axis_index("t")
    own = tokens.shape[0]
    nq = w_query.shape[1] // 4
    nk = w_key.shape[1] // 4
    ff = w_gate.shape[1] // 4
    head = nk
    cut = nq + 2 * nk

    gains = jnp.stack([attn_gain, mlp_gain], axis=1)
    gains = jnp.pad(gains, ((0, 0), (0, GAIN_COLS - 2)))
    quarter = lambda w, i: w[:, i * w.shape[1] // 4 : (i + 1) * w.shape[1] // 4]
    attn_pack = [
        jnp.concatenate(
            [quarter(w, i) for w in (w_query, w_key, w_value, w_out.T)] + [gains], axis=1
        )
        for i in range(4)
    ]
    attn_rows, attn_got = spread(attn_pack, a, c)
    attn_w = lax.all_gather(attn_rows, ("z", "y"), axis=0, tiled=True)
    x_own, c_own = to_place(tokens), to_place(cotangent)
    x_pieces = gather_rows(after(x_own, attn_got))
    mlp_pack = [
        jnp.concatenate([quarter(w, i) for w in (w_gate, w_up, w_down.T)], axis=1) for i in range(4)
    ]
    mlp_rows, mlp_got = spread(mlp_pack, a, c, x_pieces[1:4])
    mlp_w = lax.all_gather(mlp_rows, ("z", "y"), axis=0, tiled=True)
    c_pieces = gather_rows(after(c_own, *x_pieces[1:4]))

    seg = jnp.stack([segment_ids, lax.ppermute(segment_ids, "a", SWAP)])
    seg = jnp.concatenate([seg, swap_core(seg)], axis=0)
    shift = jnp.stack([t, t ^ a, t, t ^ a])[:, None]
    cosines, sines, mask = token_tables(seg, shift, own, head)

    forward = attn_forward(x_pieces, attn_w, cosines, sines, mask, head)
    mine, other, normed, factor1, query, key, value, probs, mixed, gain_rows = forward
    gain_m = gain_rows[1]
    parts = chip_parts(mine, swap_core(after(other, *c_pieces[1:4])))
    resid = x_own.astype(F32) + total_of(parts, send_parts(parts))

    factor2 = lax.rsqrt(jnp.mean(resid * resid, axis=-1, keepdims=True) + EPSILON)
    u2 = resid * factor2
    n_pieces = gather_rows((u2 * gain_m).astype(BF))
    d_gate, d_up, hidden, mine, other = mlp(n_pieces, c_pieces, mlp_w)
    swapped = swap_core(other)
    grads = mlp_grads(n_pieces, c_pieces, d_gate, d_up, hidden)
    mlp_grad = lax.psum_scatter(grads, ("z", "y"), scatter_dimension=0, tiled=True)
    parts = chip_parts(mine, after(swapped, grads))
    got = send_parts(parts)
    out_mine, out_other = mlp_out(after(hidden, parts[1]), mlp_w)
    d_n2 = total_of(parts, after(got, out_mine))

    d_resid = c_own.astype(F32) + norm_back(u2, factor2, gain_m, d_n2)
    d_branch = d_resid.astype(BF)
    d_chips = [from_chip(d_branch, k) for k in (2, 1, 3)]
    out_parts = chip_parts(out_mine, swap_core(after(out_other, d_branch)))
    d_chips = after(d_chips, out_parts[1])
    out_got = send_parts(out_parts)
    d_pieces = [d_branch, *d_chips]
    d_pieces += [swap_core(piece) for piece in d_pieces]
    saved = (normed, query, key, value, probs, mixed)
    mine, other, attn_grads = attn_backward(d_pieces, attn_w, cosines, sines, saved, head)
    attn_grads = attn_grads.reshape(32, -1, attn_grads.shape[1])
    h = lax.all_to_all(attn_grads, ("z", "y", "c"), split_axis=0, concat_axis=0, tiled=True)
    parts = chip_parts(mine, swap_core(after(other, *out_got)))
    got = send_parts(parts)
    mlp_grad = after(mlp_grad, parts[1])

    by_x, came = unspread_x(mlp_grad, a)
    g, by_core = unspread_core(by_x, came, a, c)
    gate_grad, up_grad, down_grad = (columns_of(g, i * ff, ff) for i in range(3))
    rows = fixed(x_own.shape)
    layer_output = finish(
        layer_output_kernel, [resid, out_parts[0], *out_got], [rows] * 5, BF
    )
    input_grad = finish(
        input_grad_kernel,
        [d_resid, x_own, factor1, gain_rows, parts[0], *got],
        [rows, rows, fixed((own, 128)), fixed(gain_rows.shape)] + [rows] * 4,
        F32,
    )
    along = lambda w, grad: jnp.sum(w.astype(F32) * grad, axis=1)
    mlp_gain_grad = along(w_gate, gate_grad) + along(w_up, up_grad)
    h = h.reshape(16, 2, 2, -1, h.shape[2])
    h = jnp.sum(h.astype(F32), axis=0)
    first = a == 0
    keep = jnp.where(first, h[:, 0], h[:, 1])
    give = jnp.where(first, h[:, 1], h[:, 0]).astype(BF)
    came = lax.ppermute(after(give, by_core), "a", SWAP).astype(F32)
    h = [*jnp.where(first, keep, came), *jnp.where(first, came, keep)]
    query_grad = columns_of(h, 0, nq)
    key_grad = columns_of(h, nq, nk)
    value_grad = columns_of(h, nq + nk, nk)
    out_grad = columns_of(h, cut, nq).T
    attn_gain_grad = along(w_query, query_grad) + along(w_key, key_grad)
    attn_gain_grad = attn_gain_grad + along(w_value, value_grad)
    gain_grads = jnp.stack([attn_gain_grad, mlp_gain_grad])
    gain_grads = gain_grads / jnp.stack([attn_gain, mlp_gain]).astype(F32)
    gain_grads = gain_grads + lax.ppermute(gain_grads, "t", SWAP)
    return (
        layer_output, input_grad, gain_grads[0], query_grad, key_grad, value_grad, out_grad,
        gain_grads[1], gate_grad, up_grad, down_grad.T,
    )


def solution(mesh):
    fine = Mesh(mesh.devices.reshape(2, 4, 4, 2, 2), ("a", "z", "y", "c", "t"))
    dp = ("a", "z", "y", "c")
    rows = P(dp + ("t",), None)
    return jax.shard_map(
        local,
        mesh=fine,
        in_specs=(
            rows, P(dp), P(dp), P(dp, "t"), P(dp, "t"), P(dp, "t"), P("t", dp),
            P(dp), P(dp, "t"), P(dp, "t"), P("t", dp), rows,
        ),
        out_specs=(
            rows, rows, P(dp), P(dp, "t"), P(dp, "t"), P(dp, "t"), P("t", dp),
            P(dp), P(dp, "t"), P(dp, "t"), P("t", dp),
        ),
        check_vma=False,
    )
```

```python
import math

import jax
import jax.numpy as jnp
from jax import lax
from jax.experimental import pallas as pl
from jax.experimental.pallas import tpu as pltpu
from jax.sharding import Mesh
from jax.sharding import PartitionSpec as P

HEADS = 32
KV_HEADS = 8
GROUP = HEADS // KV_HEADS
EPSILON = 1e-05
ROPE_BASE = 500000.0
MASKED = -1e30
VMEM_LIMIT = 56 * 2**20
BF = jnp.bfloat16
F32 = jnp.float32


def cost(micros):
    return pl.CostEstimate(flops=micros * 10**9, bytes_accessed=2**20, transcendentals=0)


SWAP = [(0, 1), (1, 0)]


def mm(left, right):
    return jnp.dot(left, right, preferred_element_type=F32)


def mm_nt(left, right):
    return lax.dot_general(left, right, (((1,), (1,)), ((), ())), preferred_element_type=F32)


def mm_tn(left, right):
    return lax.dot_general(left, right, (((0,), (0,)), ((), ())), preferred_element_type=F32)


AT = (0, 2, 1, 3)


def from_chip(value, k):
    return lax.ppermute(value, ("a", "t"), [(AT[(i + k) % 4], AT[i]) for i in range(4)])


def to_chip(value, k):
    return lax.ppermute(value, ("a", "t"), [(AT[i], AT[(i + k) % 4]) for i in range(4)])


def after(value, *others):
    return lax.optimization_barrier((value, *others))[0]


def swap_core(value):
    return lax.ppermute(value, "c", SWAP)


def gather_rows(rows):
    mine = [rows, from_chip(rows, 2), from_chip(rows, 1), from_chip(rows, 3)]
    return mine + [swap_core(piece) for piece in mine]


def chip_parts(mine, got):
    rows = mine.shape[0] // 4
    parts = [
        mine[i * rows : (i + 1) * rows].astype(F32) + got[i * rows : (i + 1) * rows].astype(F32)
        for i in range(4)
    ]
    return [parts[0]] + [part.astype(BF) for part in parts[1:]]


def send_parts(parts):
    return [to_chip(part, k) for part, k in zip(parts[1:], (2, 1, 3))]


def total_of(parts, got):
    total = parts[0]
    for part in got:
        total = total + part.astype(F32)
    return total


def split_quarters(quarters, c):
    first = c == 0
    keep = [jnp.where(first, quarters[2 * i], quarters[2 * i + 1]) for i in range(2)]
    give = [jnp.where(first, quarters[2 * i + 1], quarters[2 * i]) for i in range(2)]
    return jnp.concatenate(keep, axis=0), jnp.concatenate(give, axis=0)


def spread(keep, give, a, c, wait=()):
    first = c == 0
    r = keep.shape[0] // 2
    got = swap_core(give)
    both = []
    for i in range(2):
        k, g = keep[i * r : (i + 1) * r], got[i * r : (i + 1) * r]
        both.append(jnp.concatenate([jnp.where(first, k, g), jnp.where(first, g, k)], axis=0))
    first_a = a == 0
    keep_a = jnp.where(first_a, both[0], both[1])
    give_a = jnp.where(first_a, both[1], both[0])
    got_a = lax.ppermute(after(give_a, *wait), "a", SWAP)
    rows = [jnp.where(first_a, keep_a, got_a), jnp.where(first_a, got_a, keep_a)]
    return jnp.concatenate(rows, axis=0), give_a


def unspread_x(rows, a):
    half = rows.shape[0] // 2
    first = a == 0
    give = jnp.where(first, rows[half:], rows[:half])
    return jnp.where(first, rows[:half], rows[half:]), lax.ppermute(give, "a", SWAP)


def unspread_core(mine, came, a, c):
    r = mine.shape[0] // 2
    first_a, first = a == 0, c == 0
    by_a = [jnp.where(first_a, mine, came), jnp.where(first_a, came, mine)]
    keep = [jnp.where(first, v[:r], v[r:]) for v in by_a]
    give = [jnp.where(first, v[r:], v[:r]) for v in by_a]
    got = swap_core(jnp.concatenate(give, axis=0))
    quarters = []
    for k, g in zip(keep, (got[:r], got[r:])):
        quarters += [jnp.where(first, k, g), jnp.where(first, g, k)]
    return quarters


def columns_of(quarters, start, width):
    return jnp.concatenate([q[:, start : start + width] for q in quarters], axis=1).astype(F32)


def to_place(rows):
    n, d = rows.shape
    return rows.reshape(n, 2, 16, d // 32).transpose(0, 2, 1, 3).reshape(n, d)


def norm_factor(values):
    return lax.rsqrt(jnp.mean(values * values, axis=-1, keepdims=True) + EPSILON)


def norm_back(values, upstream):
    factor = norm_factor(values)
    rescaled = values * factor
    return factor * (upstream - rescaled * jnp.mean(upstream * rescaled, axis=-1, keepdims=True))


def step_block(s):
    return (s + 2) % 4


def row_block(width):
    return lambda rows: pl.BlockSpec((rows, width), lambda s: (step_block(s), 0))


def fixed(shape):
    return pl.BlockSpec(shape, lambda *_: (0,) * len(shape))


def halves(rows, width):
    return [
        pl.BlockSpec((rows, width), lambda s: (jnp.maximum(s - 2, 0), 0)),
        pl.BlockSpec((rows, width), lambda s: (jnp.minimum(s, 1), 0)),
    ]


def load_block(s, pieces, scratch):
    part = pieces[0].shape[0]
    for b in range(4):

        @pl.when(step_block(s) == b)
        def _():
            scratch[:part] = pieces[2 * b][...]
            scratch[part:] = pieces[2 * b + 1][...]


def store_half(s, mine_ref, other_ref, value):
    @pl.when(s < 2)
    def _():
        other_ref[...] = value

    @pl.when(s >= 2)
    def _():
        mine_ref[...] = value


def turn(values, cosines, sines, head):
    width = values.shape[1]
    lane = lax.broadcasted_iota(jnp.int32, values.shape, 1)
    low = lane % head < head // 2
    partner = jnp.where(
        low, pltpu.roll(values, width - head // 2, 1), pltpu.roll(values, head // 2, 1)
    )
    return values * cosines + partner * sines


def double(values, times):
    return jnp.concatenate([values] * times, axis=1)


def by_head(values, head):
    lane = lax.broadcasted_iota(jnp.int32, values.shape, 1) // head
    zero = jnp.zeros_like(values)
    return jnp.concatenate([jnp.where(lane == h, values, zero) for h in range(GROUP)], axis=0)


def take_heads(values, rows, head):
    lane = lax.broadcasted_iota(jnp.int32, (rows, values.shape[1]), 1) // head
    out = values[:rows]
    for h in range(1, GROUP):
        out = jnp.where(lane == h, values[h * rows : (h + 1) * rows], out)
    return out


def fold_heads(values, head):
    pair = values[:, : 2 * head] + values[:, 2 * head :]
    return pair + pltpu.roll(pair, head, 1)


def pack_kernel(c_ref, gain_ref, wq_ref, wk_ref, wv_ref, wo_ref, keep_ref, give_ref):
    r, wide = wq_ref.shape[0], wq_ref.shape[1] // 4
    head = wk_ref.shape[1] // 4
    row = jnp.broadcast_to(gain_ref[...].astype(F32), (8, r))
    row = jnp.where(lax.broadcasted_iota(jnp.int32, row.shape, 0) == 0, row, 0.0).astype(BF)
    gain = mm_tn(row, jnp.ones((8, 2 * head), BF))
    queries = (wq_ref[...].astype(F32) * double(gain, wq_ref.shape[1] // (2 * head))).astype(BF)
    keys = wk_ref[...].astype(F32) * double(gain, 2)
    values = wv_ref[...].astype(F32) * double(gain, 2)
    low = lax.broadcasted_iota(jnp.int32, (r, 2 * head), 1) < head

    def fill(ref, a, q):
        rows = slice(a * r, (a + 1) * r)
        columns = slice(q * wide, (q + 1) * wide)
        pair = slice(q // 2 * 2 * head, (q // 2 + 1) * 2 * head)
        key, value = keys[:, pair], values[:, pair]
        if q % 2:
            key = pltpu.roll(key, head, 1)
        else:
            value = pltpu.roll(value, head, 1)
        ref[rows, :wide] = queries[:, columns]
        ref[rows, wide : wide + 2 * head] = jnp.where(low, key, value).astype(BF)
        ref[rows, wide + 2 * head :] = wo_ref[:, columns]

    for own in range(2):

        @pl.when(c_ref[0] == own)
        def _():
            for a in range(2):
                fill(keep_ref, a, 2 * a + own)
                fill(give_ref, a, 2 * a + 1 - own)


def pack_attn(c, gain, w_query, w_key, w_value, w_out_t):
    r, columns = w_query.shape
    shape = jax.ShapeDtypeStruct((2 * r, columns // 2 + w_key.shape[1] // 2), BF)
    vmem = pl.BlockSpec(memory_space=pltpu.VMEM)
    return pl.pallas_call(
        pack_kernel,
        in_specs=[pl.BlockSpec(memory_space=pltpu.SMEM)] + [vmem] * 5,
        out_specs=[vmem] * 2,
        out_shape=[shape, shape],
        cost_estimate=cost(2),
    )(c.reshape(1).astype(jnp.int32), gain, w_query, w_key, w_value, w_out_t)


def attn_forward_kernel(head, *refs):
    pieces = refs[:8]
    (w_ref, cos_ref, sin_ref, mask_ref,
     mine_ref, other_ref, normed_ref, q_ref, k_ref, v_ref, probs_ref, mixed_ref,
     x_ref) = refs[8:]
    s = pl.program_id(0)
    nq, cut = GROUP * head, (GROUP + 2) * head
    rows = x_ref.shape[0]

    load_block(s, pieces, x_ref)
    x = x_ref[...].astype(F32)
    factor = lax.rsqrt(jnp.mean(x * x, axis=-1, keepdims=True) + EPSILON)
    normed = (x * factor).astype(BF)
    normed_ref[...] = normed
    qkv = mm(normed, w_ref[:, :cut])
    cosines, sines = cos_ref[...], sin_ref[...]
    query = turn(qkv[:, :nq], double(cosines, 2), double(sines, 2), head).astype(BF)
    kv = qkv[:, nq:]
    turned = turn(kv, cosines, sines, head)
    low = lax.broadcasted_iota(jnp.int32, kv.shape, 1) < head
    key = double(jnp.where(low, turned, pltpu.roll(turned, head, 1)), 2).astype(BF)
    value = double(jnp.where(low, pltpu.roll(kv, head, 1), kv), 2).astype(BF)
    q_ref[...] = query
    k_ref[...] = key
    v_ref[...] = value
    scores = mm_nt(by_head(query, head), key) * (1.0 / math.sqrt(head))
    allowed = mask_ref[...] == 0
    scores = jnp.where(jnp.concatenate([allowed] * GROUP, axis=0), scores, MASKED)
    weights = jnp.exp(scores - jnp.max(scores, axis=-1, keepdims=True))
    probs = weights / jnp.sum(weights, axis=-1, keepdims=True)
    probs_ref[...] = probs
    mixed = take_heads(mm(probs.astype(BF), value), rows, head).astype(BF)
    mixed_ref[...] = mixed
    store_half(s, mine_ref, other_ref, mm_nt(mixed, w_ref[:, cut : cut + nq]).astype(BF))


def attn_forward(pieces, w, cosines, sines, mask, head):
    part, d = pieces[0].shape
    rows = 2 * part
    nq = GROUP * head
    spec = lambda width: row_block(width)(rows)
    return pl.pallas_call(
        lambda *refs: attn_forward_kernel(head, *refs),
        grid=(4,),
        in_specs=[fixed(p.shape) for p in pieces]
        + [fixed(w.shape), spec(2 * head), spec(2 * head), spec(rows)],
        out_specs=halves(rows, d)
        + [spec(d), spec(nq), spec(nq), spec(nq)]
        + [pl.BlockSpec((GROUP * rows, rows), lambda s: (step_block(s), 0)), spec(nq)],
        out_shape=[jax.ShapeDtypeStruct((2 * rows, d), BF)] * 2
        + [jax.ShapeDtypeStruct((4 * rows, d), BF)]
        + [jax.ShapeDtypeStruct((4 * rows, nq), BF)] * 3
        + [
            jax.ShapeDtypeStruct((4 * GROUP * rows, rows), F32),
            jax.ShapeDtypeStruct((4 * rows, nq), BF),
        ],
        scratch_shapes=[pltpu.VMEM((rows, d), BF)],
        compiler_params=pltpu.CompilerParams(vmem_limit_bytes=VMEM_LIMIT),
        cost_estimate=cost(30),
    )(*pieces, w, cosines, sines, mask)


def attn_backward_kernel(head, *refs):
    d_pieces = refs[:8]
    (w_ref, cos_ref, sin_ref, normed_ref, q_ref, k_ref, v_ref, probs_ref, mixed_ref,
     mine_ref, other_ref, grad_ref, d_scr, n_scr, qkv_scr) = refs[8:]
    s = pl.program_id(0)
    nq, cut = GROUP * head, (GROUP + 2) * head
    part = d_pieces[0].shape[0]
    rows = 2 * part
    scale = 1.0 / math.sqrt(head)

    @pl.when(s == 0)
    def _():
        for i in range(8):
            d_scr[i * part : (i + 1) * part] = d_pieces[i][...]

    here = pl.ds(pl.multiple_of(step_block(s) * rows, rows), rows)
    n_scr[here] = normed_ref[...]
    d_branch = d_scr[here]
    d_mixed = by_head(mm(d_branch, w_ref[:, cut : cut + nq]).astype(BF), head)
    d_probs = mm_nt(d_mixed, v_ref[...])
    probs = probs_ref[...]
    d_value = fold_heads(mm_tn(probs.astype(BF), d_mixed), head)
    d_scores = probs * (d_probs - jnp.sum(d_probs * probs, axis=-1, keepdims=True))
    d_scores = d_scores.astype(BF)
    d_query = take_heads(mm(d_scores, k_ref[...]), rows, head) * scale
    d_key = fold_heads(mm_tn(d_scores, by_head(q_ref[...], head)), head) * scale
    cosines, sines = cos_ref[...], -sin_ref[...]
    d_query = turn(d_query, double(cosines, 2), double(sines, 2), head).astype(BF)
    d_key = turn(d_key, cosines, sines, head)
    low = lax.broadcasted_iota(jnp.int32, d_key.shape, 1) < head
    d_kv = jnp.where(low, d_key, d_value).astype(BF)
    d_qkv = jnp.concatenate([d_query, d_kv], axis=1)
    qkv_scr[here] = d_qkv
    d_normed = mm_nt(d_qkv, w_ref[:, :cut])
    store_half(s, mine_ref, other_ref, d_normed.astype(BF))

    @pl.when(s == 3)
    def _():
        def put(value, start):
            size = value.shape[0] // 64
            for zy in range(16):
                for k, old in enumerate((0, 2, 1, 3)):
                    to, at = (zy * 4 + k) * size, (zy * 4 + old) * size
                    grad_ref[to : to + size, start : start + value.shape[1]] = value[at : at + size]

        put(mm_tn(n_scr[...], qkv_scr[...]).astype(BF), 0)
        put(mm_tn(d_scr[...], mixed_ref[...]).astype(BF), cut)


def attn_backward(d_pieces, w, cosines, sines, saved, head):
    normed, query, key, value, probs, mixed = saved
    part, d = d_pieces[0].shape
    rows = 2 * part
    nq, cut = GROUP * head, (GROUP + 2) * head
    wide = cut + nq
    spec = lambda width: row_block(width)(rows)
    return pl.pallas_call(
        lambda *refs: attn_backward_kernel(head, *refs),
        grid=(4,),
        in_specs=[fixed(p.shape) for p in d_pieces]
        + [fixed(w.shape), spec(2 * head), spec(2 * head), spec(d)]
        + [spec(nq), spec(nq), spec(nq)]
        + [pl.BlockSpec((GROUP * rows, rows), lambda s: (step_block(s), 0)), fixed(mixed.shape)],
        out_specs=halves(rows, d) + [fixed((d, wide))],
        out_shape=[jax.ShapeDtypeStruct((2 * rows, d), BF)] * 2
        + [jax.ShapeDtypeStruct((d, wide), BF)],
        scratch_shapes=[
            pltpu.VMEM((4 * rows, d), BF),
            pltpu.VMEM((4 * rows, d), BF),
            pltpu.VMEM((4 * rows, cut), BF),
        ],
        compiler_params=pltpu.CompilerParams(vmem_limit_bytes=VMEM_LIMIT),
        cost_estimate=cost(10),
    )(*d_pieces, w, cosines, sines, normed, query, key, value, probs, mixed)


def mlp_kernel(*refs):
    n_pieces, c_pieces = refs[:8], refs[8:16]
    (wg_ref, wu_ref, wd_ref, dg_ref, du_ref, hid_ref, mine_ref, other_ref,
     n_scr, c_scr, w_scr, d_scr) = refs[16:]
    j = pl.program_id(0)
    part = n_pieces[0].shape[0]
    tile = wg_ref.shape[1]
    ff = 4 * tile

    @pl.when(j == 0)
    def _():
        for i in range(8):
            n_scr[i * part : (i + 1) * part] = n_pieces[i][...]
            c_scr[i * part : (i + 1) * part] = c_pieces[i][...]

    for step in range(4):

        @pl.when(j == step)
        def _():
            w_scr[:, step * tile : (step + 1) * tile] = wg_ref[...]
            w_scr[:, ff + step * tile : ff + (step + 1) * tile] = wu_ref[...]
            gate = mm(n_scr[...], wg_ref[...])
            up = mm(n_scr[...], wu_ref[...])
            d_hidden = mm(c_scr[...], wd_ref[...])
            sig = jax.nn.sigmoid(gate)
            silu = gate * sig
            hid_ref[...] = (silu * up).astype(BF)
            d_gate = (d_hidden * up * sig * (1.0 + gate * (1.0 - sig))).astype(BF)
            d_up = (d_hidden * silu).astype(BF)
            dg_ref[...] = d_gate
            du_ref[...] = d_up
            d_scr[:, step * tile : (step + 1) * tile] = d_gate
            d_scr[:, ff + step * tile : ff + (step + 1) * tile] = d_up

    @pl.when(j >= 4)
    def _():
        wide = mine_ref.shape[1]
        rows = pl.ds(pl.multiple_of((j - 4) * wide, wide), wide)
        d_n2 = mm_nt(d_scr[...], w_scr[rows, :]).astype(BF)
        mine_ref[...] = d_n2[: 4 * part]
        other_ref[...] = d_n2[4 * part :]


def mlp(n_pieces, c_pieces, w):
    part, d = n_pieces[0].shape
    rows, ff = 8 * part, w.shape[1] // 3
    tile, wide = ff // 4, d // 4
    at = lambda k: pl.BlockSpec((d, tile), lambda j: (0, 4 * k + jnp.minimum(j, 3)))
    return pl.pallas_call(
        mlp_kernel,
        grid=(8,),
        in_specs=[fixed((part, d))] * 16 + [at(0), at(1), at(2)],
        out_specs=[pl.BlockSpec((rows, tile), lambda j: (0, jnp.minimum(j, 3)))] * 3
        + [pl.BlockSpec((rows // 2, wide), lambda j: (0, jnp.maximum(j - 4, 0)))] * 2,
        out_shape=[jax.ShapeDtypeStruct((rows, ff), BF)] * 3
        + [jax.ShapeDtypeStruct((rows // 2, d), BF)] * 2,
        scratch_shapes=[
            pltpu.VMEM((rows, d), BF),
            pltpu.VMEM((rows, d), BF),
            pltpu.VMEM((d, 2 * ff), BF),
            pltpu.VMEM((rows, 2 * ff), BF),
        ],
        compiler_params=pltpu.CompilerParams(vmem_limit_bytes=VMEM_LIMIT),
        cost_estimate=cost(40),
    )(*n_pieces, *c_pieces, w, w, w)


def mlp_grads_kernel(*refs):
    n_pieces, c_pieces = refs[:8], refs[8:16]
    dg_ref, du_ref, hid_ref, g_ref = refs[16:]
    ff = dg_ref.shape[1]
    n_part = jnp.concatenate([piece[...] for piece in n_pieces], axis=0).T
    c_part = jnp.concatenate([piece[...] for piece in c_pieces], axis=0).T
    g_ref[:, :ff] = mm(n_part, dg_ref[...]).astype(BF)
    g_ref[:, ff : 2 * ff] = mm(n_part, du_ref[...]).astype(BF)
    g_ref[:, 2 * ff :] = mm(c_part, hid_ref[...]).astype(BF)


def mlp_grads(n_pieces, c_pieces, d_gate, d_up, hidden):
    part, d = n_pieces[0].shape
    rows, ff = hidden.shape
    wide = d // 8
    return pl.pallas_call(
        mlp_grads_kernel,
        grid=(8,),
        in_specs=[pl.BlockSpec((part, wide), lambda j: (0, j))] * 16 + [fixed((rows, ff))] * 3,
        out_specs=pl.BlockSpec((wide, 3 * ff), lambda j: (j, 0)),
        out_shape=jax.ShapeDtypeStruct((d, 3 * ff), BF),
        compiler_params=pltpu.CompilerParams(vmem_limit_bytes=VMEM_LIMIT),
        cost_estimate=cost(40),
    )(*n_pieces, *c_pieces, d_gate, d_up, hidden)


def mlp_out_kernel(x_ref, w_ref, mine_ref, other_ref):
    half = x_ref.shape[0] // 2
    out = mm_nt(x_ref[...], w_ref[...]).astype(BF)
    mine_ref[...] = out[:half]
    other_ref[...] = out[half:]


def mlp_out(hid, w):
    rows, ff = hid.shape
    d = w.shape[0]
    wide = d // 4
    return pl.pallas_call(
        mlp_out_kernel,
        grid=(4,),
        in_specs=[fixed((rows, ff)), pl.BlockSpec((wide, ff), lambda j: (j, 2))],
        out_specs=[pl.BlockSpec((rows // 2, wide), lambda j: (0, j))] * 2,
        out_shape=[jax.ShapeDtypeStruct((rows // 2, d), BF)] * 2,
        compiler_params=pltpu.CompilerParams(vmem_limit_bytes=VMEM_LIMIT),
        cost_estimate=cost(5),
    )(hid, w)


def store_placed(ref, value):
    tile = value.shape[1] // 16
    half = tile // 2
    low = lax.broadcasted_iota(jnp.int32, (value.shape[0], tile), 1) < half
    for i in range(8):
        even = value[:, 2 * i * tile : (2 * i + 1) * tile]
        odd = value[:, (2 * i + 1) * tile : (2 * i + 2) * tile]
        first = jnp.where(low, even, pltpu.roll(odd, half, 1))
        second = jnp.where(low, pltpu.roll(even, half, 1), odd)
        ref[:, i * tile : (i + 1) * tile] = first.astype(ref.dtype)
        ref[:, (8 + i) * tile : (9 + i) * tile] = second.astype(ref.dtype)


def d_resid_kernel(c_ref, resid_ref, own_ref, g2_ref, g1_ref, g3_ref, out_ref, low_ref):
    d_normed = total_of([own_ref[...]], [g2_ref[...], g1_ref[...], g3_ref[...]])
    out = c_ref[...].astype(F32) + norm_back(resid_ref[...], d_normed)
    out_ref[...] = out
    low_ref[...] = out.astype(BF)


def layer_output_kernel(resid_ref, own_ref, g2_ref, g1_ref, g3_ref, out_ref):
    total = total_of([own_ref[...]], [g2_ref[...], g1_ref[...], g3_ref[...]])
    store_placed(out_ref, resid_ref[...] + total)


def input_grad_kernel(d_resid_ref, x_ref, own_ref, g2_ref, g1_ref, g3_ref, out_ref):
    d_normed = total_of([own_ref[...]], [g2_ref[...], g1_ref[...], g3_ref[...]])
    back = norm_back(x_ref[...].astype(F32), d_normed)
    store_placed(out_ref, d_resid_ref[...] + back)


def finish(kernel, arrays, dtypes):
    shape = arrays[0].shape
    return pl.pallas_call(
        kernel,
        grid=(1,),
        in_specs=[fixed(shape)] * len(arrays),
        out_specs=[fixed(shape) for _ in dtypes],
        out_shape=[jax.ShapeDtypeStruct(shape, dtype) for dtype in dtypes],
        compiler_params=pltpu.CompilerParams(vmem_limit_bytes=VMEM_LIMIT),
        cost_estimate=cost(2),
    )(*arrays)


def token_tables(seg, shift, own, head):
    count, block = seg.shape
    seg = jnp.where(shift == 0, seg, jnp.roll(seg, own, axis=1))
    order = (jnp.arange(block, dtype=jnp.int32)[None, :] + shift * own) % block
    earlier = jnp.sum((seg[:, None, :] < seg[:, :, None]).astype(jnp.int32), axis=2)
    positions = (order - earlier).reshape(count * block, 1)
    allowed = (seg[:, :, None] == seg[:, None, :]) & (order[:, None, :] <= order[:, :, None])
    mask = jnp.where(allowed, 0.0, MASKED).astype(F32).reshape(count * block, block)
    lane = jnp.arange(2 * head)
    frequency = jnp.exp(-math.log(ROPE_BASE) * ((lane % (head // 2)).astype(F32) / (head // 2)))
    angles = positions.astype(F32) * frequency
    sines = jnp.where(lane % head < head // 2, -1.0, 1.0) * jnp.sin(angles)
    return jnp.cos(angles), sines, mask


def local(
    tokens, segment_ids, attn_gain, w_query, w_key, w_value, w_out,
    mlp_gain, w_gate, w_up, w_down, cotangent,
):
    a, c, t = lax.axis_index("a"), lax.axis_index("c"), lax.axis_index("t")
    own = tokens.shape[0]
    nq = w_query.shape[1] // 4
    nk = w_key.shape[1] // 4
    ff = w_gate.shape[1] // 4
    head = nk
    cut = nq + 2 * nk

    packed = pack_attn(c, attn_gain[None], w_query, w_key, w_value, w_out.T)
    attn_rows, attn_give = spread(*packed, a, c)
    attn_w = lax.all_gather(attn_rows, ("z", "y"), axis=0, tiled=True)
    x_own, c_own = to_place(tokens), to_place(cotangent)
    x_pieces = gather_rows(after(x_own, attn_give))
    gain_a, gain_m = after((attn_gain, mlp_gain), attn_give)
    gain_a, gain_m = gain_a.astype(F32)[:, None], gain_m.astype(F32)[:, None]
    quarter = lambda w, i: w[:, i * w.shape[1] // 4 : (i + 1) * w.shape[1] // 4]
    scaled = [(w.astype(F32) * gain_m).astype(BF) for w in (w_gate, w_up)]
    mlp_pack = [
        jnp.concatenate([quarter(w, i) for w in (*scaled, w_down.T)], axis=1) for i in range(4)
    ]
    mlp_rows, _ = spread(*split_quarters(mlp_pack, c), a, c, x_pieces[1:4])
    mlp_w = lax.all_gather(mlp_rows, ("z", "y"), axis=0, tiled=True)
    c_pieces = gather_rows(after(c_own, *x_pieces[1:4]))

    seg = jnp.stack([segment_ids, lax.ppermute(segment_ids, "a", SWAP)])
    seg = jnp.concatenate([seg, swap_core(seg)], axis=0)
    shift = jnp.stack([t, t ^ a, t, t ^ a])[:, None]
    cosines, sines, mask = token_tables(seg, shift, own, head)

    forward = attn_forward(x_pieces, attn_w, cosines, sines, mask, head)
    mine, other, normed, query, key, value, probs, mixed = forward
    parts = chip_parts(mine, swap_core(after(other, *c_pieces[1:4])))
    resid = x_own.astype(F32) + total_of(parts, send_parts(parts))

    n_pieces = gather_rows((resid * norm_factor(resid)).astype(BF))
    d_gate, d_up, hidden, mine, other = mlp(n_pieces, c_pieces, mlp_w)
    swapped = swap_core(other)
    grads = mlp_grads(n_pieces, c_pieces, d_gate, d_up, hidden)
    mlp_grad = lax.psum_scatter(grads, ("z", "y"), scatter_dimension=0, tiled=True)
    parts = chip_parts(mine, after(swapped, grads))
    got = send_parts(parts)
    out_mine, out_other = mlp_out(after(hidden, parts[1]), mlp_w)
    got = after(got, out_mine)

    d_resid, d_branch = finish(d_resid_kernel, [c_own, resid, parts[0], *got], [F32, BF])
    d_chips = [from_chip(d_branch, k) for k in (2, 1, 3)]
    out_parts = chip_parts(out_mine, swap_core(after(out_other, d_branch)))
    d_chips = after(d_chips, out_parts[1])
    out_got = send_parts(out_parts)
    d_pieces = [d_branch, *d_chips]
    d_pieces += [swap_core(piece) for piece in d_pieces]
    saved = (normed, query, key, value, probs, mixed)
    mine, other, attn_grads = attn_backward(d_pieces, attn_w, cosines, sines, saved, head)
    attn_grads = attn_grads.reshape(32, -1, attn_grads.shape[1])
    h = lax.all_to_all(attn_grads, ("z", "y", "c"), split_axis=0, concat_axis=0, tiled=True)
    parts = chip_parts(mine, swap_core(after(other, *out_got)))
    got = send_parts(parts)
    mlp_grad = after(mlp_grad, parts[1])

    by_x, came = unspread_x(mlp_grad, a)
    g = unspread_core(by_x, came, a, c)
    gate_grad, up_grad, down_grad = (columns_of(g, i * ff, ff) for i in range(3))
    arrays = [resid, out_parts[0], *after(out_got, parts[1])]
    (layer_output,) = finish(layer_output_kernel, arrays, [BF])
    arrays = [d_resid, x_own, parts[0], *after(got, came)]
    (input_grad,) = finish(input_grad_kernel, arrays, [F32])
    along = lambda w, grad: jnp.sum(w.astype(F32) * grad, axis=1)
    mlp_gain_grad = along(w_gate, gate_grad) + along(w_up, up_grad)
    gate_grad, up_grad = gate_grad * gain_m, up_grad * gain_m
    h = h.reshape(16, 2, 2, -1, h.shape[2])
    h = jnp.sum(h.astype(F32), axis=0)
    first = a == 0
    keep = jnp.where(first, h[:, 0], h[:, 1])
    give = jnp.where(first, h[:, 1], h[:, 0]).astype(BF)
    came = lax.ppermute(after(give, came, input_grad), "a", SWAP).astype(F32)
    h = [*jnp.where(first, keep, came), *jnp.where(first, came, keep)]
    query_grad = columns_of(h, 0, nq)
    key_grad = columns_of(h, nq, nk)
    value_grad = columns_of(h, nq + nk, nk)
    out_grad = columns_of(h, cut, nq).T
    attn_gain_grad = along(w_query, query_grad) + along(w_key, key_grad)
    attn_gain_grad = attn_gain_grad + along(w_value, value_grad)
    query_grad, key_grad, value_grad = (v * gain_a for v in (query_grad, key_grad, value_grad))
    gain_grads = jnp.stack([attn_gain_grad, mlp_gain_grad])
    gain_grads = gain_grads + lax.ppermute(gain_grads, "t", SWAP)
    return (
        layer_output, input_grad, gain_grads[0], query_grad, key_grad, value_grad, out_grad,
        gain_grads[1], gate_grad, up_grad, down_grad.T,
    )


def solution(mesh):
    fine = Mesh(mesh.devices.reshape(2, 4, 4, 2, 2), ("a", "z", "y", "c", "t"))
    dp = ("a", "z", "y", "c")
    rows = P(dp + ("t",), None)
    return jax.shard_map(
        local,
        mesh=fine,
        in_specs=(
            rows, P(dp), P(dp), P(dp, "t"), P(dp, "t"), P(dp, "t"), P("t", dp),
            P(dp), P(dp, "t"), P(dp, "t"), P("t", dp), rows,
        ),
        out_specs=(
            rows, rows, P(dp), P(dp, "t"), P(dp, "t"), P(dp, "t"), P("t", dp),
            P(dp), P(dp, "t"), P(dp, "t"), P("t", dp),
        ),
        check_vma=False,
    )
```

```python
import math

import jax
import jax.numpy as jnp
from jax import lax
from jax.experimental import pallas as pl
from jax.experimental.pallas import tpu as pltpu
from jax.sharding import Mesh
from jax.sharding import PartitionSpec as P

HEADS = 32
KV_HEADS = 8
GROUP = HEADS // KV_HEADS
EPSILON = 1e-05
ROPE_BASE = 500000.0
MASKED = -1e30
VMEM_LIMIT = 56 * 2**20
BF = jnp.bfloat16
F32 = jnp.float32


def cost(micros):
    return pl.CostEstimate(flops=micros * 10**9, bytes_accessed=2**20, transcendentals=0)


SWAP = [(0, 1), (1, 0)]


def mm(left, right):
    return jnp.dot(left, right, preferred_element_type=F32)


def mm_nt(left, right):
    return lax.dot_general(left, right, (((1,), (1,)), ((), ())), preferred_element_type=F32)


def mm_tn(left, right):
    return lax.dot_general(left, right, (((0,), (0,)), ((), ())), preferred_element_type=F32)


AT = (0, 2, 1, 3)


def from_chip(value, k):
    return lax.ppermute(value, ("a", "t"), [(AT[(i + k) % 4], AT[i]) for i in range(4)])


def to_chip(value, k):
    return lax.ppermute(value, ("a", "t"), [(AT[i], AT[(i + k) % 4]) for i in range(4)])


def after(value, *others):
    return lax.optimization_barrier((value, *others))[0]


def swap_core(value):
    return lax.ppermute(value, "c", SWAP)


def gather_rows(rows):
    mine = [rows, from_chip(rows, 2), from_chip(rows, 1), from_chip(rows, 3)]
    return mine + [swap_core(piece) for piece in mine]


def chip_parts(mine, got):
    rows = mine.shape[0] // 4
    parts = [
        mine[i * rows : (i + 1) * rows].astype(F32) + got[i * rows : (i + 1) * rows].astype(F32)
        for i in range(4)
    ]
    return [parts[0]] + [part.astype(BF) for part in parts[1:]]


def send_parts(parts):
    return [to_chip(part, k) for part, k in zip(parts[1:], (2, 1, 3))]


def total_of(parts, got):
    total = parts[0]
    for part in got:
        total = total + part.astype(F32)
    return total


def split_quarters(quarters, c):
    first = c == 0
    keep = [jnp.where(first, quarters[2 * i], quarters[2 * i + 1]) for i in range(2)]
    give = [jnp.where(first, quarters[2 * i + 1], quarters[2 * i]) for i in range(2)]
    return jnp.concatenate(keep, axis=0), jnp.concatenate(give, axis=0)


def spread(keep, give, a, c, wait=()):
    first = c == 0
    r = keep.shape[0] // 2
    got = swap_core(give)
    both = []
    for i in range(2):
        k, g = keep[i * r : (i + 1) * r], got[i * r : (i + 1) * r]
        both.append(jnp.concatenate([jnp.where(first, k, g), jnp.where(first, g, k)], axis=0))
    first_a = a == 0
    keep_a = jnp.where(first_a, both[0], both[1])
    give_a = jnp.where(first_a, both[1], both[0])
    got_a = lax.ppermute(after(give_a, *wait), "a", SWAP)
    rows = [jnp.where(first_a, keep_a, got_a), jnp.where(first_a, got_a, keep_a)]
    return jnp.concatenate(rows, axis=0), give_a


def unspread_x(rows, a):
    half = rows.shape[0] // 2
    first = a == 0
    give = jnp.where(first, rows[half:], rows[:half])
    return jnp.where(first, rows[:half], rows[half:]), lax.ppermute(give, "a", SWAP)


def unspread_core(mine, came, a, c):
    r = mine.shape[0] // 2
    first_a, first = a == 0, c == 0
    by_a = [jnp.where(first_a, mine, came), jnp.where(first_a, came, mine)]
    keep = [jnp.where(first, v[:r], v[r:]) for v in by_a]
    give = [jnp.where(first, v[r:], v[:r]) for v in by_a]
    got = swap_core(jnp.concatenate(give, axis=0))
    quarters = []
    for k, g in zip(keep, (got[:r], got[r:])):
        quarters += [jnp.where(first, k, g), jnp.where(first, g, k)]
    return quarters


def columns_of(quarters, start, width):
    return jnp.concatenate([q[:, start : start + width] for q in quarters], axis=1).astype(F32)


def to_place(rows):
    n, d = rows.shape
    return rows.reshape(n, 2, 16, d // 32).transpose(0, 2, 1, 3).reshape(n, d)


def norm_factor(values):
    return lax.rsqrt(jnp.mean(values * values, axis=-1, keepdims=True) + EPSILON)


def norm_back(values, upstream):
    factor = norm_factor(values)
    rescaled = values * factor
    return factor * (upstream - rescaled * jnp.mean(upstream * rescaled, axis=-1, keepdims=True))


def step_block(s):
    return (s + 2) % 4


def row_block(width):
    return lambda rows: pl.BlockSpec((rows, width), lambda s: (step_block(s), 0))


def fixed(shape):
    return pl.BlockSpec(shape, lambda *_: (0,) * len(shape))


def halves(rows, width):
    return [
        pl.BlockSpec((rows, width), lambda s: (jnp.maximum(s - 2, 0), 0)),
        pl.BlockSpec((rows, width), lambda s: (jnp.minimum(s, 1), 0)),
    ]


def load_block(s, pieces, scratch):
    part = pieces[0].shape[0]
    for b in range(4):

        @pl.when(step_block(s) == b)
        def _():
            scratch[:part] = pieces[2 * b][...]
            scratch[part:] = pieces[2 * b + 1][...]


def store_half(s, mine_ref, other_ref, value):
    @pl.when(s < 2)
    def _():
        other_ref[...] = value

    @pl.when(s >= 2)
    def _():
        mine_ref[...] = value


def turn(values, cosines, sines, head):
    width = values.shape[1]
    lane = lax.broadcasted_iota(jnp.int32, values.shape, 1)
    low = lane % head < head // 2
    partner = jnp.where(
        low, pltpu.roll(values, width - head // 2, 1), pltpu.roll(values, head // 2, 1)
    )
    return values * cosines + partner * sines


def double(values, times):
    return jnp.concatenate([values] * times, axis=1)


def by_head(values, head):
    lane = lax.broadcasted_iota(jnp.int32, values.shape, 1) // head
    zero = jnp.zeros_like(values)
    return jnp.concatenate([jnp.where(lane == h, values, zero) for h in range(GROUP)], axis=0)


def take_heads(values, rows, head):
    lane = lax.broadcasted_iota(jnp.int32, (rows, values.shape[1]), 1) // head
    out = values[:rows]
    for h in range(1, GROUP):
        out = jnp.where(lane == h, values[h * rows : (h + 1) * rows], out)
    return out


def fold_heads(values, head):
    pair = values[:, : 2 * head] + values[:, 2 * head :]
    return pair + pltpu.roll(pair, head, 1)


def pack_kernel(place_ref, gain_ref, wq_ref, wk_ref, wv_ref, wo_ref, *out_refs):
    r, wide = wq_ref.shape[0], wq_ref.shape[1] // 4
    head = wk_ref.shape[1] // 4
    row = jnp.broadcast_to(gain_ref[...].astype(F32), (8, r))
    row = jnp.where(lax.broadcasted_iota(jnp.int32, row.shape, 0) == 0, row, 0.0).astype(BF)
    gain = mm_tn(row, jnp.ones((8, 2 * head), BF))
    queries = (wq_ref[...].astype(F32) * double(gain, wq_ref.shape[1] // (2 * head))).astype(BF)
    keys = wk_ref[...].astype(F32) * double(gain, 2)
    values = wv_ref[...].astype(F32) * double(gain, 2)
    low = lax.broadcasted_iota(jnp.int32, (r, 2 * head), 1) < head

    def fill(ref, q):
        columns = slice(q * wide, (q + 1) * wide)
        pair = slice(q // 2 * 2 * head, (q // 2 + 1) * 2 * head)
        key, value = keys[:, pair], values[:, pair]
        if q % 2:
            key = pltpu.roll(key, head, 1)
        else:
            value = pltpu.roll(value, head, 1)
        ref[:, :wide] = queries[:, columns]
        ref[:, wide : wide + 2 * head] = jnp.where(low, key, value).astype(BF)
        ref[:, wide + 2 * head :] = wo_ref[:, columns]

    for own in range(4):

        @pl.when(place_ref[0] == own)
        def _():
            for other in range(4):
                fill(out_refs[other], own ^ other)


def pack_attn(place, gain, w_query, w_key, w_value, w_out_t):
    r, columns = w_query.shape
    shape = jax.ShapeDtypeStruct((r, columns // 4 + w_key.shape[1] // 2 + columns // 4), BF)
    vmem = pl.BlockSpec(memory_space=pltpu.VMEM)
    return pl.pallas_call(
        pack_kernel,
        in_specs=[pl.BlockSpec(memory_space=pltpu.SMEM)] + [vmem] * 5,
        out_specs=[vmem] * 4,
        out_shape=[shape] * 4,
        cost_estimate=cost(2),
    )(place.reshape(1).astype(jnp.int32), gain, w_query, w_key, w_value, w_out_t)


def attn_forward_kernel(head, *refs):
    pieces = refs[:8]
    (w_ref, cos_ref, sin_ref, mask_ref,
     mine_ref, other_ref, normed_ref, q_ref, k_ref, v_ref, probs_ref, mixed_ref,
     x_ref) = refs[8:]
    s = pl.program_id(0)
    nq, cut = GROUP * head, (GROUP + 2) * head
    rows = x_ref.shape[0]

    load_block(s, pieces, x_ref)
    x = x_ref[...].astype(F32)
    factor = lax.rsqrt(jnp.mean(x * x, axis=-1, keepdims=True) + EPSILON)
    normed = (x * factor).astype(BF)
    normed_ref[...] = normed
    qkv = mm(normed, w_ref[:, :cut])
    cosines, sines = cos_ref[...], sin_ref[...]
    query = turn(qkv[:, :nq], double(cosines, 2), double(sines, 2), head).astype(BF)
    kv = qkv[:, nq:]
    turned = turn(kv, cosines, sines, head)
    low = lax.broadcasted_iota(jnp.int32, kv.shape, 1) < head
    key = double(jnp.where(low, turned, pltpu.roll(turned, head, 1)), 2).astype(BF)
    value = double(jnp.where(low, pltpu.roll(kv, head, 1), kv), 2).astype(BF)
    q_ref[...] = query
    k_ref[...] = key
    v_ref[...] = value
    scores = mm_nt(by_head(query, head), key) * (1.0 / math.sqrt(head))
    allowed = mask_ref[...] == 0
    scores = jnp.where(jnp.concatenate([allowed] * GROUP, axis=0), scores, MASKED)
    weights = jnp.exp(scores - jnp.max(scores, axis=-1, keepdims=True))
    probs = weights / jnp.sum(weights, axis=-1, keepdims=True)
    probs_ref[...] = probs
    mixed = take_heads(mm(probs.astype(BF), value), rows, head).astype(BF)
    mixed_ref[...] = mixed
    store_half(s, mine_ref, other_ref, mm_nt(mixed, w_ref[:, cut : cut + nq]).astype(BF))


def attn_forward(pieces, w, cosines, sines, mask, head):
    part, d = pieces[0].shape
    rows = 2 * part
    nq = GROUP * head
    spec = lambda width: row_block(width)(rows)
    return pl.pallas_call(
        lambda *refs: attn_forward_kernel(head, *refs),
        grid=(4,),
        in_specs=[fixed(p.shape) for p in pieces]
        + [fixed(w.shape), spec(2 * head), spec(2 * head), spec(rows)],
        out_specs=halves(rows, d)
        + [spec(d), spec(nq), spec(nq), spec(nq)]
        + [pl.BlockSpec((GROUP * rows, rows), lambda s: (step_block(s), 0)), spec(nq)],
        out_shape=[jax.ShapeDtypeStruct((2 * rows, d), BF)] * 2
        + [jax.ShapeDtypeStruct((4 * rows, d), BF)]
        + [jax.ShapeDtypeStruct((4 * rows, nq), BF)] * 3
        + [
            jax.ShapeDtypeStruct((4 * GROUP * rows, rows), F32),
            jax.ShapeDtypeStruct((4 * rows, nq), BF),
        ],
        scratch_shapes=[pltpu.VMEM((rows, d), BF)],
        compiler_params=pltpu.CompilerParams(vmem_limit_bytes=VMEM_LIMIT),
        cost_estimate=cost(30),
    )(*pieces, w, cosines, sines, mask)


def attn_backward_kernel(head, *refs):
    d_pieces = refs[:8]
    (w_ref, cos_ref, sin_ref, normed_ref, q_ref, k_ref, v_ref, probs_ref, mixed_ref,
     mine_ref, other_ref, grad_ref, d_scr, n_scr, qkv_scr) = refs[8:]
    s = pl.program_id(0)
    nq, cut = GROUP * head, (GROUP + 2) * head
    part = d_pieces[0].shape[0]
    rows = 2 * part
    scale = 1.0 / math.sqrt(head)

    @pl.when(s == 0)
    def _():
        for i in range(8):
            d_scr[i * part : (i + 1) * part] = d_pieces[i][...]

    here = pl.ds(pl.multiple_of(step_block(s) * rows, rows), rows)
    n_scr[here] = normed_ref[...]
    d_branch = d_scr[here]
    d_mixed = by_head(mm(d_branch, w_ref[:, cut : cut + nq]).astype(BF), head)
    d_probs = mm_nt(d_mixed, v_ref[...])
    probs = probs_ref[...]
    d_value = fold_heads(mm_tn(probs.astype(BF), d_mixed), head)
    d_scores = probs * (d_probs - jnp.sum(d_probs * probs, axis=-1, keepdims=True))
    d_scores = d_scores.astype(BF)
    d_query = take_heads(mm(d_scores, k_ref[...]), rows, head) * scale
    d_key = fold_heads(mm_tn(d_scores, by_head(q_ref[...], head)), head) * scale
    cosines, sines = cos_ref[...], -sin_ref[...]
    d_query = turn(d_query, double(cosines, 2), double(sines, 2), head).astype(BF)
    d_key = turn(d_key, cosines, sines, head)
    low = lax.broadcasted_iota(jnp.int32, d_key.shape, 1) < head
    d_kv = jnp.where(low, d_key, d_value).astype(BF)
    d_qkv = jnp.concatenate([d_query, d_kv], axis=1)
    qkv_scr[here] = d_qkv
    d_normed = mm_nt(d_qkv, w_ref[:, :cut])
    store_half(s, mine_ref, other_ref, d_normed.astype(BF))

    @pl.when(s == 3)
    def _():
        def put(value, start):
            size = value.shape[0] // 64
            for zy in range(16):
                for k, old in enumerate((0, 2, 1, 3)):
                    to, at = (zy * 4 + k) * size, (zy * 4 + old) * size
                    grad_ref[to : to + size, start : start + value.shape[1]] = value[at : at + size]

        put(mm_tn(n_scr[...], qkv_scr[...]).astype(BF), 0)
        put(mm_tn(d_scr[...], mixed_ref[...]).astype(BF), cut)


def attn_backward(d_pieces, w, cosines, sines, saved, head):
    normed, query, key, value, probs, mixed = saved
    part, d = d_pieces[0].shape
    rows = 2 * part
    nq, cut = GROUP * head, (GROUP + 2) * head
    wide = cut + nq
    spec = lambda width: row_block(width)(rows)
    return pl.pallas_call(
        lambda *refs: attn_backward_kernel(head, *refs),
        grid=(4,),
        in_specs=[fixed(p.shape) for p in d_pieces]
        + [fixed(w.shape), spec(2 * head), spec(2 * head), spec(d)]
        + [spec(nq), spec(nq), spec(nq)]
        + [pl.BlockSpec((GROUP * rows, rows), lambda s: (step_block(s), 0)), fixed(mixed.shape)],
        out_specs=halves(rows, d) + [fixed((d, wide))],
        out_shape=[jax.ShapeDtypeStruct((2 * rows, d), BF)] * 2
        + [jax.ShapeDtypeStruct((d, wide), BF)],
        scratch_shapes=[
            pltpu.VMEM((4 * rows, d), BF),
            pltpu.VMEM((4 * rows, d), BF),
            pltpu.VMEM((4 * rows, cut), BF),
        ],
        compiler_params=pltpu.CompilerParams(vmem_limit_bytes=VMEM_LIMIT),
        cost_estimate=cost(10),
    )(*d_pieces, w, cosines, sines, normed, query, key, value, probs, mixed)


def mlp_kernel(*refs):
    n_pieces, c_pieces = refs[:8], refs[8:16]
    (wg_ref, wu_ref, wd_ref, dg_ref, du_ref, hid_ref, mine_ref, other_ref,
     n_scr, c_scr, w_scr, d_scr) = refs[16:]
    j = pl.program_id(0)
    part = n_pieces[0].shape[0]
    tile = wg_ref.shape[1]
    ff = 4 * tile

    @pl.when(j == 0)
    def _():
        for i in range(8):
            n_scr[i * part : (i + 1) * part] = n_pieces[i][...]
            c_scr[i * part : (i + 1) * part] = c_pieces[i][...]

    for step in range(4):

        @pl.when(j == step)
        def _():
            w_scr[:, step * tile : (step + 1) * tile] = wg_ref[...]
            w_scr[:, ff + step * tile : ff + (step + 1) * tile] = wu_ref[...]
            gate = mm(n_scr[...], wg_ref[...])
            up = mm(n_scr[...], wu_ref[...])
            d_hidden = mm(c_scr[...], wd_ref[...])
            sig = jax.nn.sigmoid(gate)
            silu = gate * sig
            hid_ref[...] = (silu * up).astype(BF)
            d_gate = (d_hidden * up * sig * (1.0 + gate * (1.0 - sig))).astype(BF)
            d_up = (d_hidden * silu).astype(BF)
            dg_ref[...] = d_gate
            du_ref[...] = d_up
            d_scr[:, step * tile : (step + 1) * tile] = d_gate
            d_scr[:, ff + step * tile : ff + (step + 1) * tile] = d_up

    @pl.when(j >= 4)
    def _():
        wide = mine_ref.shape[1]
        rows = pl.ds(pl.multiple_of((j - 4) * wide, wide), wide)
        d_n2 = mm_nt(d_scr[...], w_scr[rows, :]).astype(BF)
        mine_ref[...] = d_n2[: 4 * part]
        other_ref[...] = d_n2[4 * part :]


def mlp(n_pieces, c_pieces, w):
    part, d = n_pieces[0].shape
    rows, ff = 8 * part, w.shape[1] // 3
    tile, wide = ff // 4, d // 4
    at = lambda k: pl.BlockSpec((d, tile), lambda j: (0, 4 * k + jnp.minimum(j, 3)))
    return pl.pallas_call(
        mlp_kernel,
        grid=(8,),
        in_specs=[fixed((part, d))] * 16 + [at(0), at(1), at(2)],
        out_specs=[pl.BlockSpec((rows, tile), lambda j: (0, jnp.minimum(j, 3)))] * 3
        + [pl.BlockSpec((rows // 2, wide), lambda j: (0, jnp.maximum(j - 4, 0)))] * 2,
        out_shape=[jax.ShapeDtypeStruct((rows, ff), BF)] * 3
        + [jax.ShapeDtypeStruct((rows // 2, d), BF)] * 2,
        scratch_shapes=[
            pltpu.VMEM((rows, d), BF),
            pltpu.VMEM((rows, d), BF),
            pltpu.VMEM((d, 2 * ff), BF),
            pltpu.VMEM((rows, 2 * ff), BF),
        ],
        compiler_params=pltpu.CompilerParams(vmem_limit_bytes=VMEM_LIMIT),
        cost_estimate=cost(40),
    )(*n_pieces, *c_pieces, w, w, w)


def mlp_grads_kernel(*refs):
    n_pieces, c_pieces = refs[:8], refs[8:16]
    dg_ref, du_ref, hid_ref, g_ref = refs[16:]
    ff = dg_ref.shape[1]
    n_part = jnp.concatenate([piece[...] for piece in n_pieces], axis=0).T
    c_part = jnp.concatenate([piece[...] for piece in c_pieces], axis=0).T
    g_ref[:, :ff] = mm(n_part, dg_ref[...]).astype(BF)
    g_ref[:, ff : 2 * ff] = mm(n_part, du_ref[...]).astype(BF)
    g_ref[:, 2 * ff :] = mm(c_part, hid_ref[...]).astype(BF)


def mlp_grads(n_pieces, c_pieces, d_gate, d_up, hidden):
    part, d = n_pieces[0].shape
    rows, ff = hidden.shape
    wide = d // 8
    return pl.pallas_call(
        mlp_grads_kernel,
        grid=(8,),
        in_specs=[pl.BlockSpec((part, wide), lambda j: (0, j))] * 16 + [fixed((rows, ff))] * 3,
        out_specs=pl.BlockSpec((wide, 3 * ff), lambda j: (j, 0)),
        out_shape=jax.ShapeDtypeStruct((d, 3 * ff), BF),
        compiler_params=pltpu.CompilerParams(vmem_limit_bytes=VMEM_LIMIT),
        cost_estimate=cost(40),
    )(*n_pieces, *c_pieces, d_gate, d_up, hidden)


def mlp_out_kernel(x_ref, w_ref, mine_ref, other_ref):
    half = x_ref.shape[0] // 2
    out = mm_nt(x_ref[...], w_ref[...]).astype(BF)
    mine_ref[...] = out[:half]
    other_ref[...] = out[half:]


def mlp_out(hid, w):
    rows, ff = hid.shape
    d = w.shape[0]
    wide = d // 4
    return pl.pallas_call(
        mlp_out_kernel,
        grid=(4,),
        in_specs=[fixed((rows, ff)), pl.BlockSpec((wide, ff), lambda j: (j, 2))],
        out_specs=[pl.BlockSpec((rows // 2, wide), lambda j: (0, j))] * 2,
        out_shape=[jax.ShapeDtypeStruct((rows // 2, d), BF)] * 2,
        compiler_params=pltpu.CompilerParams(vmem_limit_bytes=VMEM_LIMIT),
        cost_estimate=cost(5),
    )(hid, w)


def store_placed(ref, value):
    tile = value.shape[1] // 16
    half = tile // 2
    low = lax.broadcasted_iota(jnp.int32, (value.shape[0], tile), 1) < half
    for i in range(8):
        even = value[:, 2 * i * tile : (2 * i + 1) * tile]
        odd = value[:, (2 * i + 1) * tile : (2 * i + 2) * tile]
        first = jnp.where(low, even, pltpu.roll(odd, half, 1))
        second = jnp.where(low, pltpu.roll(even, half, 1), odd)
        ref[:, i * tile : (i + 1) * tile] = first.astype(ref.dtype)
        ref[:, (8 + i) * tile : (9 + i) * tile] = second.astype(ref.dtype)


def d_resid_kernel(c_ref, resid_ref, own_ref, g2_ref, g1_ref, g3_ref, out_ref, low_ref):
    d_normed = total_of([own_ref[...]], [g2_ref[...], g1_ref[...], g3_ref[...]])
    out = c_ref[...].astype(F32) + norm_back(resid_ref[...], d_normed)
    out_ref[...] = out
    low_ref[...] = out.astype(BF)


def layer_output_kernel(resid_ref, own_ref, g2_ref, g1_ref, g3_ref, out_ref):
    total = total_of([own_ref[...]], [g2_ref[...], g1_ref[...], g3_ref[...]])
    store_placed(out_ref, resid_ref[...] + total)


def input_grad_kernel(d_resid_ref, x_ref, own_ref, g2_ref, g1_ref, g3_ref, out_ref):
    d_normed = total_of([own_ref[...]], [g2_ref[...], g1_ref[...], g3_ref[...]])
    back = norm_back(x_ref[...].astype(F32), d_normed)
    store_placed(out_ref, d_resid_ref[...] + back)


def finish(kernel, arrays, dtypes):
    shape = arrays[0].shape
    return pl.pallas_call(
        kernel,
        grid=(1,),
        in_specs=[fixed(shape)] * len(arrays),
        out_specs=[fixed(shape) for _ in dtypes],
        out_shape=[jax.ShapeDtypeStruct(shape, dtype) for dtype in dtypes],
        compiler_params=pltpu.CompilerParams(vmem_limit_bytes=VMEM_LIMIT),
        cost_estimate=cost(2),
    )(*arrays)


def token_tables(seg, shift, own, head):
    count, block = seg.shape
    seg = jnp.where(shift == 0, seg, jnp.roll(seg, own, axis=1))
    order = (jnp.arange(block, dtype=jnp.int32)[None, :] + shift * own) % block
    earlier = jnp.sum((seg[:, None, :] < seg[:, :, None]).astype(jnp.int32), axis=2)
    positions = (order - earlier).reshape(count * block, 1)
    allowed = (seg[:, :, None] == seg[:, None, :]) & (order[:, None, :] <= order[:, :, None])
    mask = jnp.where(allowed, 0.0, MASKED).astype(F32).reshape(count * block, block)
    lane = jnp.arange(2 * head)
    frequency = jnp.exp(-math.log(ROPE_BASE) * ((lane % (head // 2)).astype(F32) / (head // 2)))
    angles = positions.astype(F32) * frequency
    sines = jnp.where(lane % head < head // 2, -1.0, 1.0) * jnp.sin(angles)
    return jnp.cos(angles), sines, mask


def local(
    tokens, segment_ids, attn_gain, w_query, w_key, w_value, w_out,
    mlp_gain, w_gate, w_up, w_down, cotangent,
):
    a, c, t = lax.axis_index("a"), lax.axis_index("c"), lax.axis_index("t")
    own = tokens.shape[0]
    nq = w_query.shape[1] // 4
    nk = w_key.shape[1] // 4
    ff = w_gate.shape[1] // 4
    head = nk
    cut = nq + 2 * nk

    own_pack, by_core, by_x, by_both = pack_attn(
        2 * a + c, attn_gain[None], w_query, w_key, w_value, w_out.T
    )
    came = [
        own_pack,
        swap_core(by_core),
        lax.ppermute(by_x, "a", SWAP),
        lax.ppermute(by_both, ("a", "c"), [(i, 3 - i) for i in range(4)]),
    ]
    same_core = [jnp.where(c == 0, came[2 * i], came[2 * i + 1]) for i in range(2)]
    next_core = [jnp.where(c == 0, came[2 * i + 1], came[2 * i]) for i in range(2)]
    attn_rows = jnp.concatenate(
        [jnp.where(a == i, v[0], v[1]) for i in range(2) for v in (same_core, next_core)], axis=0
    )
    attn_w = lax.all_gather(attn_rows, ("z", "y"), axis=0, tiled=True)
    x_own, c_own = to_place(tokens), to_place(cotangent)
    x_pieces = gather_rows(after(x_own, own_pack))
    gain_a, gain_m = after((attn_gain, mlp_gain), own_pack)
    gain_a, gain_m = gain_a.astype(F32)[:, None], gain_m.astype(F32)[:, None]
    quarter = lambda w, i: w[:, i * w.shape[1] // 4 : (i + 1) * w.shape[1] // 4]
    scaled = [(w.astype(F32) * gain_m).astype(BF) for w in (w_gate, w_up)]
    mlp_pack = [
        jnp.concatenate([quarter(w, i) for w in (*scaled, w_down.T)], axis=1) for i in range(4)
    ]
    mlp_rows, _ = spread(*split_quarters(mlp_pack, c), a, c, x_pieces[1:4])
    mlp_w = lax.all_gather(mlp_rows, ("z", "y"), axis=0, tiled=True)
    c_pieces = gather_rows(after(c_own, *x_pieces[1:4]))

    seg = jnp.stack([segment_ids, lax.ppermute(segment_ids, "a", SWAP)])
    seg = jnp.concatenate([seg, swap_core(seg)], axis=0)
    shift = jnp.stack([t, t ^ a, t, t ^ a])[:, None]
    cosines, sines, mask = token_tables(seg, shift, own, head)

    forward = attn_forward(x_pieces, attn_w, cosines, sines, mask, head)
    mine, other, normed, query, key, value, probs, mixed = forward
    parts = chip_parts(mine, swap_core(after(other, *c_pieces[1:4])))
    resid = x_own.astype(F32) + total_of(parts, send_parts(parts))

    n_pieces = gather_rows((resid * norm_factor(resid)).astype(BF))
    d_gate, d_up, hidden, mine, other = mlp(n_pieces, c_pieces, mlp_w)
    swapped = swap_core(other)
    grads = mlp_grads(n_pieces, c_pieces, d_gate, d_up, hidden)
    mlp_grad = lax.psum_scatter(grads, ("z", "y"), scatter_dimension=0, tiled=True)
    parts = chip_parts(mine, after(swapped, grads))
    got = send_parts(parts)
    out_mine, out_other = mlp_out(after(hidden, parts[1]), mlp_w)
    got = after(got, out_mine)

    d_resid, d_branch = finish(d_resid_kernel, [c_own, resid, parts[0], *got], [F32, BF])
    d_chips = [from_chip(d_branch, k) for k in (2, 1, 3)]
    out_parts = chip_parts(out_mine, swap_core(after(out_other, d_branch)))
    d_chips = after(d_chips, out_parts[1])
    out_got = send_parts(out_parts)
    d_pieces = [d_branch, *d_chips]
    d_pieces += [swap_core(piece) for piece in d_pieces]
    saved = (normed, query, key, value, probs, mixed)
    mine, other, attn_grads = attn_backward(d_pieces, attn_w, cosines, sines, saved, head)
    attn_grads = attn_grads.reshape(32, -1, attn_grads.shape[1])
    h = lax.all_to_all(attn_grads, ("z", "y", "c"), split_axis=0, concat_axis=0, tiled=True)
    parts = chip_parts(mine, swap_core(after(other, *out_got)))
    got = send_parts(parts)
    mlp_grad = after(mlp_grad, parts[1])

    by_x, came = unspread_x(mlp_grad, a)
    g = unspread_core(by_x, came, a, c)
    gate_grad, up_grad, down_grad = (columns_of(g, i * ff, ff) for i in range(3))
    arrays = [resid, out_parts[0], *after(out_got, parts[1])]
    (layer_output,) = finish(layer_output_kernel, arrays, [BF])
    arrays = [d_resid, x_own, parts[0], *after(got, came)]
    (input_grad,) = finish(input_grad_kernel, arrays, [F32])
    along = lambda w, grad: jnp.sum(w.astype(F32) * grad, axis=1)
    mlp_gain_grad = along(w_gate, gate_grad) + along(w_up, up_grad)
    gate_grad, up_grad = gate_grad * gain_m, up_grad * gain_m
    h = h.reshape(16, 2, 2, -1, h.shape[2])
    h = jnp.sum(h.astype(F32), axis=0)
    first = a == 0
    keep = jnp.where(first, h[:, 0], h[:, 1])
    give = jnp.where(first, h[:, 1], h[:, 0]).astype(BF)
    came = lax.ppermute(after(give, came, input_grad), "a", SWAP).astype(F32)
    h = [*jnp.where(first, keep, came), *jnp.where(first, came, keep)]
    query_grad = columns_of(h, 0, nq)
    key_grad = columns_of(h, nq, nk)
    value_grad = columns_of(h, nq + nk, nk)
    out_grad = columns_of(h, cut, nq).T
    attn_gain_grad = along(w_query, query_grad) + along(w_key, key_grad)
    attn_gain_grad = attn_gain_grad + along(w_value, value_grad)
    query_grad, key_grad, value_grad = (v * gain_a for v in (query_grad, key_grad, value_grad))
    gain_grads = jnp.stack([attn_gain_grad, mlp_gain_grad])
    gain_grads = gain_grads + lax.ppermute(gain_grads, "t", SWAP)
    return (
        layer_output, input_grad, gain_grads[0], query_grad, key_grad, value_grad, out_grad,
        gain_grads[1], gate_grad, up_grad, down_grad.T,
    )


def solution(mesh):
    fine = Mesh(mesh.devices.reshape(2, 4, 4, 2, 2), ("a", "z", "y", "c", "t"))
    dp = ("a", "z", "y", "c")
    rows = P(dp + ("t",), None)
    return jax.shard_map(
        local,
        mesh=fine,
        in_specs=(
            rows, P(dp), P(dp), P(dp, "t"), P(dp, "t"), P(dp, "t"), P("t", dp),
            P(dp), P(dp, "t"), P(dp, "t"), P("t", dp), rows,
        ),
        out_specs=(
            rows, rows, P(dp), P(dp, "t"), P(dp, "t"), P(dp, "t"), P("t", dp),
            P(dp), P(dp, "t"), P(dp, "t"), P("t", dp),
        ),
        check_vma=False,
    )
```

```python
import math

import jax
import jax.numpy as jnp
from jax import lax
from jax.experimental import pallas as pl
from jax.experimental.pallas import tpu as pltpu
from jax.sharding import Mesh
from jax.sharding import PartitionSpec as P

HEADS = 32
KV_HEADS = 8
GROUP = HEADS // KV_HEADS
EPSILON = 1e-05
ROPE_BASE = 500000.0
MASKED = -1e30
VMEM_LIMIT = 56 * 2**20
BF = jnp.bfloat16
F32 = jnp.float32


def cost(micros):
    return pl.CostEstimate(flops=micros * 10**9, bytes_accessed=2**20, transcendentals=0)


SWAP = [(0, 1), (1, 0)]


def mm(left, right):
    return jnp.dot(left, right, preferred_element_type=F32)


def mm_nt(left, right):
    return lax.dot_general(left, right, (((1,), (1,)), ((), ())), preferred_element_type=F32)


def mm_tn(left, right):
    return lax.dot_general(left, right, (((0,), (0,)), ((), ())), preferred_element_type=F32)


AT = (0, 2, 1, 3)


def from_chip(value, k):
    return lax.ppermute(value, ("a", "t"), [(AT[(i + k) % 4], AT[i]) for i in range(4)])


def to_chip(value, k):
    return lax.ppermute(value, ("a", "t"), [(AT[i], AT[(i + k) % 4]) for i in range(4)])


def after(value, *others):
    return lax.optimization_barrier((value, *others))[0]


def swap_core(value):
    return lax.ppermute(value, "c", SWAP)


def gather_rows(rows):
    mine = [rows, from_chip(rows, 2), from_chip(rows, 1), from_chip(rows, 3)]
    return mine + [swap_core(piece) for piece in mine]


def chip_parts(mine, got):
    rows = mine.shape[0] // 4
    parts = [
        mine[i * rows : (i + 1) * rows].astype(F32) + got[i * rows : (i + 1) * rows].astype(F32)
        for i in range(4)
    ]
    return [parts[0]] + [part.astype(BF) for part in parts[1:]]


def send_parts(parts):
    return [to_chip(part, k) for part, k in zip(parts[1:], (2, 1, 3))]


def total_of(parts, got):
    total = parts[0]
    for part in got:
        total = total + part.astype(F32)
    return total


def split_quarters(quarters, c):
    first = c == 0
    keep = [jnp.where(first, quarters[2 * i], quarters[2 * i + 1]) for i in range(2)]
    give = [jnp.where(first, quarters[2 * i + 1], quarters[2 * i]) for i in range(2)]
    return jnp.concatenate(keep, axis=0), jnp.concatenate(give, axis=0)


def spread(keep, give, a, c, wait=()):
    first = c == 0
    r = keep.shape[0] // 2
    got = swap_core(give)
    both = []
    for i in range(2):
        k, g = keep[i * r : (i + 1) * r], got[i * r : (i + 1) * r]
        both.append(jnp.concatenate([jnp.where(first, k, g), jnp.where(first, g, k)], axis=0))
    first_a = a == 0
    keep_a = jnp.where(first_a, both[0], both[1])
    give_a = jnp.where(first_a, both[1], both[0])
    got_a = lax.ppermute(after(give_a, *wait), "a", SWAP)
    rows = [jnp.where(first_a, keep_a, got_a), jnp.where(first_a, got_a, keep_a)]
    return jnp.concatenate(rows, axis=0), give_a


def unspread_x(rows, a):
    half = rows.shape[0] // 2
    first = a == 0
    give = jnp.where(first, rows[half:], rows[:half])
    return jnp.where(first, rows[:half], rows[half:]), lax.ppermute(give, "a", SWAP)


def unspread_core(mine, came, a, c):
    r = mine.shape[0] // 2
    first_a, first = a == 0, c == 0
    by_a = [jnp.where(first_a, mine, came), jnp.where(first_a, came, mine)]
    keep = [jnp.where(first, v[:r], v[r:]) for v in by_a]
    give = [jnp.where(first, v[r:], v[:r]) for v in by_a]
    got = swap_core(jnp.concatenate(give, axis=0))
    quarters = []
    for k, g in zip(keep, (got[:r], got[r:])):
        quarters += [jnp.where(first, k, g), jnp.where(first, g, k)]
    return quarters, got


def columns_of(quarters, start, width):
    return jnp.concatenate([q[:, start : start + width] for q in quarters], axis=1).astype(F32)


def to_place(rows):
    n, d = rows.shape
    return rows.reshape(n, 2, 16, d // 32).transpose(0, 2, 1, 3).reshape(n, d)


def norm_factor(values):
    return lax.rsqrt(jnp.mean(values * values, axis=-1, keepdims=True) + EPSILON)


def norm_back(values, upstream):
    factor = norm_factor(values)
    rescaled = values * factor
    return factor * (upstream - rescaled * jnp.mean(upstream * rescaled, axis=-1, keepdims=True))


def step_block(s):
    return (s + 2) % 4


def row_block(width):
    return lambda rows: pl.BlockSpec((rows, width), lambda s: (step_block(s), 0))


def fixed(shape):
    return pl.BlockSpec(shape, lambda *_: (0,) * len(shape))


def halves(rows, width):
    return [
        pl.BlockSpec((rows, width), lambda s: (jnp.maximum(s - 2, 0), 0)),
        pl.BlockSpec((rows, width), lambda s: (jnp.minimum(s, 1), 0)),
    ]


def load_block(s, pieces, scratch):
    part = pieces[0].shape[0]
    for b in range(4):

        @pl.when(step_block(s) == b)
        def _():
            scratch[:part] = pieces[2 * b][...]
            scratch[part:] = pieces[2 * b + 1][...]


def store_half(s, mine_ref, other_ref, value):
    @pl.when(s < 2)
    def _():
        other_ref[...] = value

    @pl.when(s >= 2)
    def _():
        mine_ref[...] = value


def turn(values, cosines, sines, head):
    width = values.shape[1]
    lane = lax.broadcasted_iota(jnp.int32, values.shape, 1)
    low = lane % head < head // 2
    partner = jnp.where(
        low, pltpu.roll(values, width - head // 2, 1), pltpu.roll(values, head // 2, 1)
    )
    return values * cosines + partner * sines


def double(values, times):
    return jnp.concatenate([values] * times, axis=1)


def by_head(values, head):
    lane = lax.broadcasted_iota(jnp.int32, values.shape, 1) // head
    zero = jnp.zeros_like(values)
    return jnp.concatenate([jnp.where(lane == h, values, zero) for h in range(GROUP)], axis=0)


def take_heads(values, rows, head):
    lane = lax.broadcasted_iota(jnp.int32, (rows, values.shape[1]), 1) // head
    out = values[:rows]
    for h in range(1, GROUP):
        out = jnp.where(lane == h, values[h * rows : (h + 1) * rows], out)
    return out


def fold_heads(values, head):
    pair = values[:, : 2 * head] + values[:, 2 * head :]
    return pair + pltpu.roll(pair, head, 1)


def pack_kernel(place_ref, gain_ref, wq_ref, wk_ref, wv_ref, wo_ref, *out_refs):
    r, wide = wq_ref.shape[0], wq_ref.shape[1] // 4
    head = wk_ref.shape[1] // 4
    row = jnp.broadcast_to(gain_ref[...].astype(F32), (8, r))
    row = jnp.where(lax.broadcasted_iota(jnp.int32, row.shape, 0) == 0, row, 0.0).astype(BF)
    gain = mm_tn(row, jnp.ones((8, 2 * head), BF))
    queries = (wq_ref[...].astype(F32) * double(gain, wq_ref.shape[1] // (2 * head))).astype(BF)
    keys = wk_ref[...].astype(F32) * double(gain, 2)
    values = wv_ref[...].astype(F32) * double(gain, 2)
    low = lax.broadcasted_iota(jnp.int32, (r, 2 * head), 1) < head

    def fill(ref, q):
        columns = slice(q * wide, (q + 1) * wide)
        pair = slice(q // 2 * 2 * head, (q // 2 + 1) * 2 * head)
        key, value = keys[:, pair], values[:, pair]
        if q % 2:
            key = pltpu.roll(key, head, 1)
        else:
            value = pltpu.roll(value, head, 1)
        ref[:, :wide] = queries[:, columns]
        ref[:, wide : wide + 2 * head] = jnp.where(low, key, value).astype(BF)
        ref[:, wide + 2 * head :] = wo_ref[:, columns]

    for own in range(4):

        @pl.when(place_ref[0] == own)
        def _():
            for other in range(4):
                fill(out_refs[other], own ^ other)


def pack_attn(place, gain, w_query, w_key, w_value, w_out_t):
    r, columns = w_query.shape
    shape = jax.ShapeDtypeStruct((r, columns // 4 + w_key.shape[1] // 2 + columns // 4), BF)
    vmem = pl.BlockSpec(memory_space=pltpu.VMEM)
    return pl.pallas_call(
        pack_kernel,
        in_specs=[pl.BlockSpec(memory_space=pltpu.SMEM)] + [vmem] * 5,
        out_specs=[vmem] * 4,
        out_shape=[shape] * 4,
        cost_estimate=cost(2),
    )(place.reshape(1).astype(jnp.int32), gain, w_query, w_key, w_value, w_out_t)


def attn_forward_kernel(head, *refs):
    pieces = refs[:8]
    (w_ref, cos_ref, sin_ref, mask_ref,
     mine_ref, other_ref, normed_ref, q_ref, k_ref, v_ref, probs_ref, mixed_ref,
     x_ref) = refs[8:]
    s = pl.program_id(0)
    nq, cut = GROUP * head, (GROUP + 2) * head
    rows = x_ref.shape[0]

    load_block(s, pieces, x_ref)
    x = x_ref[...].astype(F32)
    factor = lax.rsqrt(jnp.mean(x * x, axis=-1, keepdims=True) + EPSILON)
    normed = (x * factor).astype(BF)
    normed_ref[...] = normed
    qkv = mm(normed, w_ref[:, :cut])
    cosines, sines = cos_ref[...], sin_ref[...]
    query = turn(qkv[:, :nq], double(cosines, 2), double(sines, 2), head).astype(BF)
    kv = qkv[:, nq:]
    turned = turn(kv, cosines, sines, head)
    low = lax.broadcasted_iota(jnp.int32, kv.shape, 1) < head
    key = double(jnp.where(low, turned, pltpu.roll(turned, head, 1)), 2).astype(BF)
    value = double(jnp.where(low, pltpu.roll(kv, head, 1), kv), 2).astype(BF)
    q_ref[...] = query
    k_ref[...] = key
    v_ref[...] = value
    scores = mm_nt(by_head(query, head), key) * (1.0 / math.sqrt(head))
    allowed = mask_ref[...] == 0
    scores = jnp.where(jnp.concatenate([allowed] * GROUP, axis=0), scores, MASKED)
    weights = jnp.exp(scores - jnp.max(scores, axis=-1, keepdims=True))
    probs = weights / jnp.sum(weights, axis=-1, keepdims=True)
    probs_ref[...] = probs
    mixed = take_heads(mm(probs.astype(BF), value), rows, head).astype(BF)
    mixed_ref[...] = mixed
    store_half(s, mine_ref, other_ref, mm_nt(mixed, w_ref[:, cut : cut + nq]).astype(BF))


def attn_forward(pieces, w, cosines, sines, mask, head):
    part, d = pieces[0].shape
    rows = 2 * part
    nq = GROUP * head
    spec = lambda width: row_block(width)(rows)
    return pl.pallas_call(
        lambda *refs: attn_forward_kernel(head, *refs),
        grid=(4,),
        in_specs=[fixed(p.shape) for p in pieces]
        + [fixed(w.shape), spec(2 * head), spec(2 * head), spec(rows)],
        out_specs=halves(rows, d)
        + [spec(d), spec(nq), spec(nq), spec(nq)]
        + [pl.BlockSpec((GROUP * rows, rows), lambda s: (step_block(s), 0)), spec(nq)],
        out_shape=[jax.ShapeDtypeStruct((2 * rows, d), BF)] * 2
        + [jax.ShapeDtypeStruct((4 * rows, d), BF)]
        + [jax.ShapeDtypeStruct((4 * rows, nq), BF)] * 3
        + [
            jax.ShapeDtypeStruct((4 * GROUP * rows, rows), F32),
            jax.ShapeDtypeStruct((4 * rows, nq), BF),
        ],
        scratch_shapes=[pltpu.VMEM((rows, d), BF)],
        compiler_params=pltpu.CompilerParams(vmem_limit_bytes=VMEM_LIMIT),
        cost_estimate=cost(30),
    )(*pieces, w, cosines, sines, mask)


def attn_backward_kernel(head, *refs):
    d_pieces = refs[:8]
    (w_ref, cos_ref, sin_ref, normed_ref, q_ref, k_ref, v_ref, probs_ref, mixed_ref,
     mine_ref, other_ref, grad_ref, d_scr, n_scr, qkv_scr) = refs[8:]
    s = pl.program_id(0)
    nq, cut = GROUP * head, (GROUP + 2) * head
    part = d_pieces[0].shape[0]
    rows = 2 * part
    scale = 1.0 / math.sqrt(head)

    @pl.when(s == 0)
    def _():
        for i in range(8):
            d_scr[i * part : (i + 1) * part] = d_pieces[i][...]

    here = pl.ds(pl.multiple_of(step_block(s) * rows, rows), rows)
    n_scr[here] = normed_ref[...]
    d_branch = d_scr[here]
    d_mixed = by_head(mm(d_branch, w_ref[:, cut : cut + nq]).astype(BF), head)
    d_probs = mm_nt(d_mixed, v_ref[...])
    probs = probs_ref[...]
    d_value = fold_heads(mm_tn(probs.astype(BF), d_mixed), head)
    d_scores = probs * (d_probs - jnp.sum(d_probs * probs, axis=-1, keepdims=True))
    d_scores = d_scores.astype(BF)
    d_query = take_heads(mm(d_scores, k_ref[...]), rows, head) * scale
    d_key = fold_heads(mm_tn(d_scores, by_head(q_ref[...], head)), head) * scale
    cosines, sines = cos_ref[...], -sin_ref[...]
    d_query = turn(d_query, double(cosines, 2), double(sines, 2), head).astype(BF)
    d_key = turn(d_key, cosines, sines, head)
    low = lax.broadcasted_iota(jnp.int32, d_key.shape, 1) < head
    d_kv = jnp.where(low, d_key, d_value).astype(BF)
    d_qkv = jnp.concatenate([d_query, d_kv], axis=1)
    qkv_scr[here] = d_qkv
    d_normed = mm_nt(d_qkv, w_ref[:, :cut])
    store_half(s, mine_ref, other_ref, d_normed.astype(BF))

    @pl.when(s == 3)
    def _():
        def put(value, start):
            size = value.shape[0] // 64
            for zy in range(16):
                for k, old in enumerate((0, 2, 1, 3)):
                    to, at = (zy * 4 + k) * size, (zy * 4 + old) * size
                    grad_ref[to : to + size, start : start + value.shape[1]] = value[at : at + size]

        put(mm_tn(n_scr[...], qkv_scr[...]).astype(BF), 0)
        put(mm_tn(d_scr[...], mixed_ref[...]).astype(BF), cut)


def attn_backward(d_pieces, w, cosines, sines, saved, head):
    normed, query, key, value, probs, mixed = saved
    part, d = d_pieces[0].shape
    rows = 2 * part
    nq, cut = GROUP * head, (GROUP + 2) * head
    wide = cut + nq
    spec = lambda width: row_block(width)(rows)
    return pl.pallas_call(
        lambda *refs: attn_backward_kernel(head, *refs),
        grid=(4,),
        in_specs=[fixed(p.shape) for p in d_pieces]
        + [fixed(w.shape), spec(2 * head), spec(2 * head), spec(d)]
        + [spec(nq), spec(nq), spec(nq)]
        + [pl.BlockSpec((GROUP * rows, rows), lambda s: (step_block(s), 0)), fixed(mixed.shape)],
        out_specs=halves(rows, d) + [fixed((d, wide))],
        out_shape=[jax.ShapeDtypeStruct((2 * rows, d), BF)] * 2
        + [jax.ShapeDtypeStruct((d, wide), BF)],
        scratch_shapes=[
            pltpu.VMEM((4 * rows, d), BF),
            pltpu.VMEM((4 * rows, d), BF),
            pltpu.VMEM((4 * rows, cut), BF),
        ],
        compiler_params=pltpu.CompilerParams(vmem_limit_bytes=VMEM_LIMIT),
        cost_estimate=cost(10),
    )(*d_pieces, w, cosines, sines, normed, query, key, value, probs, mixed)


def mlp_kernel(*refs):
    n_pieces, c_pieces = refs[:8], refs[8:16]
    (wg_ref, wu_ref, wd_ref, dg_ref, du_ref, hid_ref, mine_ref, other_ref,
     n_scr, c_scr, w_scr, d_scr) = refs[16:]
    j = pl.program_id(0)
    part = n_pieces[0].shape[0]
    tile = wg_ref.shape[1]
    ff = 4 * tile

    @pl.when(j == 0)
    def _():
        for i in range(8):
            n_scr[i * part : (i + 1) * part] = n_pieces[i][...]
            c_scr[i * part : (i + 1) * part] = c_pieces[i][...]

    for step in range(4):

        @pl.when(j == step)
        def _():
            w_scr[:, step * tile : (step + 1) * tile] = wg_ref[...]
            w_scr[:, ff + step * tile : ff + (step + 1) * tile] = wu_ref[...]
            gate = mm(n_scr[...], wg_ref[...])
            up = mm(n_scr[...], wu_ref[...])
            d_hidden = mm(c_scr[...], wd_ref[...])
            sig = jax.nn.sigmoid(gate)
            silu = gate * sig
            hid_ref[...] = (silu * up).astype(BF)
            d_gate = (d_hidden * up * sig * (1.0 + gate * (1.0 - sig))).astype(BF)
            d_up = (d_hidden * silu).astype(BF)
            dg_ref[...] = d_gate
            du_ref[...] = d_up
            d_scr[:, step * tile : (step + 1) * tile] = d_gate
            d_scr[:, ff + step * tile : ff + (step + 1) * tile] = d_up

    @pl.when(j >= 4)
    def _():
        wide = mine_ref.shape[1]
        rows = pl.ds(pl.multiple_of((j - 4) * wide, wide), wide)
        d_n2 = mm_nt(d_scr[...], w_scr[rows, :]).astype(BF)
        mine_ref[...] = d_n2[: 4 * part]
        other_ref[...] = d_n2[4 * part :]


def mlp(n_pieces, c_pieces, w):
    part, d = n_pieces[0].shape
    rows, ff = 8 * part, w.shape[1] // 3
    tile, wide = ff // 4, d // 4
    at = lambda k: pl.BlockSpec((d, tile), lambda j: (0, 4 * k + jnp.minimum(j, 3)))
    return pl.pallas_call(
        mlp_kernel,
        grid=(8,),
        in_specs=[fixed((part, d))] * 16 + [at(0), at(1), at(2)],
        out_specs=[pl.BlockSpec((rows, tile), lambda j: (0, jnp.minimum(j, 3)))] * 3
        + [pl.BlockSpec((rows // 2, wide), lambda j: (0, jnp.maximum(j - 4, 0)))] * 2,
        out_shape=[jax.ShapeDtypeStruct((rows, ff), BF)] * 3
        + [jax.ShapeDtypeStruct((rows // 2, d), BF)] * 2,
        scratch_shapes=[
            pltpu.VMEM((rows, d), BF),
            pltpu.VMEM((rows, d), BF),
            pltpu.VMEM((d, 2 * ff), BF),
            pltpu.VMEM((rows, 2 * ff), BF),
        ],
        compiler_params=pltpu.CompilerParams(vmem_limit_bytes=VMEM_LIMIT),
        cost_estimate=cost(40),
    )(*n_pieces, *c_pieces, w, w, w)


def mlp_grads_kernel(*refs):
    n_pieces, c_pieces = refs[:8], refs[8:16]
    dg_ref, du_ref, hid_ref, g_ref = refs[16:]
    ff = dg_ref.shape[1]
    n_part = jnp.concatenate([piece[...] for piece in n_pieces], axis=0).T
    c_part = jnp.concatenate([piece[...] for piece in c_pieces], axis=0).T
    g_ref[:, :ff] = mm(n_part, dg_ref[...]).astype(BF)
    g_ref[:, ff : 2 * ff] = mm(n_part, du_ref[...]).astype(BF)
    g_ref[:, 2 * ff :] = mm(c_part, hid_ref[...]).astype(BF)


def mlp_grads(n_pieces, c_pieces, d_gate, d_up, hidden):
    part, d = n_pieces[0].shape
    rows, ff = hidden.shape
    wide = d // 8
    return pl.pallas_call(
        mlp_grads_kernel,
        grid=(8,),
        in_specs=[pl.BlockSpec((part, wide), lambda j: (0, j))] * 16 + [fixed((rows, ff))] * 3,
        out_specs=pl.BlockSpec((wide, 3 * ff), lambda j: (j, 0)),
        out_shape=jax.ShapeDtypeStruct((d, 3 * ff), BF),
        compiler_params=pltpu.CompilerParams(vmem_limit_bytes=VMEM_LIMIT),
        cost_estimate=cost(40),
    )(*n_pieces, *c_pieces, d_gate, d_up, hidden)


def mlp_out_kernel(x_ref, w_ref, mine_ref, other_ref):
    half = x_ref.shape[0] // 2
    out = mm_nt(x_ref[...], w_ref[...]).astype(BF)
    mine_ref[...] = out[:half]
    other_ref[...] = out[half:]


def mlp_out(hid, w):
    rows, ff = hid.shape
    d = w.shape[0]
    wide = d // 4
    return pl.pallas_call(
        mlp_out_kernel,
        grid=(4,),
        in_specs=[fixed((rows, ff)), pl.BlockSpec((wide, ff), lambda j: (j, 2))],
        out_specs=[pl.BlockSpec((rows // 2, wide), lambda j: (0, j))] * 2,
        out_shape=[jax.ShapeDtypeStruct((rows // 2, d), BF)] * 2,
        compiler_params=pltpu.CompilerParams(vmem_limit_bytes=VMEM_LIMIT),
        cost_estimate=cost(5),
    )(hid, w)


def store_placed(ref, value):
    tile = value.shape[1] // 16
    half = tile // 2
    low = lax.broadcasted_iota(jnp.int32, (value.shape[0], tile), 1) < half
    for i in range(8):
        even = value[:, 2 * i * tile : (2 * i + 1) * tile]
        odd = value[:, (2 * i + 1) * tile : (2 * i + 2) * tile]
        first = jnp.where(low, even, pltpu.roll(odd, half, 1))
        second = jnp.where(low, pltpu.roll(even, half, 1), odd)
        ref[:, i * tile : (i + 1) * tile] = first.astype(ref.dtype)
        ref[:, (8 + i) * tile : (9 + i) * tile] = second.astype(ref.dtype)


def d_resid_kernel(c_ref, resid_ref, own_ref, g2_ref, g1_ref, g3_ref, out_ref, low_ref):
    d_normed = total_of([own_ref[...]], [g2_ref[...], g1_ref[...], g3_ref[...]])
    out = c_ref[...].astype(F32) + norm_back(resid_ref[...], d_normed)
    out_ref[...] = out
    low_ref[...] = out.astype(BF)


def layer_output_kernel(resid_ref, own_ref, g2_ref, g1_ref, g3_ref, out_ref):
    total = total_of([own_ref[...]], [g2_ref[...], g1_ref[...], g3_ref[...]])
    store_placed(out_ref, resid_ref[...] + total)


def input_grad_kernel(d_resid_ref, x_ref, own_ref, g2_ref, g1_ref, g3_ref, out_ref):
    d_normed = total_of([own_ref[...]], [g2_ref[...], g1_ref[...], g3_ref[...]])
    back = norm_back(x_ref[...].astype(F32), d_normed)
    store_placed(out_ref, d_resid_ref[...] + back)


def finish(kernel, arrays, dtypes):
    shape = arrays[0].shape
    return pl.pallas_call(
        kernel,
        grid=(1,),
        in_specs=[fixed(shape)] * len(arrays),
        out_specs=[fixed(shape) for _ in dtypes],
        out_shape=[jax.ShapeDtypeStruct(shape, dtype) for dtype in dtypes],
        compiler_params=pltpu.CompilerParams(vmem_limit_bytes=VMEM_LIMIT),
        cost_estimate=cost(2),
    )(*arrays)


def token_tables(seg, shift, own, head):
    count, block = seg.shape
    seg = jnp.where(shift == 0, seg, jnp.roll(seg, own, axis=1))
    order = (jnp.arange(block, dtype=jnp.int32)[None, :] + shift * own) % block
    earlier = jnp.sum((seg[:, None, :] < seg[:, :, None]).astype(jnp.int32), axis=2)
    positions = (order - earlier).reshape(count * block, 1)
    allowed = (seg[:, :, None] == seg[:, None, :]) & (order[:, None, :] <= order[:, :, None])
    mask = jnp.where(allowed, 0.0, MASKED).astype(F32).reshape(count * block, block)
    lane = jnp.arange(2 * head)
    frequency = jnp.exp(-math.log(ROPE_BASE) * ((lane % (head // 2)).astype(F32) / (head // 2)))
    angles = positions.astype(F32) * frequency
    sines = jnp.where(lane % head < head // 2, -1.0, 1.0) * jnp.sin(angles)
    return jnp.cos(angles), sines, mask


def local(
    tokens, segment_ids, attn_gain, w_query, w_key, w_value, w_out,
    mlp_gain, w_gate, w_up, w_down, cotangent,
):
    a, c, t = lax.axis_index("a"), lax.axis_index("c"), lax.axis_index("t")
    own = tokens.shape[0]
    nq = w_query.shape[1] // 4
    nk = w_key.shape[1] // 4
    ff = w_gate.shape[1] // 4
    head = nk
    cut = nq + 2 * nk

    own_pack, by_core, by_x, by_both = pack_attn(
        2 * a + c, attn_gain[None], w_query, w_key, w_value, w_out.T
    )
    came = [
        own_pack,
        swap_core(by_core),
        lax.ppermute(by_x, "a", SWAP),
        lax.ppermute(by_both, ("a", "c"), [(i, 3 - i) for i in range(4)]),
    ]
    same_core = [jnp.where(c == 0, came[2 * i], came[2 * i + 1]) for i in range(2)]
    next_core = [jnp.where(c == 0, came[2 * i + 1], came[2 * i]) for i in range(2)]
    attn_rows = jnp.concatenate(
        [jnp.where(a == i, v[0], v[1]) for i in range(2) for v in (same_core, next_core)], axis=0
    )
    attn_w = lax.all_gather(attn_rows, ("z", "y"), axis=0, tiled=True)
    x_own, c_own = to_place(tokens), to_place(cotangent)
    x_pieces = gather_rows(after(x_own, own_pack))
    gain_a, gain_m = after((attn_gain, mlp_gain), own_pack)
    gain_a, gain_m = gain_a.astype(F32)[:, None], gain_m.astype(F32)[:, None]
    quarter = lambda w, i: w[:, i * w.shape[1] // 4 : (i + 1) * w.shape[1] // 4]
    scaled = [(w.astype(F32) * gain_m).astype(BF) for w in (w_gate, w_up)]
    mlp_pack = [
        jnp.concatenate([quarter(w, i) for w in (*scaled, w_down.T)], axis=1) for i in range(4)
    ]
    mlp_rows, _ = spread(*split_quarters(mlp_pack, c), a, c, x_pieces[1:4])
    mlp_w = lax.all_gather(mlp_rows, ("z", "y"), axis=0, tiled=True)
    c_pieces = gather_rows(after(c_own, *x_pieces[1:4]))

    seg = jnp.stack([segment_ids, lax.ppermute(segment_ids, "a", SWAP)])
    seg = jnp.concatenate([seg, swap_core(seg)], axis=0)
    shift = jnp.stack([t, t ^ a, t, t ^ a])[:, None]
    cosines, sines, mask = token_tables(seg, shift, own, head)

    forward = attn_forward(x_pieces, attn_w, cosines, sines, mask, head)
    mine, other, normed, query, key, value, probs, mixed = forward
    parts = chip_parts(mine, swap_core(after(other, *c_pieces[1:4])))
    resid = x_own.astype(F32) + total_of(parts, send_parts(parts))

    n_pieces = gather_rows((resid * norm_factor(resid)).astype(BF))
    d_gate, d_up, hidden, mine, other = mlp(n_pieces, c_pieces, mlp_w)
    swapped = swap_core(other)
    grads = mlp_grads(n_pieces, c_pieces, d_gate, d_up, hidden)
    mlp_grad = lax.psum_scatter(grads, ("z", "y"), scatter_dimension=0, tiled=True)
    parts = chip_parts(mine, after(swapped, grads))
    got = send_parts(parts)
    out_mine, out_other = mlp_out(after(hidden, parts[1]), mlp_w)
    got = after(got, out_mine)

    d_resid, d_branch = finish(d_resid_kernel, [c_own, resid, parts[0], *got], [F32, BF])
    d_chips = [from_chip(d_branch, k) for k in (2, 1, 3)]
    out_parts = chip_parts(out_mine, swap_core(after(out_other, d_branch)))
    d_chips = after(d_chips, out_parts[1])
    out_got = send_parts(out_parts)
    d_pieces = [d_branch, *d_chips]
    d_pieces += [swap_core(piece) for piece in d_pieces]
    saved = (normed, query, key, value, probs, mixed)
    mine, other, attn_grads = attn_backward(d_pieces, attn_w, cosines, sines, saved, head)
    attn_grads = attn_grads.reshape(32, -1, attn_grads.shape[1])
    h = lax.all_to_all(attn_grads, ("z", "y", "c"), split_axis=0, concat_axis=0, tiled=True)
    parts = chip_parts(mine, swap_core(after(other, *out_got)))
    got = send_parts(parts)
    mlp_grad = after(mlp_grad, parts[1])

    by_x, came = unspread_x(mlp_grad, a)
    g, by_core = unspread_core(by_x, came, a, c)
    gate_grad, up_grad, down_grad = (columns_of(g, i * ff, ff) for i in range(3))
    arrays = [resid, out_parts[0], *after(out_got, parts[1])]
    (layer_output,) = finish(layer_output_kernel, arrays, [BF])
    arrays = [d_resid, x_own, parts[0], *got]
    (input_grad,) = finish(input_grad_kernel, arrays, [F32])
    along = lambda w, grad: jnp.sum(w.astype(F32) * grad, axis=1)
    mlp_gain_grad = along(w_gate, gate_grad) + along(w_up, up_grad)
    gate_grad, up_grad = gate_grad * gain_m, up_grad * gain_m
    h = h.reshape(16, 2, 2, -1, h.shape[2])
    h = jnp.sum(h.astype(F32), axis=0)
    first = a == 0
    keep = jnp.where(first, h[:, 0], h[:, 1])
    give = jnp.where(first, h[:, 1], h[:, 0]).astype(BF)
    came = lax.ppermute(after(give, by_core), "a", SWAP).astype(F32)
    h = [*jnp.where(first, keep, came), *jnp.where(first, came, keep)]
    query_grad = columns_of(h, 0, nq)
    key_grad = columns_of(h, nq, nk)
    value_grad = columns_of(h, nq + nk, nk)
    out_grad = columns_of(h, cut, nq).T
    attn_gain_grad = along(w_query, query_grad) + along(w_key, key_grad)
    attn_gain_grad = attn_gain_grad + along(w_value, value_grad)
    query_grad, key_grad, value_grad = (v * gain_a for v in (query_grad, key_grad, value_grad))
    gain_grads = jnp.stack([attn_gain_grad, mlp_gain_grad])
    gain_grads = gain_grads + lax.ppermute(gain_grads, "t", SWAP)
    return (
        layer_output, input_grad, gain_grads[0], query_grad, key_grad, value_grad, out_grad,
        gain_grads[1], gate_grad, up_grad, down_grad.T,
    )


def solution(mesh):
    fine = Mesh(mesh.devices.reshape(2, 4, 4, 2, 2), ("a", "z", "y", "c", "t"))
    dp = ("a", "z", "y", "c")
    rows = P(dp + ("t",), None)
    return jax.shard_map(
        local,
        mesh=fine,
        in_specs=(
            rows, P(dp), P(dp), P(dp, "t"), P(dp, "t"), P(dp, "t"), P("t", dp),
            P(dp), P(dp, "t"), P(dp, "t"), P("t", dp), rows,
        ),
        out_specs=(
            rows, rows, P(dp), P(dp, "t"), P(dp, "t"), P(dp, "t"), P("t", dp),
            P(dp), P(dp, "t"), P(dp, "t"), P("t", dp),
        ),
        check_vma=False,
    )
```

```python
import math

import jax
import jax.numpy as jnp
from jax import lax
from jax.experimental import pallas as pl
from jax.experimental.pallas import tpu as pltpu
from jax.sharding import Mesh
from jax.sharding import PartitionSpec as P

HEADS = 32
KV_HEADS = 8
GROUP = HEADS // KV_HEADS
EPSILON = 1e-05
ROPE_BASE = 500000.0
MASKED = -1e30
VMEM_LIMIT = 56 * 2**20
BF = jnp.bfloat16
F32 = jnp.float32


def cost(micros):
    return pl.CostEstimate(flops=micros * 10**9, bytes_accessed=2**20, transcendentals=0)


SWAP = [(0, 1), (1, 0)]


def mm(left, right):
    return jnp.dot(left, right, preferred_element_type=F32)


def mm_nt(left, right):
    return lax.dot_general(left, right, (((1,), (1,)), ((), ())), preferred_element_type=F32)


def mm_tn(left, right):
    return lax.dot_general(left, right, (((0,), (0,)), ((), ())), preferred_element_type=F32)


AT = (0, 2, 1, 3)


def from_chip(value, k):
    return lax.ppermute(value, ("a", "t"), [(AT[(i + k) % 4], AT[i]) for i in range(4)])


def to_chip(value, k):
    return lax.ppermute(value, ("a", "t"), [(AT[i], AT[(i + k) % 4]) for i in range(4)])


def after(value, *others):
    return lax.optimization_barrier((value, *others))[0]


def swap_core(value):
    return lax.ppermute(value, "c", SWAP)


def gather_rows(rows):
    mine = [rows, from_chip(rows, 2), from_chip(rows, 1), from_chip(rows, 3)]
    return mine + [swap_core(piece) for piece in mine]


def chip_parts(mine, got):
    rows = mine.shape[0] // 4
    parts = [
        mine[i * rows : (i + 1) * rows].astype(F32) + got[i * rows : (i + 1) * rows].astype(F32)
        for i in range(4)
    ]
    return [parts[0]] + [part.astype(BF) for part in parts[1:]]


def send_parts(parts):
    return [to_chip(part, k) for part, k in zip(parts[1:], (2, 1, 3))]


def total_of(parts, got):
    total = parts[0]
    for part in got:
        total = total + part.astype(F32)
    return total


def split_quarters(quarters, c):
    first = c == 0
    keep = [jnp.where(first, quarters[2 * i], quarters[2 * i + 1]) for i in range(2)]
    give = [jnp.where(first, quarters[2 * i + 1], quarters[2 * i]) for i in range(2)]
    return jnp.concatenate(keep, axis=0), jnp.concatenate(give, axis=0)


def spread(keep, give, a, c, wait=()):
    first = c == 0
    r = keep.shape[0] // 2
    got = swap_core(give)
    both = []
    for i in range(2):
        k, g = keep[i * r : (i + 1) * r], got[i * r : (i + 1) * r]
        both.append(jnp.concatenate([jnp.where(first, k, g), jnp.where(first, g, k)], axis=0))
    first_a = a == 0
    keep_a = jnp.where(first_a, both[0], both[1])
    give_a = jnp.where(first_a, both[1], both[0])
    got_a = lax.ppermute(after(give_a, *wait), "a", SWAP)
    rows = [jnp.where(first_a, keep_a, got_a), jnp.where(first_a, got_a, keep_a)]
    return jnp.concatenate(rows, axis=0), give_a


def unspread_x(rows, a):
    half = rows.shape[0] // 2
    first = a == 0
    give = jnp.where(first, rows[half:], rows[:half])
    return jnp.where(first, rows[:half], rows[half:]), lax.ppermute(give, "a", SWAP)


def unspread_core(mine, came, a, c):
    r = mine.shape[0] // 2
    first_a, first = a == 0, c == 0
    by_a = [jnp.where(first_a, mine, came), jnp.where(first_a, came, mine)]
    keep = [jnp.where(first, v[:r], v[r:]) for v in by_a]
    give = [jnp.where(first, v[r:], v[:r]) for v in by_a]
    got = swap_core(jnp.concatenate(give, axis=0))
    quarters = []
    for k, g in zip(keep, (got[:r], got[r:])):
        quarters += [jnp.where(first, k, g), jnp.where(first, g, k)]
    return quarters, got


def columns_of(quarters, start, width):
    return jnp.concatenate([q[:, start : start + width] for q in quarters], axis=1).astype(F32)


def to_place(rows):
    n, d = rows.shape
    return rows.reshape(n, 2, 16, d // 32).transpose(0, 2, 1, 3).reshape(n, d)


def norm_factor(values):
    return lax.rsqrt(jnp.mean(values * values, axis=-1, keepdims=True) + EPSILON)


def norm_back(values, upstream):
    factor = norm_factor(values)
    rescaled = values * factor
    return factor * (upstream - rescaled * jnp.mean(upstream * rescaled, axis=-1, keepdims=True))


def step_block(s):
    return (s + 2) % 4


def row_block(width):
    return lambda rows: pl.BlockSpec((rows, width), lambda s: (step_block(s), 0))


def fixed(shape):
    return pl.BlockSpec(shape, lambda *_: (0,) * len(shape))


def halves(rows, width):
    return [
        pl.BlockSpec((rows, width), lambda s: (jnp.maximum(s - 2, 0), 0)),
        pl.BlockSpec((rows, width), lambda s: (jnp.minimum(s, 1), 0)),
    ]


def load_block(s, pieces, scratch):
    part = pieces[0].shape[0]
    for b in range(4):

        @pl.when(step_block(s) == b)
        def _():
            scratch[:part] = pieces[2 * b][...]
            scratch[part:] = pieces[2 * b + 1][...]


def store_half(s, mine_ref, other_ref, value):
    @pl.when(s < 2)
    def _():
        other_ref[...] = value

    @pl.when(s >= 2)
    def _():
        mine_ref[...] = value


def turn(values, cosines, sines, head):
    width = values.shape[1]
    lane = lax.broadcasted_iota(jnp.int32, values.shape, 1)
    low = lane % head < head // 2
    partner = jnp.where(
        low, pltpu.roll(values, width - head // 2, 1), pltpu.roll(values, head // 2, 1)
    )
    return values * cosines + partner * sines


def double(values, times):
    return jnp.concatenate([values] * times, axis=1)


def by_head(values, head):
    lane = lax.broadcasted_iota(jnp.int32, values.shape, 1) // head
    zero = jnp.zeros_like(values)
    return jnp.concatenate([jnp.where(lane == h, values, zero) for h in range(GROUP)], axis=0)


def take_heads(values, rows, head):
    lane = lax.broadcasted_iota(jnp.int32, (rows, values.shape[1]), 1) // head
    out = values[:rows]
    for h in range(1, GROUP):
        out = jnp.where(lane == h, values[h * rows : (h + 1) * rows], out)
    return out


def fold_heads(values, head):
    pair = values[:, : 2 * head] + values[:, 2 * head :]
    return pair + pltpu.roll(pair, head, 1)


def pack_kernel(place_ref, gain_ref, wq_ref, wk_ref, wv_ref, wo_ref, *out_refs):
    r, wide = wq_ref.shape[0], wq_ref.shape[1] // 4
    head = wk_ref.shape[1] // 4
    row = jnp.broadcast_to(gain_ref[...].astype(F32), (8, r))
    row = jnp.where(lax.broadcasted_iota(jnp.int32, row.shape, 0) == 0, row, 0.0).astype(BF)
    gain = mm_tn(row, jnp.ones((8, 2 * head), BF))
    queries = (wq_ref[...].astype(F32) * double(gain, wq_ref.shape[1] // (2 * head))).astype(BF)
    keys = wk_ref[...].astype(F32) * double(gain, 2)
    values = wv_ref[...].astype(F32) * double(gain, 2)
    low = lax.broadcasted_iota(jnp.int32, (r, 2 * head), 1) < head

    def fill(ref, q):
        columns = slice(q * wide, (q + 1) * wide)
        pair = slice(q // 2 * 2 * head, (q // 2 + 1) * 2 * head)
        key, value = keys[:, pair], values[:, pair]
        if q % 2:
            key = pltpu.roll(key, head, 1)
        else:
            value = pltpu.roll(value, head, 1)
        ref[:, :wide] = queries[:, columns]
        ref[:, wide : wide + 2 * head] = jnp.where(low, key, value).astype(BF)
        ref[:, wide + 2 * head :] = wo_ref[:, columns]

    for own in range(4):

        @pl.when(place_ref[0] == own)
        def _():
            for other in range(4):
                fill(out_refs[other], own ^ other)


def pack_attn(place, gain, w_query, w_key, w_value, w_out_t):
    r, columns = w_query.shape
    shape = jax.ShapeDtypeStruct((r, columns // 4 + w_key.shape[1] // 2 + columns // 4), BF)
    vmem = pl.BlockSpec(memory_space=pltpu.VMEM)
    return pl.pallas_call(
        pack_kernel,
        in_specs=[pl.BlockSpec(memory_space=pltpu.SMEM)] + [vmem] * 5,
        out_specs=[vmem] * 4,
        out_shape=[shape] * 4,
        cost_estimate=cost(2),
    )(place.reshape(1).astype(jnp.int32), gain, w_query, w_key, w_value, w_out_t)


def attn_forward_kernel(head, *refs):
    pieces = refs[:8]
    (w_ref, cos_ref, sin_ref, mask_ref,
     mine_ref, other_ref, normed_ref, q_ref, k_ref, v_ref, probs_ref, mixed_ref,
     x_ref) = refs[8:]
    s = pl.program_id(0)
    nq, cut = GROUP * head, (GROUP + 2) * head
    rows = x_ref.shape[0]

    load_block(s, pieces, x_ref)
    x = x_ref[...].astype(F32)
    factor = lax.rsqrt(jnp.mean(x * x, axis=-1, keepdims=True) + EPSILON)
    normed = (x * factor).astype(BF)
    normed_ref[...] = normed
    qkv = mm(normed, w_ref[:, :cut])
    cosines, sines = cos_ref[...], sin_ref[...]
    query = turn(qkv[:, :nq], double(cosines, 2), double(sines, 2), head).astype(BF)
    kv = qkv[:, nq:]
    turned = turn(kv, cosines, sines, head)
    low = lax.broadcasted_iota(jnp.int32, kv.shape, 1) < head
    key = double(jnp.where(low, turned, pltpu.roll(turned, head, 1)), 2).astype(BF)
    value = double(jnp.where(low, pltpu.roll(kv, head, 1), kv), 2).astype(BF)
    q_ref[...] = query
    k_ref[...] = key
    v_ref[...] = value
    scores = mm_nt(by_head(query, head), key) * (1.0 / math.sqrt(head))
    allowed = mask_ref[...] == 0
    scores = jnp.where(jnp.concatenate([allowed] * GROUP, axis=0), scores, MASKED)
    weights = jnp.exp(scores - jnp.max(scores, axis=-1, keepdims=True))
    probs = weights / jnp.sum(weights, axis=-1, keepdims=True)
    probs_ref[...] = probs
    mixed = take_heads(mm(probs.astype(BF), value), rows, head).astype(BF)
    mixed_ref[...] = mixed
    store_half(s, mine_ref, other_ref, mm_nt(mixed, w_ref[:, cut : cut + nq]).astype(BF))


def attn_forward(pieces, w, cosines, sines, mask, head):
    part, d = pieces[0].shape
    rows = 2 * part
    nq = GROUP * head
    spec = lambda width: row_block(width)(rows)
    return pl.pallas_call(
        lambda *refs: attn_forward_kernel(head, *refs),
        grid=(4,),
        in_specs=[fixed(p.shape) for p in pieces]
        + [fixed(w.shape), spec(2 * head), spec(2 * head), spec(rows)],
        out_specs=halves(rows, d)
        + [spec(d), spec(nq), spec(nq), spec(nq)]
        + [pl.BlockSpec((GROUP * rows, rows), lambda s: (step_block(s), 0)), spec(nq)],
        out_shape=[jax.ShapeDtypeStruct((2 * rows, d), BF)] * 2
        + [jax.ShapeDtypeStruct((4 * rows, d), BF)]
        + [jax.ShapeDtypeStruct((4 * rows, nq), BF)] * 3
        + [
            jax.ShapeDtypeStruct((4 * GROUP * rows, rows), F32),
            jax.ShapeDtypeStruct((4 * rows, nq), BF),
        ],
        scratch_shapes=[pltpu.VMEM((rows, d), BF)],
        compiler_params=pltpu.CompilerParams(vmem_limit_bytes=VMEM_LIMIT),
        cost_estimate=cost(30),
    )(*pieces, w, cosines, sines, mask)


def attn_backward_kernel(head, *refs):
    d_pieces = refs[:8]
    (w_ref, cos_ref, sin_ref, normed_ref, q_ref, k_ref, v_ref, probs_ref, mixed_ref,
     mine_ref, other_ref, grad_ref, d_scr, n_scr, qkv_scr) = refs[8:]
    s = pl.program_id(0)
    nq, cut = GROUP * head, (GROUP + 2) * head
    part = d_pieces[0].shape[0]
    rows = 2 * part
    scale = 1.0 / math.sqrt(head)

    @pl.when(s == 0)
    def _():
        for i in range(8):
            d_scr[i * part : (i + 1) * part] = d_pieces[i][...]

    here = pl.ds(pl.multiple_of(step_block(s) * rows, rows), rows)
    n_scr[here] = normed_ref[...]
    d_branch = d_scr[here]
    d_mixed = by_head(mm(d_branch, w_ref[:, cut : cut + nq]).astype(BF), head)
    d_probs = mm_nt(d_mixed, v_ref[...])
    probs = probs_ref[...]
    d_value = fold_heads(mm_tn(probs.astype(BF), d_mixed), head)
    d_scores = probs * (d_probs - jnp.sum(d_probs * probs, axis=-1, keepdims=True))
    d_scores = d_scores.astype(BF)
    d_query = take_heads(mm(d_scores, k_ref[...]), rows, head) * scale
    d_key = fold_heads(mm_tn(d_scores, by_head(q_ref[...], head)), head) * scale
    cosines, sines = cos_ref[...], -sin_ref[...]
    d_query = turn(d_query, double(cosines, 2), double(sines, 2), head).astype(BF)
    d_key = turn(d_key, cosines, sines, head)
    low = lax.broadcasted_iota(jnp.int32, d_key.shape, 1) < head
    d_kv = jnp.where(low, d_key, d_value).astype(BF)
    d_qkv = jnp.concatenate([d_query, d_kv], axis=1)
    qkv_scr[here] = d_qkv
    d_normed = mm_nt(d_qkv, w_ref[:, :cut])
    store_half(s, mine_ref, other_ref, d_normed.astype(BF))

    @pl.when(s == 3)
    def _():
        def put(value, start):
            size = value.shape[0] // 64
            for zy in range(16):
                for k, old in enumerate((0, 2, 1, 3)):
                    to, at = (zy * 4 + k) * size, (zy * 4 + old) * size
                    grad_ref[to : to + size, start : start + value.shape[1]] = value[at : at + size]

        put(mm_tn(n_scr[...], qkv_scr[...]).astype(BF), 0)
        put(mm_tn(d_scr[...], mixed_ref[...]).astype(BF), cut)


def attn_backward(d_pieces, w, cosines, sines, saved, head):
    normed, query, key, value, probs, mixed = saved
    part, d = d_pieces[0].shape
    rows = 2 * part
    nq, cut = GROUP * head, (GROUP + 2) * head
    wide = cut + nq
    spec = lambda width: row_block(width)(rows)
    return pl.pallas_call(
        lambda *refs: attn_backward_kernel(head, *refs),
        grid=(4,),
        in_specs=[fixed(p.shape) for p in d_pieces]
        + [fixed(w.shape), spec(2 * head), spec(2 * head), spec(d)]
        + [spec(nq), spec(nq), spec(nq)]
        + [pl.BlockSpec((GROUP * rows, rows), lambda s: (step_block(s), 0)), fixed(mixed.shape)],
        out_specs=halves(rows, d) + [fixed((d, wide))],
        out_shape=[jax.ShapeDtypeStruct((2 * rows, d), BF)] * 2
        + [jax.ShapeDtypeStruct((d, wide), BF)],
        scratch_shapes=[
            pltpu.VMEM((4 * rows, d), BF),
            pltpu.VMEM((4 * rows, d), BF),
            pltpu.VMEM((4 * rows, cut), BF),
        ],
        compiler_params=pltpu.CompilerParams(vmem_limit_bytes=VMEM_LIMIT),
        cost_estimate=cost(10),
    )(*d_pieces, w, cosines, sines, normed, query, key, value, probs, mixed)


def mlp_kernel(*refs):
    n_pieces, c_pieces = refs[:8], refs[8:16]
    (wg_ref, wu_ref, wd_ref, dg_ref, du_ref, hid_ref, mine_ref, other_ref,
     n_scr, c_scr, w_scr, d_scr) = refs[16:]
    j = pl.program_id(0)
    part = n_pieces[0].shape[0]
    tile = wg_ref.shape[1]
    ff = 4 * tile

    @pl.when(j == 0)
    def _():
        for i in range(8):
            n_scr[i * part : (i + 1) * part] = n_pieces[i][...]
            c_scr[i * part : (i + 1) * part] = c_pieces[i][...]

    for step in range(4):

        @pl.when(j == step)
        def _():
            w_scr[:, step * tile : (step + 1) * tile] = wg_ref[...]
            w_scr[:, ff + step * tile : ff + (step + 1) * tile] = wu_ref[...]
            gate = mm(n_scr[...], wg_ref[...])
            up = mm(n_scr[...], wu_ref[...])
            d_hidden = mm(c_scr[...], wd_ref[...])
            sig = jax.nn.sigmoid(gate)
            silu = gate * sig
            hid_ref[...] = (silu * up).astype(BF)
            d_gate = (d_hidden * up * sig * (1.0 + gate * (1.0 - sig))).astype(BF)
            d_up = (d_hidden * silu).astype(BF)
            dg_ref[...] = d_gate
            du_ref[...] = d_up
            d_scr[:, step * tile : (step + 1) * tile] = d_gate
            d_scr[:, ff + step * tile : ff + (step + 1) * tile] = d_up

    @pl.when(j >= 4)
    def _():
        wide = mine_ref.shape[1]
        rows = pl.ds(pl.multiple_of((j - 4) * wide, wide), wide)
        d_n2 = mm_nt(d_scr[...], w_scr[rows, :]).astype(BF)
        mine_ref[...] = d_n2[: 4 * part]
        other_ref[...] = d_n2[4 * part :]


def mlp(n_pieces, c_pieces, w):
    part, d = n_pieces[0].shape
    rows, ff = 8 * part, w.shape[1] // 3
    tile, wide = ff // 4, d // 4
    at = lambda k: pl.BlockSpec((d, tile), lambda j: (0, 4 * k + jnp.minimum(j, 3)))
    return pl.pallas_call(
        mlp_kernel,
        grid=(8,),
        in_specs=[fixed((part, d))] * 16 + [at(0), at(1), at(2)],
        out_specs=[pl.BlockSpec((rows, tile), lambda j: (0, jnp.minimum(j, 3)))] * 3
        + [pl.BlockSpec((rows // 2, wide), lambda j: (0, jnp.maximum(j - 4, 0)))] * 2,
        out_shape=[jax.ShapeDtypeStruct((rows, ff), BF)] * 3
        + [jax.ShapeDtypeStruct((rows // 2, d), BF)] * 2,
        scratch_shapes=[
            pltpu.VMEM((rows, d), BF),
            pltpu.VMEM((rows, d), BF),
            pltpu.VMEM((d, 2 * ff), BF),
            pltpu.VMEM((rows, 2 * ff), BF),
        ],
        compiler_params=pltpu.CompilerParams(vmem_limit_bytes=VMEM_LIMIT),
        cost_estimate=cost(40),
    )(*n_pieces, *c_pieces, w, w, w)


def mlp_grads_kernel(*refs):
    n_pieces, c_pieces = refs[:8], refs[8:16]
    dg_ref, du_ref, hid_ref, g_ref = refs[16:]
    ff = dg_ref.shape[1]
    n_part = jnp.concatenate([piece[...] for piece in n_pieces], axis=0).T
    c_part = jnp.concatenate([piece[...] for piece in c_pieces], axis=0).T
    g_ref[:, :ff] = mm(n_part, dg_ref[...]).astype(BF)
    g_ref[:, ff : 2 * ff] = mm(n_part, du_ref[...]).astype(BF)
    g_ref[:, 2 * ff :] = mm(c_part, hid_ref[...]).astype(BF)


def mlp_grads(n_pieces, c_pieces, d_gate, d_up, hidden):
    part, d = n_pieces[0].shape
    rows, ff = hidden.shape
    wide = d // 8
    return pl.pallas_call(
        mlp_grads_kernel,
        grid=(8,),
        in_specs=[pl.BlockSpec((part, wide), lambda j: (0, j))] * 16 + [fixed((rows, ff))] * 3,
        out_specs=pl.BlockSpec((wide, 3 * ff), lambda j: (j, 0)),
        out_shape=jax.ShapeDtypeStruct((d, 3 * ff), BF),
        compiler_params=pltpu.CompilerParams(vmem_limit_bytes=VMEM_LIMIT),
        cost_estimate=cost(40),
    )(*n_pieces, *c_pieces, d_gate, d_up, hidden)


def mlp_out_kernel(x_ref, w_ref, mine_ref, other_ref):
    half = x_ref.shape[0] // 2
    out = mm_nt(x_ref[...], w_ref[...]).astype(BF)
    mine_ref[...] = out[:half]
    other_ref[...] = out[half:]


def mlp_out(hid, w):
    rows, ff = hid.shape
    d = w.shape[0]
    wide = d // 4
    return pl.pallas_call(
        mlp_out_kernel,
        grid=(4,),
        in_specs=[fixed((rows, ff)), pl.BlockSpec((wide, ff), lambda j: (j, 2))],
        out_specs=[pl.BlockSpec((rows // 2, wide), lambda j: (0, j))] * 2,
        out_shape=[jax.ShapeDtypeStruct((rows // 2, d), BF)] * 2,
        compiler_params=pltpu.CompilerParams(vmem_limit_bytes=VMEM_LIMIT),
        cost_estimate=cost(5),
    )(hid, w)


def store_placed(ref, value):
    tile = value.shape[1] // 16
    half = tile // 2
    low = lax.broadcasted_iota(jnp.int32, (value.shape[0], tile), 1) < half
    for i in range(8):
        even = value[:, 2 * i * tile : (2 * i + 1) * tile]
        odd = value[:, (2 * i + 1) * tile : (2 * i + 2) * tile]
        first = jnp.where(low, even, pltpu.roll(odd, half, 1))
        second = jnp.where(low, pltpu.roll(even, half, 1), odd)
        ref[:, i * tile : (i + 1) * tile] = first.astype(ref.dtype)
        ref[:, (8 + i) * tile : (9 + i) * tile] = second.astype(ref.dtype)


def d_resid_kernel(c_ref, resid_ref, mine_ref, swap_ref, g2_ref, g1_ref, g3_ref, out_ref, low_ref):
    d_normed = total_of(
        [mine_ref[...].astype(F32)], [swap_ref[...], g2_ref[...], g1_ref[...], g3_ref[...]]
    )
    out = c_ref[...].astype(F32) + norm_back(resid_ref[...], d_normed)
    out_ref[...] = out
    low_ref[...] = out.astype(BF)


def layer_output_kernel(resid_ref, mine_ref, swap_ref, g2_ref, g1_ref, g3_ref, out_ref):
    total = total_of(
        [mine_ref[...].astype(F32)], [swap_ref[...], g2_ref[...], g1_ref[...], g3_ref[...]]
    )
    store_placed(out_ref, resid_ref[...] + total)


def input_grad_kernel(d_resid_ref, x_ref, mine_ref, swap_ref, g2_ref, g1_ref, g3_ref, out_ref):
    d_normed = total_of(
        [mine_ref[...].astype(F32)], [swap_ref[...], g2_ref[...], g1_ref[...], g3_ref[...]]
    )
    back = norm_back(x_ref[...].astype(F32), d_normed)
    store_placed(out_ref, d_resid_ref[...] + back)


def finish(kernel, arrays, dtypes):
    shape = arrays[0].shape
    return pl.pallas_call(
        kernel,
        grid=(1,),
        in_specs=[fixed(shape)] * len(arrays),
        out_specs=[fixed(shape) for _ in dtypes],
        out_shape=[jax.ShapeDtypeStruct(shape, dtype) for dtype in dtypes],
        compiler_params=pltpu.CompilerParams(vmem_limit_bytes=VMEM_LIMIT),
        cost_estimate=cost(2),
    )(*arrays)


def token_tables(seg, shift, own, head):
    count, block = seg.shape
    seg = jnp.where(shift == 0, seg, jnp.roll(seg, own, axis=1))
    order = (jnp.arange(block, dtype=jnp.int32)[None, :] + shift * own) % block
    earlier = jnp.sum((seg[:, None, :] < seg[:, :, None]).astype(jnp.int32), axis=2)
    positions = (order - earlier).reshape(count * block, 1)
    allowed = (seg[:, :, None] == seg[:, None, :]) & (order[:, None, :] <= order[:, :, None])
    mask = jnp.where(allowed, 0.0, MASKED).astype(F32).reshape(count * block, block)
    lane = jnp.arange(2 * head)
    frequency = jnp.exp(-math.log(ROPE_BASE) * ((lane % (head // 2)).astype(F32) / (head // 2)))
    angles = positions.astype(F32) * frequency
    sines = jnp.where(lane % head < head // 2, -1.0, 1.0) * jnp.sin(angles)
    return jnp.cos(angles), sines, mask


def local(
    tokens, segment_ids, attn_gain, w_query, w_key, w_value, w_out,
    mlp_gain, w_gate, w_up, w_down, cotangent,
):
    a, c, t = lax.axis_index("a"), lax.axis_index("c"), lax.axis_index("t")
    own = tokens.shape[0]
    nq = w_query.shape[1] // 4
    nk = w_key.shape[1] // 4
    ff = w_gate.shape[1] // 4
    head = nk
    cut = nq + 2 * nk

    own_pack, by_core, by_x, by_both = pack_attn(
        2 * a + c, attn_gain[None], w_query, w_key, w_value, w_out.T
    )
    came = [
        own_pack,
        swap_core(by_core),
        lax.ppermute(by_x, "a", SWAP),
        lax.ppermute(by_both, ("a", "c"), [(i, 3 - i) for i in range(4)]),
    ]
    same_core = [jnp.where(c == 0, came[2 * i], came[2 * i + 1]) for i in range(2)]
    next_core = [jnp.where(c == 0, came[2 * i + 1], came[2 * i]) for i in range(2)]
    attn_rows = jnp.concatenate(
        [jnp.where(a == i, v[0], v[1]) for i in range(2) for v in (same_core, next_core)], axis=0
    )
    attn_w = lax.all_gather(attn_rows, ("z", "y"), axis=0, tiled=True)
    x_own, c_own = to_place(tokens), to_place(cotangent)
    x_pieces = gather_rows(after(x_own, own_pack))
    gain_a, gain_m = after((attn_gain, mlp_gain), own_pack)
    gain_a, gain_m = gain_a.astype(F32)[:, None], gain_m.astype(F32)[:, None]
    quarter = lambda w, i: w[:, i * w.shape[1] // 4 : (i + 1) * w.shape[1] // 4]
    scaled = [(w.astype(F32) * gain_m).astype(BF) for w in (w_gate, w_up)]
    mlp_pack = [
        jnp.concatenate([quarter(w, i) for w in (*scaled, w_down.T)], axis=1) for i in range(4)
    ]
    mlp_rows, _ = spread(*split_quarters(mlp_pack, c), a, c, x_pieces[1:4])
    mlp_w = lax.all_gather(mlp_rows, ("z", "y"), axis=0, tiled=True)
    c_pieces = gather_rows(after(c_own, *x_pieces[1:4]))

    seg = jnp.stack([segment_ids, lax.ppermute(segment_ids, "a", SWAP)])
    seg = jnp.concatenate([seg, swap_core(seg)], axis=0)
    shift = jnp.stack([t, t ^ a, t, t ^ a])[:, None]
    cosines, sines, mask = token_tables(seg, shift, own, head)

    forward = attn_forward(x_pieces, attn_w, cosines, sines, mask, head)
    mine, other, normed, query, key, value, probs, mixed = forward
    parts = chip_parts(mine, swap_core(after(other, *c_pieces[1:4])))
    resid = x_own.astype(F32) + total_of(parts, send_parts(parts))

    n_pieces = gather_rows((resid * norm_factor(resid)).astype(BF))
    d_gate, d_up, hidden, mine, other = mlp(n_pieces, c_pieces, mlp_w)
    swapped = swap_core(other)
    grads = mlp_grads(n_pieces, c_pieces, d_gate, d_up, hidden)
    mlp_grad = lax.psum_scatter(grads, ("z", "y"), scatter_dimension=0, tiled=True)
    swapped = after(swapped, grads)
    parts = chip_parts(mine, swapped)
    mlp_pair = mine, swapped
    got = send_parts(parts)
    out_mine, out_other = mlp_out(after(hidden, parts[1]), mlp_w)
    got = after(got, out_mine)

    d_resid, d_branch = finish(d_resid_kernel, [c_own, resid, *mlp_pair, *got], [F32, BF])
    d_chips = [from_chip(d_branch, k) for k in (2, 1, 3)]
    out_pair = out_mine, swap_core(after(out_other, d_branch))
    out_parts = chip_parts(*out_pair)
    d_chips = after(d_chips, out_parts[1])
    out_got = send_parts(out_parts)
    d_pieces = [d_branch, *d_chips]
    d_pieces += [swap_core(piece) for piece in d_pieces]
    saved = (normed, query, key, value, probs, mixed)
    mine, other, attn_grads = attn_backward(d_pieces, attn_w, cosines, sines, saved, head)
    attn_grads = attn_grads.reshape(32, -1, attn_grads.shape[1])
    h = lax.all_to_all(attn_grads, ("z", "y", "c"), split_axis=0, concat_axis=0, tiled=True)
    attn_pair = mine, swap_core(after(other, *out_got))
    parts = chip_parts(*attn_pair)
    got = send_parts(parts)
    mlp_grad = after(mlp_grad, parts[1])

    by_x, came = unspread_x(mlp_grad, a)
    g, by_core = unspread_core(by_x, came, a, c)
    gate_grad, up_grad, down_grad = (columns_of(g, i * ff, ff) for i in range(3))
    arrays = [resid, *out_pair, *after(out_got, parts[1])]
    (layer_output,) = finish(layer_output_kernel, arrays, [BF])
    arrays = [d_resid, x_own, *attn_pair, *got]
    (input_grad,) = finish(input_grad_kernel, arrays, [F32])
    along = lambda w, grad: jnp.sum(w.astype(F32) * grad, axis=1)
    mlp_gain_grad = along(w_gate, gate_grad) + along(w_up, up_grad)
    gate_grad, up_grad = gate_grad * gain_m, up_grad * gain_m
    h = h.reshape(16, 2, 2, -1, h.shape[2])
    h = jnp.sum(h.astype(F32), axis=0)
    first = a == 0
    keep = jnp.where(first, h[:, 0], h[:, 1])
    give = jnp.where(first, h[:, 1], h[:, 0]).astype(BF)
    came = lax.ppermute(after(give, by_core), "a", SWAP).astype(F32)
    h = [*jnp.where(first, keep, came), *jnp.where(first, came, keep)]
    query_grad = columns_of(h, 0, nq)
    key_grad = columns_of(h, nq, nk)
    value_grad = columns_of(h, nq + nk, nk)
    out_grad = columns_of(h, cut, nq).T
    attn_gain_grad = along(w_query, query_grad) + along(w_key, key_grad)
    attn_gain_grad = attn_gain_grad + along(w_value, value_grad)
    query_grad, key_grad, value_grad = (v * gain_a for v in (query_grad, key_grad, value_grad))
    gain_grads = jnp.stack([attn_gain_grad, mlp_gain_grad])
    gain_grads = gain_grads + lax.ppermute(gain_grads, "t", SWAP)
    return (
        layer_output, input_grad, gain_grads[0], query_grad, key_grad, value_grad, out_grad,
        gain_grads[1], gate_grad, up_grad, down_grad.T,
    )


def solution(mesh):
    fine = Mesh(mesh.devices.reshape(2, 4, 4, 2, 2), ("a", "z", "y", "c", "t"))
    dp = ("a", "z", "y", "c")
    rows = P(dp + ("t",), None)
    return jax.shard_map(
        local,
        mesh=fine,
        in_specs=(
            rows, P(dp), P(dp), P(dp, "t"), P(dp, "t"), P(dp, "t"), P("t", dp),
            P(dp), P(dp, "t"), P(dp, "t"), P("t", dp), rows,
        ),
        out_specs=(
            rows, rows, P(dp), P(dp, "t"), P(dp, "t"), P(dp, "t"), P("t", dp),
            P(dp), P(dp, "t"), P(dp, "t"), P("t", dp),
        ),
        check_vma=False,
    )
```
